256 devices in a mesh: role: 2 (over y_hi), fsdp: 64 (over x, z, core), seq: 2 (over y_lo).
Axes of the slice: x: 4, y: 4 (y_hi: 2, y_lo: 2; y = y_hi * 2 + y_lo), z: 8, core: 2. Of those that a mesh axis runs over, the one named last changes fastest.
Arguments:
- base_latents: bfloat16 [2, 64, 256, 64], P('role', 'fsdp', 'seq'), may hold values from -6 to 6
- noise_latents: bfloat16 [2, 64, 256, 64], P('role', 'fsdp', 'seq'), may hold values from -6 to 6
- noise_levels: float32 [2, 64], P('role', 'fsdp'), may hold values from 0.1 to 0.95
- replay_latents: bfloat16 [2, 64, 256, 64], P('role', 'fsdp', 'seq'), may hold values from -6 to 6
- replay_levels: float32 [2, 64], P('role', 'fsdp'), may hold values from 0.1 to 0.95
- cotangent: bfloat16 [2, 64, 256, 64], P('role', 'fsdp', 'seq'), may hold values from -6 to 6
- embed_weight: bfloat16 [2, 64, 3072], P('role'), may hold values from -0.75 to 0.75
- qkv_weight: bfloat16 [2, 3072, 4608], P('role', 'fsdp', 'seq'), as said below
- output_weight: bfloat16 [2, 1536, 64], P('role', 'seq'), may hold values from -0.15625 to 0.15625
- modulation: float32 [2, 2, 2, 3072], P('role'), may hold values from -3 to 3
Outputs:
- crossed: bfloat16 [2, 64, 256, 64], P('role', 'fsdp', 'seq')
- mod_grads: float32 [2, 2, 3072], P('role')
The draws below stay inside these ranges and needn't reach their ends.
Inputs may be any that keep to these rules, and one draw needn't show every extreme that they name: `qkv_weight`: each head's query, key and value columns stand in that order, head after head.
All inputs are finite; a program needn't handle non-finite values.
Results may differ from the reference program's by a relative error of at most 0.0076.
Values may be sent and summed in bfloat16 or wider, within the bound.
No kernel may reach another device: no remote copies, remote signals or barrier semaphores. Data moves between devices by JAX's collectives and lax.ppermute only.
A program may use at most 128 MiB of HBM per device.

```python
import math
import jax
import jax.numpy as jnp
from jax import lax

D = 3072
HEAD_DIM = 128
CHANNELS = 64
HEADS = 12
SAMPLES = 64
LENGTH = 256


def draw_qkv_weight(key, part):
    key = jax.random.fold_in(key, 11)
    normal_key = jax.random.fold_in(key, 0)
    base = jax.random.normal(normal_key, (2, D, HEADS, 3, HEAD_DIM), jnp.float32) * D ** (-0.5)
    return base.reshape(2, D, HEADS * 3 * HEAD_DIM).astype(jnp.bfloat16)


def draw_cotangent(key, part):
    key = jax.random.fold_in(key, 13)
    sign_key, size_key, noise_key = jax.random.split(key, 3)
    signs = jnp.where(jax.random.uniform(sign_key, (2, 1, 1, CHANNELS), jnp.float32) < 0.5, -1.0, 1.0)
    sizes = jax.random.uniform(size_key, (2, 1, 1, CHANNELS), jnp.float32, 0.75, 1.5)
    noise = jnp.clip(jax.random.normal(noise_key, (2, SAMPLES, LENGTH, CHANNELS), jnp.float32), -4.0, 4.0)
    return (signs * sizes + noise).astype(jnp.bfloat16)


def shard_levels(key, extent, shards, low, top_value):
    def one(position, blocks):
        draws = jax.random.uniform(jax.random.fold_in(jax.random.fold_in(key, 6), position), (blocks,), jnp.float32, low / len(shards), top_value / len(shards))
        return jnp.repeat(jnp.exp(draws), extent[position] // blocks).reshape((-1,) + (1,) * (len(extent) - position - 1))

    factor_of = one(*shards[0])
    for cut in shards[1:]:
        factor_of = factor_of * one(*cut)
    return factor_of


def centred(stream_key, dims, width, most, shards=(), dtype=jnp.bfloat16):
    level = shard_levels(stream_key, dims, shards, -0.22, 0.18) if shards else 1.0
    values = jax.random.normal(stream_key, dims, jnp.float32) * width * level
    return jnp.minimum(jnp.maximum(values, -most), most).astype(dtype)


def setup_inputs(seed: int = 0) -> dict:
    key_of = jax.random.split(jax.random.key(seed), 11)
    base_latents = centred(key_of[0], (2, SAMPLES, LENGTH, CHANNELS), 1.0, 6.0, ((0, 2), (1, 64), (2, 2)))
    noise_latents = centred(key_of[1], (2, SAMPLES, LENGTH, CHANNELS), 1.0, 6.0, ((0, 2), (1, 64), (2, 2)))
    noise_levels = jnp.clip(0.1 + 0.84999999 * jax.random.uniform(key_of[2], (2, SAMPLES), jnp.float32) ** shard_levels(key_of[2], (2, SAMPLES), ((0, 2), (1, 64)), -0.2, 0.2), 0.1, 0.95)
    replay_latents = centred(key_of[3], (2, SAMPLES, LENGTH, CHANNELS), 1.0, 6.0, ((0, 2), (1, 64), (2, 2)))
    replay_levels = jnp.clip(0.1 + 0.84999999 * jax.random.uniform(key_of[4], (2, SAMPLES), jnp.float32) ** shard_levels(key_of[4], (2, SAMPLES), ((0, 2), (1, 64)), -0.2, 0.2), 0.1, 0.95)
    cotangent = draw_cotangent(jax.random.fold_in(key_of[10], 71), 0)
    embed_weight = centred(key_of[6], (2, CHANNELS, D), CHANNELS ** -0.5, 0.75, ((0, 2),))
    qkv_weight = draw_qkv_weight(jax.random.fold_in(key_of[10], 71), 0)
    output_weight = centred(key_of[8], (2, HEADS * HEAD_DIM, CHANNELS), (HEADS * HEAD_DIM) ** -0.5, 0.15625, ((0, 2), (1, 2)))
    modulation = centred(key_of[9], (2, 2, 2, D), 0.5, 3.0, ((0, 2),), jnp.float32)
    return {"base_latents": base_latents, "noise_latents": noise_latents, "noise_levels": noise_levels, "replay_latents": replay_latents, "replay_levels": replay_levels, "cotangent": cotangent, "embed_weight": embed_weight, "qkv_weight": qkv_weight, "output_weight": output_weight, "modulation": modulation}


EPSILON = 1e-06

def embed_normed(latents, embed_weight):
    embedded = jnp.dot(latents, embed_weight, preferred_element_type=jnp.float32)
    return embedded * lax.rsqrt(lax.optimization_barrier(jnp.mean(embedded * embedded, axis=-1, keepdims=True)) + EPSILON)

def modulated(normed, level, mod_pair):
    return (normed * (1.0 + level * mod_pair[0]) + level * mod_pair[1]).astype(jnp.bfloat16)

def attend_heads(qkv_rows, head_count):
    tokens = qkv_rows.shape[0]
    split = qkv_rows.reshape(tokens, head_count, 3, HEAD_DIM).astype(jnp.float32)
    scores = jnp.einsum('shd,thd->hst', split[:, :, 0], split[:, :, 1]) / math.sqrt(HEAD_DIM)
    weights = jax.nn.softmax(scores, axis=-1)
    rounded = lax.optimization_barrier(weights.astype(jnp.bfloat16)).astype(jnp.float32)
    mixed = jnp.einsum('hst,thd->shd', rounded, split[:, :, 2])
    return (mixed.astype(jnp.bfloat16).reshape(tokens, head_count * HEAD_DIM), weights)

def attend_back(qkv_rows, weights, grad_mixed, head_count):
    tokens = qkv_rows.shape[0]
    split = qkv_rows.reshape(tokens, head_count, 3, HEAD_DIM).astype(jnp.float32)
    grad_heads = grad_mixed.reshape(tokens, head_count, HEAD_DIM).astype(jnp.float32)
    rounded = lax.optimization_barrier(weights.astype(jnp.bfloat16)).astype(jnp.float32)
    grad_value = jnp.einsum('hst,shd->thd', rounded, grad_heads).astype(jnp.bfloat16)
    grad_weights = jnp.einsum('shd,thd->hst', grad_heads, split[:, :, 2])
    grad_scores = weights * (grad_weights - lax.optimization_barrier(jnp.sum(grad_weights * weights, axis=-1, keepdims=True))) / math.sqrt(HEAD_DIM)
    grad_rounded = lax.optimization_barrier(grad_scores.astype(jnp.bfloat16)).astype(jnp.float32)
    grad_query = jnp.einsum('hst,thd->shd', grad_rounded, split[:, :, 1]).astype(jnp.bfloat16)
    grad_key = jnp.einsum('hst,shd->thd', grad_rounded, split[:, :, 0]).astype(jnp.bfloat16)
    return jnp.stack([grad_query, grad_key, grad_value], axis=2).reshape(tokens, -1)

def role_pass(role_index, base_latents, noise_latents, noise_levels, replay_latents, replay_levels, cotangent, embed_weight, qkv_weight, output_weight, modulation):
    base_f = base_latents.astype(jnp.float32)
    noise_f = noise_latents.astype(jnp.float32)
    level_col = noise_levels[:, None, None]
    input_a = ((1.0 - level_col) * base_f + level_col * noise_f).astype(jnp.bfloat16)
    if role_index == 0:
        input_b = replay_latents
        levels_b = replay_levels
        mod_b = modulation[0]
    else:
        input_b = input_a
        levels_b = noise_levels
        mod_b = modulation[1]
    mod_a = modulation[0]
    target = noise_f - base_f
    out_float = output_weight.astype(jnp.float32)

    def one_sample(items):
        rows_a, rows_b, level_a, level_b, cot_rows, target_rows = items
        normed_a = embed_normed(rows_a, embed_weight)
        hidden_a = modulated(normed_a, level_a, mod_a)
        qkv_a = jnp.dot(hidden_a, qkv_weight, preferred_element_type=jnp.float32).astype(jnp.bfloat16)
        mixed_a, _ = attend_heads(qkv_a, HEADS)
        vel_a = jnp.dot(mixed_a, output_weight, preferred_element_type=jnp.float32)
        normed_b = embed_normed(rows_b, embed_weight)
        hidden_b = modulated(normed_b, level_b, mod_b)
        qkv_b = jnp.dot(hidden_b, qkv_weight, preferred_element_type=jnp.float32).astype(jnp.bfloat16)
        mixed_b, weights_b = attend_heads(qkv_b, HEADS)
        vel_b = jnp.dot(mixed_b, output_weight, preferred_element_type=jnp.float32)
        if role_index == 0:
            payload = rows_a.astype(jnp.float32) - level_a * vel_a
            grad_vel = cot_rows.astype(jnp.float32)
        else:
            payload = vel_b - vel_a
            grad_vel = vel_b - target_rows
        grad_mixed = jnp.dot(grad_vel, out_float.T, preferred_element_type=jnp.float32).astype(jnp.bfloat16)
        grad_qkv = attend_back(qkv_b, weights_b, grad_mixed, HEADS)
        grad_hidden = jnp.dot(grad_qkv, qkv_weight.T, preferred_element_type=jnp.float32)
        grad_scale = lax.optimization_barrier(jnp.sum(grad_hidden * normed_b, axis=0)) * level_b
        grad_shift = lax.optimization_barrier(jnp.sum(grad_hidden, axis=0)) * level_b
        return (payload.astype(jnp.bfloat16), jnp.stack([grad_scale, grad_shift]))
    payloads, grads = lax.map(one_sample, (input_a, input_b, noise_levels, levels_b, cotangent, target))
    return (payloads, lax.optimization_barrier(jnp.sum(grads, axis=0)) / (SAMPLES * LENGTH))

def reference(base_latents, noise_latents, noise_levels, replay_latents, replay_levels, cotangent, embed_weight, qkv_weight, output_weight, modulation):
    results = [role_pass(index, base_latents[index], noise_latents[index], noise_levels[index], replay_latents[index], replay_levels[index], cotangent[index], embed_weight[index], qkv_weight[index], output_weight[index], modulation[index]) for index in range(2)]
    crossed = jnp.stack([results[1][0], results[0][0]])
    mod_grads = jnp.stack([results[0][1], results[1][1]])
    return (crossed, mod_grads)
```

```python
import functools

import jax
import jax.numpy as jnp
from jax import lax
from jax.experimental import pallas as pl
from jax.experimental.pallas import tpu as pltpu
from jax.sharding import PartitionSpec as P

HEAD_DIM = 128
CHANNELS = 64
EPSILON = 1e-06
F32 = jnp.float32
BF16 = jnp.bfloat16
NT = (((1,), (1,)), ((), ()))
NN = (((1,), (0,)), ((), ()))
TN = (((0,), (0,)), ((), ()))


def dot(a, b, dims=NN):
    return lax.dot_general(a, b, dims, preferred_element_type=F32)


def round_up(value, step):
    return (value + step - 1) // step * step


def rounded(value):
    return value.astype(BF16).astype(F32)


def three_parts(value):
    high = rounded(value)
    middle = rounded(value - high)
    return high, middle, rounded(value - high - middle)


def lane_index(shape):
    return lax.broadcasted_iota(jnp.int32, shape, len(shape) - 1)


def row_index(shape):
    return lax.broadcasted_iota(jnp.int32, shape, len(shape) - 2)


def pack_kernel(flags, levels, base, noise, replay, cotangent, embed, pack):
    critic = flags[1] == 1
    level = levels[0]
    base_f = base[...].astype(F32)
    noise_f = noise[...].astype(F32)
    input_a = rounded((1.0 - level) * base_f + level * noise_f)
    input_b = jnp.where(critic, input_a, replay[...].astype(F32))
    known = jnp.where(critic, noise_f - base_f, cotangent[...].astype(F32))
    known_high = rounded(known)
    tokens = input_a.shape[0]
    rows = jnp.concatenate([input_a, input_b], axis=0).astype(BF16)
    total = jnp.zeros((2 * tokens, 1), F32)
    width = embed.shape[1]
    for start in range(0, width, 512):
        embedded = dot(rows, embed[:, start : start + 512])
        total = total + jnp.sum(embedded * embedded, axis=-1, keepdims=True)
    scale = lax.rsqrt(total / width + EPSILON)
    lane = lane_index((tokens, 128))
    tail = jnp.zeros((tokens, 128), F32)
    for which in range(2):
        column = scale[which * tokens : (which + 1) * tokens]
        for part, value in enumerate(three_parts(column)):
            tail = jnp.where(lane == which * 3 + part, value, tail)
    pack[:, 0:64] = input_a.astype(BF16)
    pack[:, 64:128] = input_b.astype(BF16)
    pack[:, 128:192] = known_high.astype(BF16)
    pack[:, 192:256] = (known - known_high).astype(BF16)
    pack[:, 256:384] = tail.astype(BF16)


def weight_kernel(chips, flags, levels, weight, received, out, turned):
    first = flags[0] == 0
    rows, columns = received.shape
    own = jnp.where(first, weight[:, 0:columns].astype(F32), weight[:, columns:].astype(F32))
    other = received[...].astype(F32)
    both = [jnp.where(first, own, other), jnp.where(first, other, own)]
    padded = out.shape[2]
    if padded > 2 * rows:
        both.append(jnp.zeros((padded - 2 * rows, columns), F32))
    whole = jnp.concatenate(both, axis=0)
    turned[0:columns, :] = whole.T
    turned[columns:, :] = jnp.zeros((turned.shape[0] - columns, padded), F32)
    block = columns // chips
    height = out.shape[1]
    lane = lane_index((1, padded))
    value = jnp.where(
        lane % 4 == 0,
        levels[0],
        jnp.where(lane % 4 == 1, levels[1], jnp.where(lane % 4 == 2, levels[2], levels[3])),
    )
    parts = three_parts(value)
    line = jnp.zeros((1, padded), F32)
    for index in range(3):
        line = jnp.where(lane // 4 == index, parts[index], line)
    row = row_index((height, padded))
    for chip in range(chips):
        piece = turned[chip * block : chip * block + height, :]
        piece = jnp.where(row < block, piece, jnp.where(row == block, line, 0.0))
        out[chip] = piece.astype(BF16)


def product_kernel(block, taken, embed, modulation_a, modulation_b, out, columns_out, lines):
    chips, height, padded = taken.shape
    width = embed.shape[1]
    depth = width // chips
    row = row_index((height, 1))
    group = 1 if depth % 128 == 0 else 128 // (depth & -depth)
    for start in range(0, chips, group):
        pieces = []
        for chip in range(start, start + group):
            piece = taken[chip].astype(F32)
            lines[chip : chip + 1, :] = piece[block : block + 1, 0:128]
            pieces.append(jnp.where(row < block, piece, 0.0)[:, 0:depth])
        joined = jnp.concatenate(pieces, axis=1) if group > 1 else pieces[0]
        columns_out[:, start * depth : (start + group) * depth] = joined.astype(BF16)
    weight = columns_out[...]
    embed_b = embed[...]
    embed_f = embed_b.astype(F32)
    plain = dot(weight, embed_b, NT)
    scaled_a = dot(weight, (embed_f * modulation_a[0:1, :]).astype(BF16), NT)
    scaled_b = dot(weight, (embed_f * modulation_b[0:1, :]).astype(BF16), NT)
    shifts = []
    for modulation in (modulation_a, modulation_b):
        shift = modulation[1:2, :]
        high = rounded(shift)
        shifts += [high, shift - high]
    shifts.append(jnp.zeros((4, width), F32))
    offsets = dot(jnp.concatenate(shifts, axis=0).astype(BF16), weight, NT)
    offset_a = offsets[0:1] + offsets[1:2]
    offset_b = offsets[2:3] + offsets[3:4]
    high_a = rounded(offset_a)
    high_b = rounded(offset_b)
    offset_rows = (high_a, offset_a - high_a, high_b, offset_b - high_b)
    pick_shape = (128, 4 * CHANNELS)
    source = row_index(pick_shape)
    pick = jnp.where((source < 12) & (source % 4 == lane_index(pick_shape) // CHANNELS), 1.0, 0.0)
    level = dot(lines[...].astype(BF16), pick.astype(BF16))
    plain_all = jnp.concatenate([plain, plain, plain, plain], axis=1)
    scaled_all = jnp.concatenate([scaled_a, scaled_b, scaled_a, scaled_b], axis=1)
    pad = jnp.zeros((1, 4 * CHANNELS - height), F32)
    row_all = row_index((height, 4 * CHANNELS))
    tail = jnp.zeros((height, 4 * CHANNELS), F32)
    for index, line in enumerate(offset_rows):
        wide = jnp.concatenate([line, pad], axis=1) if 4 * CHANNELS > height else line[:, : 4 * CHANNELS]
        tail = jnp.where(row_all == block + index, wide, tail)
    for chip in range(chips):
        matrix = plain_all + level[chip : chip + 1] * scaled_all
        out[chip] = jnp.where(row_all < block, matrix, tail).astype(BF16)


def token_rows(first, second, start, stop):
    return jnp.concatenate([first[:, start:stop], second[:, start:stop]], axis=0)


def inverse_norms(pack_one, pack_two, which):
    tail = token_rows(pack_one, pack_two, 256, 384).astype(F32)
    at = 3 * which
    return tail[:, at : at + 1] + tail[:, at + 1 : at + 2] + tail[:, at + 2 : at + 3]


def forward(which, levels, packs, matrices, offsets, output_weight, keep, velocity):
    heads = output_weight.shape[0] // HEAD_DIM
    offset = offsets[2 * which : 2 * which + 1, :] + offsets[2 * which + 1 : 2 * which + 2, :]
    lane = lane_index((1, 128))
    chosen = lane // CHANNELS == which
    for sample in range(2):
        one, two = packs[2 * sample], packs[2 * sample + 1]
        rows = jnp.where(chosen, token_rows(one, two, 0, 128).astype(F32), 0.0).astype(BF16)
        scale = inverse_norms(one, two, which)
        shift = offset * levels[2 * sample + which]
        total = jnp.zeros((rows.shape[0], CHANNELS), F32)
        for head in range(heads):
            at = head * 3 * HEAD_DIM
            matrix = matrices[at : at + 3 * HEAD_DIM, sample * 128 : (sample + 1) * 128]
            qkv = dot(rows, matrix, NT) * scale + shift[:, at : at + 3 * HEAD_DIM]
            qkv = qkv.astype(BF16)
            if keep is not None:
                keep[sample, :, at : at + 3 * HEAD_DIM] = qkv
            query = qkv[:, 0:HEAD_DIM]
            key = qkv[:, HEAD_DIM : 2 * HEAD_DIM]
            value = qkv[:, 2 * HEAD_DIM :]
            scores = dot(query, key, NT) * (HEAD_DIM**-0.5)
            top = jnp.max(scores, axis=-1, keepdims=True)
            powers = jnp.exp(scores - top)
            probs = powers / jnp.sum(powers, axis=-1, keepdims=True)
            mixed = dot(probs.astype(BF16), value).astype(BF16)
            total = total + dot(mixed, output_weight[head * HEAD_DIM : (head + 1) * HEAD_DIM, :])
        velocity[:, sample * CHANNELS : (sample + 1) * CHANNELS] = total


def second_pass_kernel(
    block, levels, taken, own, seq, core, both, output_weight, matrices, offsets, keep, velocity, stacked
):
    chips = taken.shape[0]
    lines = []
    for chip in range(chips):
        piece = taken[chip].astype(F32)
        stacked[chip * block : (chip + 1) * block, :] = piece[0:block]
        lines.append(piece[block : block + 4, 0:block] if block <= 256 else None)
    matrices[...] = stacked[...].astype(BF16)
    offsets[...] = jnp.concatenate([jnp.concatenate(lines, axis=1), jnp.zeros((4, offsets.shape[1]), F32)], axis=0)
    forward(1, levels, (own, seq, core, both), matrices, offsets, output_weight, keep, velocity)


def first_pass_kernel(levels, matrices, offsets, own, seq, core, both, output_weight, velocity):
    forward(0, levels, (own, seq, core, both), matrices, offsets, output_weight, None, velocity)


def swap_tokens(value):
    half = value.shape[0] // 2
    return jnp.concatenate([value[half:], value[:half]], axis=0)


def backward_kernel(
    block, flags, levels, kept, own, seq, core, both, vel_own, vel_seq, vel_core, vel_both, output_weight, out, gathered
):
    critic = flags[1] == 1
    packs = (own, seq, core, both)
    heads = output_weight.shape[0] // HEAD_DIM
    velocity = vel_own[...] + swap_tokens(vel_seq[...])
    crossing = vel_core[...] + swap_tokens(vel_both[...])
    lane = lane_index((1, 128))
    grads, rows = [], []
    for sample in range(2):
        one, two = packs[2 * sample], packs[2 * sample + 1]
        known = token_rows(one, two, 128, 256).astype(F32)
        known = known[:, 0:CHANNELS] + known[:, CHANNELS:]
        at = sample * CHANNELS
        back = (1 - sample) * CHANNELS
        total = velocity[:, at : at + CHANNELS] + crossing[:, back : back + CHANNELS]
        grads.append(jnp.where(critic, total - known, known).astype(BF16))
        level = levels[2 * sample + 1]
        scaled = token_rows(one, two, 0, 128).astype(F32) * (inverse_norms(one, two, 1) * level)
        level_line = jnp.full((1, 128), level, F32)
        high = rounded(level_line)
        ends = jnp.where(lane == 0, high, jnp.where(lane == 1, level_line - high, 0.0))
        scaled = jnp.where(lane < CHANNELS, ends, scaled)
        rows.append(scaled.T.astype(BF16))
    for head in range(heads):
        at = head * 3 * HEAD_DIM
        total = None
        for sample in range(2):
            qkv = kept[sample, :, at : at + 3 * HEAD_DIM]
            query = qkv[:, 0:HEAD_DIM]
            key = qkv[:, HEAD_DIM : 2 * HEAD_DIM]
            value = qkv[:, 2 * HEAD_DIM :]
            grad_mixed = dot(grads[sample], output_weight[head * HEAD_DIM : (head + 1) * HEAD_DIM, :], NT).astype(BF16)
            scores = dot(key, query, NT) * (HEAD_DIM**-0.5)
            top = jnp.max(scores, axis=0, keepdims=True)
            powers = jnp.exp(scores - top)
            probs = powers / jnp.sum(powers, axis=0, keepdims=True)
            grad_value = dot(probs.astype(BF16), grad_mixed)
            grad_probs = dot(value, grad_mixed, NT)
            inner = jnp.sum(grad_probs * probs, axis=0, keepdims=True)
            grad_scores = (probs * (grad_probs - inner) * (HEAD_DIM**-0.5)).astype(BF16)
            grad_key = dot(grad_scores, query)
            grad_query = dot(grad_scores, key, TN)
            grad = jnp.concatenate([grad_query, grad_key, grad_value], axis=1).astype(BF16)
            term = dot(rows[sample], grad)
            total = term if total is None else total + term
        gathered[at : at + 3 * HEAD_DIM, :] = total.T
    columns = heads * 3 * HEAD_DIM
    gathered[columns:, :] = jnp.zeros((gathered.shape[0] - columns, 128), F32)
    chips, height = out.shape[0], out.shape[1]
    row = row_index((height, 128))
    for chip in range(chips):
        piece = gathered[chip * block : chip * block + height, :]
        out[chip] = jnp.where(row < block, piece, 0.0).astype(BF16)


def closing_kernel(factor, flags, taken, weight, embed, kept, sent):
    first = flags[0] == 0
    total = taken[0].astype(F32)
    for chip in range(1, taken.shape[0]):
        total = total + taken[chip].astype(F32)
    turned = total.T
    high = turned.astype(BF16)
    low = (turned - high.astype(F32)).astype(BF16)
    half = embed.shape[1] // 2
    step = half // 3
    halves = []
    for start in range(0, 2 * half, step):
        columns = weight[:, start : start + step]
        product = dot(high, columns) + dot(low, columns)
        scale = jnp.sum(product[CHANNELS:] * embed[:, start : start + step].astype(F32), axis=0, keepdims=True)
        shift = product[0:1] + product[1:2]
        halves.append(jnp.concatenate([scale, shift], axis=0) * factor)
    left = jnp.concatenate(halves[:3], axis=1)
    right = jnp.concatenate(halves[3:], axis=1)
    kept[...] = jnp.where(first, left, right)
    sent[...] = jnp.where(first, right, left)


def call(kernel, out_shapes, inputs, scalars, scratch=(), flops=0, moved=0):
    specs = [pl.BlockSpec(memory_space=pltpu.SMEM)] * scalars
    specs += [pl.BlockSpec(memory_space=pltpu.VMEM)] * (len(inputs) - scalars)
    return pl.pallas_call(
        kernel,
        out_shape=out_shapes,
        in_specs=specs,
        out_specs=jax.tree.map(lambda _: pl.BlockSpec(memory_space=pltpu.VMEM), out_shapes),
        scratch_shapes=list(scratch),
        compiler_params=pltpu.CompilerParams(vmem_limit_bytes=28 * 2**20),
        cost_estimate=pl.CostEstimate(flops=flops, bytes_accessed=moved, transcendentals=0),
    )(*inputs)


def struct(shape, dtype):
    return jax.ShapeDtypeStruct(shape, dtype)


def other_core(value):
    return lax.ppermute(value, "fsdp", [(i, i ^ 1) for i in range(lax.axis_size("fsdp"))])


def other_half(value):
    return lax.ppermute(value, "seq", [(0, 1), (1, 0)])


def other_both(value):
    count = lax.axis_size("fsdp") * 2
    return lax.ppermute(value, ("fsdp", "seq"), [(i, i ^ 3) for i in range(count)])


def between_chips(value):
    count = lax.axis_size("fsdp")
    groups = [list(range(core, count, 2)) for core in range(2)]
    return lax.all_to_all(value, "fsdp", 0, 0, tiled=True, axis_index_groups=groups)


def per_device(
    base_latents,
    noise_latents,
    noise_levels,
    replay_latents,
    replay_levels,
    cotangent,
    embed_weight,
    qkv_weight,
    output_weight,
    modulation,
):
    is_critic = lax.axis_index("role") == 1
    core = lax.rem(lax.axis_index("fsdp"), 2)
    devices = lax.axis_size("fsdp")
    chips = devices // 2
    embed = embed_weight[0]
    weight = qkv_weight[0]
    width = embed.shape[1]
    columns = weight.shape[1] // 2
    block = columns // chips
    height = round_up(block + 4, 8)
    padded = round_up(2 * weight.shape[0], 128)
    tokens = base_latents.shape[2]
    out_rows = output_weight.shape[1] // 2
    out_half = jnp.where(core == 0, output_weight[0, :out_rows], output_weight[0, out_rows:])

    received = other_core(jnp.where(core == 0, weight[:, columns:], weight[:, :columns]))
    level_two = jnp.where(is_critic, noise_levels[0, 0], replay_levels[0, 0])
    own_levels = jnp.stack([noise_levels[0, 0], level_two])
    levels = jnp.concatenate([own_levels, other_core(own_levels)])
    flags = jnp.stack([core.astype(jnp.int32), is_critic.astype(jnp.int32)])
    modulation_a = modulation[0, 0]
    modulation_b = jnp.where(is_critic, modulation[0, 1], modulation[0, 0])

    own = call(
        pack_kernel,
        struct((tokens, 384), BF16),
        (flags, own_levels, base_latents[0, 0], noise_latents[0, 0], replay_latents[0, 0], cotangent[0, 0], embed),
        2,
    )
    seq, near, both = other_half(own), other_core(own), other_both(own)

    turned = call(
        functools.partial(weight_kernel, chips),
        struct((chips, height, padded), BF16),
        (flags, levels, weight, received),
        2,
        [pltpu.VMEM((columns + height - block, padded), F32)],
    )
    taken = between_chips(turned)
    matrices, own_columns = call(
        functools.partial(product_kernel, block),
        (struct((chips, height, 4 * CHANNELS), BF16), struct((height, width), BF16)),
        (taken, embed, modulation_a, modulation_b),
        0,
        [pltpu.VMEM((chips, 128), F32)],
    )
    taken = between_chips(matrices)

    packs = (own, seq, near, both)
    whole, offsets, kept, vel_b = call(
        functools.partial(second_pass_kernel, block),
        (
            struct((columns, 4 * CHANNELS), BF16),
            struct((8, columns), F32),
            struct((2, 2 * tokens, columns), BF16),
            struct((2 * tokens, 2 * CHANNELS), F32),
        ),
        (levels, taken) + packs + (out_half,),
        1,
        [pltpu.VMEM((columns, 4 * CHANNELS), F32)],
    )
    vel_seq, vel_near, vel_both = other_half(vel_b), other_core(vel_b), other_both(vel_b)
    vel_a = call(
        first_pass_kernel,
        struct((2 * tokens, 2 * CHANNELS), F32),
        (levels, whole, offsets) + packs + (out_half,),
        1,
    )
    products = call(
        functools.partial(backward_kernel, block),
        struct((chips, height, 128), BF16),
        (flags, levels, kept) + packs + (vel_b, vel_seq, vel_near, vel_both, out_half),
        2,
        [pltpu.VMEM((columns + height - block, 128), F32)],
    )

    own_a = vel_a[:tokens, :CHANNELS] + other_half(vel_a[tokens:, :CHANNELS])
    own_a = own_a + other_core(vel_a[:tokens, CHANNELS:]) + other_both(vel_a[tokens:, CHANNELS:])
    own_b = vel_b[:tokens, :CHANNELS] + vel_seq[tokens:, :CHANNELS]
    own_b = own_b + vel_near[:tokens, CHANNELS:] + vel_both[tokens:, CHANNELS:]
    payload = jnp.where(is_critic, own_b - own_a, own[:, :CHANNELS].astype(F32) - own_levels[0] * own_a)
    crossed = lax.ppermute(payload.astype(BF16), "role", [(0, 1), (1, 0)])

    samples = devices * base_latents.shape[1]
    kept_half, sent_half = call(
        functools.partial(closing_kernel, 1.0 / (samples * 2 * tokens)),
        (struct((2, width // 2), F32), struct((2, width // 2), F32)),
        (flags, between_chips(products), own_columns, embed),
        1,
    )
    total = kept_half + other_core(sent_half)
    total = total + other_half(total)
    spread = between_chips(jnp.broadcast_to(total[None], (chips,) + total.shape))
    total = jnp.sum(spread, axis=0)
    near_total = other_core(total)
    mod_grads = jnp.where(
        core == 0,
        jnp.concatenate([total, near_total], axis=1),
        jnp.concatenate([near_total, total], axis=1),
    )
    return (crossed[None, None], mod_grads[None])


def solution(mesh):
    return jax.shard_map(
        per_device,
        mesh=mesh,
        in_specs=(
            P("role", "fsdp", "seq", None),
            P("role", "fsdp", "seq", None),
            P("role", "fsdp"),
            P("role", "fsdp", "seq", None),
            P("role", "fsdp"),
            P("role", "fsdp", "seq", None),
            P("role", None, None),
            P("role", "fsdp", "seq"),
            P("role", "seq", None),
            P("role", None, None, None),
        ),
        out_specs=(P("role", "fsdp", "seq", None), P("role", None, None)),
        check_vma=False,
    )
```

```python
import functools

import jax
import jax.numpy as jnp
from jax import lax
from jax.experimental import pallas as pl
from jax.experimental.pallas import tpu as pltpu
from jax.sharding import PartitionSpec as P

HEAD_DIM = 128
CHANNELS = 64
EPSILON = 1e-06
F32 = jnp.float32
BF16 = jnp.bfloat16
NT = (((1,), (1,)), ((), ()))
NN = (((1,), (0,)), ((), ()))
TN = (((0,), (0,)), ((), ()))


def dot(a, b, dims=NN):
    return lax.dot_general(a, b, dims, preferred_element_type=F32)


def round_up(value, step):
    return (value + step - 1) // step * step


def rounded(value):
    return value.astype(BF16).astype(F32)


def three_parts(value):
    high = rounded(value)
    middle = rounded(value - high)
    return high, middle, rounded(value - high - middle)


def lane_index(shape):
    return lax.broadcasted_iota(jnp.int32, shape, len(shape) - 1)


def row_index(shape):
    return lax.broadcasted_iota(jnp.int32, shape, len(shape) - 2)


def pack_kernel(flags, levels, base, noise, replay, cotangent, embed, pack):
    critic = flags[1] == 1
    level = levels[0]
    base_f = base[...].astype(F32)
    noise_f = noise[...].astype(F32)
    input_a = rounded((1.0 - level) * base_f + level * noise_f)
    input_b = jnp.where(critic, input_a, replay[...].astype(F32))
    known = jnp.where(critic, noise_f - base_f, cotangent[...].astype(F32))
    known_high = rounded(known)
    tokens = input_a.shape[0]
    rows = jnp.concatenate([input_a, input_b], axis=0).astype(BF16)
    total = jnp.zeros((2 * tokens, 1), F32)
    width = embed.shape[1]
    for start in range(0, width, 512):
        embedded = dot(rows, embed[:, start : start + 512])
        total = total + jnp.sum(embedded * embedded, axis=-1, keepdims=True)
    scale = lax.rsqrt(total / width + EPSILON)
    lane = lane_index((tokens, 128))
    tail = jnp.zeros((tokens, 128), F32)
    for which in range(2):
        column = scale[which * tokens : (which + 1) * tokens]
        for part, value in enumerate(three_parts(column)):
            tail = jnp.where(lane == which * 3 + part, value, tail)
    pack[:, 0:64] = input_a.astype(BF16)
    pack[:, 64:128] = input_b.astype(BF16)
    pack[:, 128:192] = known_high.astype(BF16)
    pack[:, 192:256] = (known - known_high).astype(BF16)
    pack[:, 256:384] = tail.astype(BF16)


def weight_kernel(chips, flags, levels, weight, received, out, turned):
    first = flags[0] == 0
    rows, columns = received.shape[0], received.shape[1] // 2
    own = jnp.where(first, weight[:, 0:columns].astype(F32), weight[:, columns:].astype(F32))
    other = jnp.where(first, received[:, 0:columns].astype(F32), received[:, columns:].astype(F32))
    both = [jnp.where(first, own, other), jnp.where(first, other, own)]
    padded = out.shape[2]
    if padded > 2 * rows:
        both.append(jnp.zeros((padded - 2 * rows, columns), F32))
    whole = jnp.concatenate(both, axis=0)
    turned[0:columns, :] = whole.T
    turned[columns:, :] = jnp.zeros((turned.shape[0] - columns, padded), F32)
    block = columns // chips
    height = out.shape[1]
    lane = lane_index((1, padded))
    value = jnp.where(
        lane % 4 == 0,
        levels[0],
        jnp.where(lane % 4 == 1, levels[1], jnp.where(lane % 4 == 2, levels[2], levels[3])),
    )
    parts = three_parts(value)
    line = jnp.zeros((1, padded), F32)
    for index in range(3):
        line = jnp.where(lane // 4 == index, parts[index], line)
    row = row_index((height, padded))
    for chip in range(chips):
        piece = turned[chip * block : chip * block + height, :]
        piece = jnp.where(row < block, piece, jnp.where(row == block, line, 0.0))
        out[chip] = piece.astype(BF16)


def product_kernel(block, flags, taken, embed, modulation, out, halves_out, columns_out, lines):
    critic = flags[1] == 1
    chips, height, padded = taken.shape
    half = block // 2
    stride = halves_out.shape[0] // 2
    row_half = row_index((stride, 1))
    width = embed.shape[1]
    depth = width // chips
    row = row_index((height, 1))
    group = 1 if depth % 128 == 0 else 128 // (depth & -depth)
    for start in range(0, chips, group):
        pieces = []
        for chip in range(start, start + group):
            piece = taken[chip].astype(F32)
            lines[chip : chip + 1, :] = piece[block : block + 1, 0:128]
            pieces.append(jnp.where(row < block, piece, 0.0)[:, 0:depth])
        joined = jnp.concatenate(pieces, axis=1) if group > 1 else pieces[0]
        span = slice(start * depth, (start + group) * depth)
        columns_out[:, span] = joined.astype(BF16)
        longer = jnp.concatenate([joined, jnp.zeros((stride, joined.shape[1]), F32)], axis=0)
        low = jnp.where(row_half < half, longer[0:stride], 0.0)
        high = jnp.where(row_half < half, longer[half : half + stride], 0.0)
        halves_out[:, span] = jnp.concatenate([low, high], axis=0).astype(BF16)
    weight = columns_out[...]
    embed_b = embed[...]
    embed_f = embed_b.astype(F32)
    modulation_a = modulation[0]
    modulation_b = jnp.where(critic, modulation[1], modulation_a)
    plain = dot(weight, embed_b, NT)
    scaled_a = dot(weight, (embed_f * modulation_a[0:1, :]).astype(BF16), NT)
    scaled_b = dot(weight, (embed_f * modulation_b[0:1, :]).astype(BF16), NT)
    shifts = []
    for pair in (modulation_a, modulation_b):
        shift = pair[1:2, :]
        high = rounded(shift)
        shifts += [high, shift - high]
    shifts.append(jnp.zeros((4, width), F32))
    offsets = dot(jnp.concatenate(shifts, axis=0).astype(BF16), weight, NT)
    offset_a = offsets[0:1] + offsets[1:2]
    offset_b = offsets[2:3] + offsets[3:4]
    high_a = rounded(offset_a)
    high_b = rounded(offset_b)
    offset_rows = (high_a, offset_a - high_a, high_b, offset_b - high_b)
    pick_shape = (128, 4 * CHANNELS)
    source = row_index(pick_shape)
    pick = jnp.where((source < 12) & (source % 4 == lane_index(pick_shape) // CHANNELS), 1.0, 0.0)
    level = dot(lines[...].astype(BF16), pick.astype(BF16))
    plain_all = jnp.concatenate([plain, plain, plain, plain], axis=1)
    scaled_all = jnp.concatenate([scaled_a, scaled_b, scaled_a, scaled_b], axis=1)
    pad = jnp.zeros((1, 4 * CHANNELS - height), F32)
    row_all = row_index((height, 4 * CHANNELS))
    tail = jnp.zeros((height, 4 * CHANNELS), F32)
    for index, line in enumerate(offset_rows):
        wide = jnp.concatenate([line, pad], axis=1) if 4 * CHANNELS > height else line[:, : 4 * CHANNELS]
        tail = jnp.where(row_all == block + index, wide, tail)
    for chip in range(chips):
        matrix = plain_all + level[chip : chip + 1] * scaled_all
        out[chip] = jnp.where(row_all < block, matrix, tail).astype(BF16)


def token_rows(packs, sample, start, stop):
    tokens = packs[0].shape[1]
    return jnp.concatenate([pack[sample, :, start:stop] for pack in packs], axis=0).reshape(2 * tokens, stop - start)


def inverse_norms(packs, sample, which):
    tail = token_rows(packs, sample, 256, 384).astype(F32)
    at = 3 * which
    return tail[:, at : at + 1] + tail[:, at + 1 : at + 2] + tail[:, at + 2 : at + 3]


def forward(which, levels, packs, matrices, offsets, output_weight, keep, velocity):
    heads = output_weight.shape[0] // HEAD_DIM
    offset = offsets[2 * which : 2 * which + 1, :] + offsets[2 * which + 1 : 2 * which + 2, :]
    lane = lane_index((1, 128))
    chosen = lane // CHANNELS == which
    for sample in range(2):
        rows = jnp.where(chosen, token_rows(packs, sample, 0, 128).astype(F32), 0.0).astype(BF16)
        scale = inverse_norms(packs, sample, which)
        shift = offset * levels[2 * sample + which]
        total = jnp.zeros((rows.shape[0], CHANNELS), F32)
        for head in range(heads):
            at = head * 3 * HEAD_DIM
            matrix = matrices[at : at + 3 * HEAD_DIM, sample * 128 : (sample + 1) * 128]
            qkv = dot(rows, matrix, NT) * scale + shift[:, at : at + 3 * HEAD_DIM]
            qkv = qkv.astype(BF16)
            if keep is not None:
                keep[sample, :, at : at + 3 * HEAD_DIM] = qkv
            query = qkv[:, 0:HEAD_DIM]
            key = qkv[:, HEAD_DIM : 2 * HEAD_DIM]
            value = qkv[:, 2 * HEAD_DIM :]
            scores = dot(query, key, NT) * (HEAD_DIM**-0.5)
            top = jnp.max(scores, axis=-1, keepdims=True)
            powers = jnp.exp(scores - top)
            probs = powers / jnp.sum(powers, axis=-1, keepdims=True)
            mixed = dot(probs.astype(BF16), value).astype(BF16)
            total = total + dot(mixed, output_weight[head * HEAD_DIM : (head + 1) * HEAD_DIM, :])
        velocity[:, sample * CHANNELS : (sample + 1) * CHANNELS] = total


def second_pass_kernel(
    block, levels, taken, here, there, output_weight, matrices, offsets, keep, velocity, crossing, stacked
):
    chips = taken.shape[0]
    lines = []
    for chip in range(chips):
        piece = taken[chip].astype(F32)
        stacked[chip * block : (chip + 1) * block, :] = piece[0:block]
        lines.append(piece[block : block + 4, 0:block] if block <= 256 else None)
    matrices[...] = stacked[...].astype(BF16)
    offsets[...] = jnp.concatenate([jnp.concatenate(lines, axis=1), jnp.zeros((4, offsets.shape[1]), F32)], axis=0)
    forward(1, levels, (here, there), matrices, offsets, output_weight, keep, velocity)
    crossing[...] = pltpu.roll(velocity[...], CHANNELS, 1)


def first_pass_kernel(levels, matrices, offsets, here, there, output_weight, velocity):
    forward(0, levels, (here, there), matrices, offsets, output_weight, None, velocity)


def swap_tokens(value):
    half = value.shape[0] // 2
    return jnp.concatenate([value[half:], value[:half]], axis=0)


def backward_kernel(block, flags, levels, kept, here, there, vel_here, vel_there, output_weight, out, gathered, summed):
    critic = flags[1] == 1
    packs = (here, there)
    heads = output_weight.shape[0] // HEAD_DIM
    velocity = vel_here[...] + swap_tokens(vel_there[...])
    lane = lane_index((1, 128))
    grads, rows = [], []
    for sample in range(2):
        known = token_rows(packs, sample, 128, 256).astype(F32)
        known = known[:, 0:CHANNELS] + known[:, CHANNELS:]
        total = velocity[:, sample * CHANNELS : (sample + 1) * CHANNELS]
        grads.append(jnp.where(critic, total - known, known).astype(BF16))
        inputs = token_rows(packs, sample, 0, 128).astype(F32)
        inputs = jnp.where(lane < CHANNELS, pltpu.roll(inputs, CHANNELS, 1), inputs)
        scaled = inputs * (inverse_norms(packs, sample, 1) * levels[2 * sample + 1])
        rows.append(scaled.T.astype(BF16))
    for head in range(heads):
        at = head * 3 * HEAD_DIM
        total, ends = None, None
        for sample in range(2):
            qkv = kept[sample, :, at : at + 3 * HEAD_DIM]
            query = qkv[:, 0:HEAD_DIM]
            key = qkv[:, HEAD_DIM : 2 * HEAD_DIM]
            value = qkv[:, 2 * HEAD_DIM :]
            grad_mixed = dot(grads[sample], output_weight[head * HEAD_DIM : (head + 1) * HEAD_DIM, :], NT).astype(BF16)
            scores = dot(key, query, NT) * (HEAD_DIM**-0.5)
            top = jnp.max(scores, axis=0, keepdims=True)
            powers = jnp.exp(scores - top)
            probs = powers / jnp.sum(powers, axis=0, keepdims=True)
            grad_value = dot(probs.astype(BF16), grad_mixed)
            grad_probs = dot(value, grad_mixed, NT)
            inner = jnp.sum(grad_probs * probs, axis=0, keepdims=True)
            grad_scores = (probs * (grad_probs - inner) * (HEAD_DIM**-0.5)).astype(BF16)
            grad_key = dot(grad_scores, query)
            grad_query = dot(grad_scores, key, TN)
            grad = jnp.concatenate([grad_query, grad_key, grad_value], axis=1).astype(BF16)
            term = dot(rows[sample], grad)
            end = jnp.sum(grad.astype(F32), axis=0, keepdims=True) * levels[2 * sample + 1]
            total = term if total is None else total + term
            ends = end if ends is None else ends + end
        gathered[at : at + 3 * HEAD_DIM, :] = total.T
        summed[:, at : at + 3 * HEAD_DIM] = ends
    columns = heads * 3 * HEAD_DIM
    gathered[columns:, :] = jnp.zeros((gathered.shape[0] - columns, 128), F32)
    chips, height = out.shape[0], out.shape[1]
    half = block // 2
    row = row_index((height, 128))
    low_lanes = lane_index((height, 128)) < CHANNELS
    pad = jnp.zeros((1, 128 - block), F32) if block < 128 else None
    for chip in range(chips):
        at = chip * block
        piece = jnp.where(low_lanes, gathered[at : at + height, :], gathered[at + half : at + half + height, :])
        line = summed[:, at : at + block]
        high = rounded(line)
        pair = [high, line - high]
        if pad is not None:
            pair = [jnp.concatenate([part, pad], axis=1) for part in pair]
        piece = jnp.where(row < half, piece, jnp.where(row == half, pair[0], jnp.where(row == half + 1, pair[1], 0.0)))
        out[chip] = piece.astype(BF16)


def closing_kernel(block, factor, flags, taken, weight, embed, kept, sent):
    first = flags[0] == 0
    total = taken[0].astype(F32)
    for chip in range(1, taken.shape[0]):
        total = total + taken[chip].astype(F32)
    half = block // 2
    height = total.shape[0]
    row = row_index((height, 128))
    ends = total[half : half + 1] + total[half + 1 : half + 2]
    turned = jnp.where(row < half, total, 0.0).T
    lane = lane_index((1, 128))
    ends_low = jnp.where(lane < half, ends, 0.0)[:, 0:height]
    ends_high = jnp.where(lane < half, pltpu.roll(ends, 128 - half, 1), 0.0)[:, 0:height]
    lower = jnp.concatenate([turned[0:CHANNELS], ends_low, jnp.zeros((7, height), F32)], axis=0)
    upper = jnp.concatenate([turned[CHANNELS:], ends_high, jnp.zeros((7, height), F32)], axis=0)
    joined = jnp.concatenate([lower, upper], axis=1)
    high = joined.astype(BF16)
    low = (joined - high.astype(F32)).astype(BF16)
    middle = embed.shape[1] // 2
    step = middle // 3
    parts = []
    for start in range(0, 2 * middle, step):
        columns = weight[:, start : start + step]
        product = dot(high, columns) + dot(low, columns)
        scale = jnp.sum(product[:CHANNELS] * embed[:, start : start + step].astype(F32), axis=0, keepdims=True)
        parts.append(jnp.concatenate([scale, product[CHANNELS : CHANNELS + 1]], axis=0) * factor)
    left = jnp.concatenate(parts[:3], axis=1)
    right = jnp.concatenate(parts[3:], axis=1)
    kept[...] = jnp.where(first, left, right)
    sent[...] = jnp.where(first, right, left)


def call(kernel, out_shapes, inputs, scalars, scratch=(), flops=0, moved=0):
    specs = [pl.BlockSpec(memory_space=pltpu.SMEM)] * scalars
    specs += [pl.BlockSpec(memory_space=pltpu.VMEM)] * (len(inputs) - scalars)
    return pl.pallas_call(
        kernel,
        out_shape=out_shapes,
        in_specs=specs,
        out_specs=jax.tree.map(lambda _: pl.BlockSpec(memory_space=pltpu.VMEM), out_shapes),
        scratch_shapes=list(scratch),
        compiler_params=pltpu.CompilerParams(vmem_limit_bytes=28 * 2**20),
        cost_estimate=pl.CostEstimate(flops=flops, bytes_accessed=moved, transcendentals=0),
    )(*inputs)


def struct(shape, dtype):
    return jax.ShapeDtypeStruct(shape, dtype)


def other_core(value):
    return lax.ppermute(value, "fsdp", [(i, i ^ 1) for i in range(lax.axis_size("fsdp"))])


def other_half(value):
    return lax.ppermute(value, "seq", [(0, 1), (1, 0)])


def between_chips(value):
    count = lax.axis_size("fsdp")
    groups = [list(range(core, count, 2)) for core in range(2)]
    return lax.all_to_all(value, "fsdp", 0, 0, tiled=True, axis_index_groups=groups)


def per_device(
    base_latents,
    noise_latents,
    noise_levels,
    replay_latents,
    replay_levels,
    cotangent,
    embed_weight,
    qkv_weight,
    output_weight,
    modulation,
):
    is_critic = lax.axis_index("role") == 1
    core = lax.rem(lax.axis_index("fsdp"), 2)
    devices = lax.axis_size("fsdp")
    chips = devices // 2
    embed = embed_weight[0]
    weight = qkv_weight[0]
    width = embed.shape[1]
    columns = weight.shape[1] // 2
    block = columns // chips
    height = round_up(block + 4, 8)
    padded = round_up(2 * weight.shape[0], 128)
    tokens = base_latents.shape[2]
    out_rows = output_weight.shape[1] // 2
    out_half = jnp.where(core == 0, output_weight[0, :out_rows], output_weight[0, out_rows:])

    received = other_core(weight)
    level_two = jnp.where(is_critic, noise_levels[0, 0], replay_levels[0, 0])
    own_levels = jnp.stack([noise_levels[0, 0], level_two])
    levels = jnp.concatenate([own_levels, other_core(own_levels)])
    flags = jnp.stack([core.astype(jnp.int32), is_critic.astype(jnp.int32)])
    own = call(
        pack_kernel,
        struct((tokens, 384), BF16),
        (flags, own_levels, base_latents[0, 0], noise_latents[0, 0], replay_latents[0, 0], cotangent[0, 0], embed),
        2,
    )
    here = jnp.stack([own, other_core(own)])
    there = other_half(here)

    turned = call(
        functools.partial(weight_kernel, chips),
        struct((chips, height, padded), BF16),
        (flags, levels, weight, received),
        2,
        [pltpu.VMEM((columns + height - block, padded), F32)],
    )
    taken = between_chips(turned)
    packed = round_up(block // 2 + 2, 8)
    matrices, own_columns = call(
        functools.partial(product_kernel, block),
        (struct((chips, height, 4 * CHANNELS), BF16), struct((2 * packed, width), BF16)),
        (flags, taken, embed, modulation[0]),
        1,
        [pltpu.VMEM((height, width), BF16), pltpu.VMEM((chips, 128), F32)],
    )
    taken = between_chips(matrices)

    whole, offsets, kept, vel_b, vel_crossing = call(
        functools.partial(second_pass_kernel, block),
        (
            struct((columns, 4 * CHANNELS), BF16),
            struct((8, columns), F32),
            struct((2, 2 * tokens, columns), BF16),
            struct((2 * tokens, 2 * CHANNELS), F32),
            struct((2 * tokens, 2 * CHANNELS), F32),
        ),
        (levels, taken, here, there, out_half),
        1,
        [pltpu.VMEM((columns, 4 * CHANNELS), F32)],
    )
    vel_here = vel_b + other_core(vel_crossing)
    vel_there = other_half(vel_here)
    vel_a = call(
        first_pass_kernel,
        struct((2 * tokens, 2 * CHANNELS), F32),
        (levels, whole, offsets, here, there, out_half),
        1,
        flops=4 * 10**9,
    )
    vel_there, vel_a = lax.optimization_barrier((vel_there, vel_a))
    products = call(
        functools.partial(backward_kernel, block),
        struct((chips, packed, 128), BF16),
        (flags, levels, kept, here, there, vel_here, vel_there, out_half),
        2,
        [pltpu.VMEM((columns + 2 * packed, 128), F32), pltpu.VMEM((1, columns), F32)],
    )
    gathered = between_chips(products)

    own_a = vel_a[:, :CHANNELS] + other_core(vel_a[:, CHANNELS:])
    own_a = own_a[:tokens] + other_half(own_a[tokens:])
    own_b = vel_here[:tokens, :CHANNELS] + vel_there[tokens:, :CHANNELS]
    payload = jnp.where(is_critic, own_b - own_a, own[:, :CHANNELS].astype(F32) - own_levels[0] * own_a)
    payload = payload.astype(BF16)
    gathered, payload = lax.optimization_barrier((gathered, payload))
    crossed = lax.ppermute(payload, "role", [(0, 1), (1, 0)])

    samples = devices * base_latents.shape[1]
    kept_half, sent_half = call(
        functools.partial(closing_kernel, block, 1.0 / (samples * 2 * tokens)),
        (struct((2, width // 2), F32), struct((2, width // 2), F32)),
        (flags, gathered, own_columns, embed),
        1,
    )
    total = kept_half + other_core(sent_half)
    total = total + other_half(total)
    spread = between_chips(jnp.broadcast_to(total[None], (chips,) + total.shape))
    total = jnp.sum(spread, axis=0)
    near_total = other_core(total)
    mod_grads = jnp.where(
        core == 0,
        jnp.concatenate([total, near_total], axis=1),
        jnp.concatenate([near_total, total], axis=1),
    )
    return (crossed[None, None], mod_grads[None])


def solution(mesh):
    return jax.shard_map(
        per_device,
        mesh=mesh,
        in_specs=(
            P("role", "fsdp", "seq", None),
            P("role", "fsdp", "seq", None),
            P("role", "fsdp"),
            P("role", "fsdp", "seq", None),
            P("role", "fsdp"),
            P("role", "fsdp", "seq", None),
            P("role", None, None),
            P("role", "fsdp", "seq"),
            P("role", "seq", None),
            P("role", None, None, None),
        ),
        out_specs=(P("role", "fsdp", "seq", None), P("role", None, None)),
        check_vma=False,
    )
```

```python
import functools

import jax
import jax.numpy as jnp
from jax import lax
from jax.experimental import pallas as pl
from jax.experimental.pallas import tpu as pltpu
from jax.sharding import PartitionSpec as P

HEAD_DIM = 128
CHANNELS = 64
EPSILON = 1e-06
F32 = jnp.float32
BF16 = jnp.bfloat16
NT = (((1,), (1,)), ((), ()))
NN = (((1,), (0,)), ((), ()))
TN = (((0,), (0,)), ((), ()))


def dot(a, b, dims=NN):
    return lax.dot_general(a, b, dims, preferred_element_type=F32)


def round_up(value, step):
    return (value + step - 1) // step * step


def rounded(value):
    return value.astype(BF16).astype(F32)


def three_parts(value):
    high = rounded(value)
    middle = rounded(value - high)
    return high, middle, rounded(value - high - middle)


def lane_index(shape):
    return lax.broadcasted_iota(jnp.int32, shape, len(shape) - 1)


def row_index(shape):
    return lax.broadcasted_iota(jnp.int32, shape, len(shape) - 2)


def on_second_core():
    return lax.rem(lax.axis_index("fsdp"), 2) == 1


def on_critic():
    return lax.axis_index("role") == 1


def pack_kernel(noise_levels, replay_levels, base, noise, replay, cotangent, embed, pack):
    critic = on_critic()
    level = noise_levels[0, 0]
    level_two = jnp.where(critic, level, replay_levels[0, 0])
    base_f = base[...].astype(F32)
    noise_f = noise[...].astype(F32)
    input_a = rounded((1.0 - level) * base_f + level * noise_f)
    input_b = jnp.where(critic, input_a, replay[...].astype(F32))
    known = jnp.where(critic, noise_f - base_f, cotangent[...].astype(F32))
    known_high = rounded(known)
    tokens = input_a.shape[0]
    rows = jnp.concatenate([input_a, input_b], axis=0).astype(BF16)
    total = jnp.zeros((2 * tokens, 1), F32)
    width = embed.shape[1]
    for start in range(0, width, 512):
        embedded = dot(rows, embed[:, start : start + 512])
        total = total + jnp.sum(embedded * embedded, axis=-1, keepdims=True)
    scale = lax.rsqrt(total / width + EPSILON)
    lane = lane_index((tokens, 128))
    tail = jnp.zeros((tokens, 128), F32)
    ones = jnp.ones((tokens, 1), F32)
    for which, column in enumerate((scale[:tokens], scale[tokens:], ones * level, ones * level_two)):
        for part, value in enumerate(three_parts(column)):
            tail = jnp.where(lane == which * 3 + part, value, tail)
    pack[:, 0:64] = input_a.astype(BF16)
    pack[:, 64:128] = input_b.astype(BF16)
    pack[:, 128:192] = known_high.astype(BF16)
    pack[:, 192:256] = (known - known_high).astype(BF16)
    pack[:, 256:384] = tail.astype(BF16)


def cut_kernel(weight, keep, send):
    second = on_second_core()
    columns = keep.shape[1]
    left = weight[:, 0:columns].astype(F32)
    right = weight[:, columns:].astype(F32)
    keep[...] = jnp.where(second, right, left).astype(BF16)
    send[...] = jnp.where(second, left, right).astype(BF16)


def weight_kernel(chips, keep, received, out, turned):
    second = on_second_core()
    rows, columns = received.shape
    own = keep[...].astype(F32)
    other = received[...].astype(F32)
    both = [jnp.where(second, other, own), jnp.where(second, own, other)]
    padded = out.shape[2]
    if padded > 2 * rows:
        both.append(jnp.zeros((padded - 2 * rows, columns), F32))
    turned[0:columns, :] = jnp.concatenate(both, axis=0).T
    turned[columns:, :] = jnp.zeros((turned.shape[0] - columns, padded), F32)
    block = columns // chips
    height = out.shape[1]
    row = row_index((height, padded))
    for chip in range(chips):
        piece = turned[chip * block : chip * block + height, :]
        out[chip] = jnp.where(row < block, piece, 0.0).astype(BF16)


def product_kernel(block, taken, embed, modulation, out, halves_out, columns_out):
    critic = on_critic()
    chips, height, padded = taken.shape
    half = block // 2
    stride = halves_out.shape[0] // 2
    width = embed.shape[1]
    depth = width // chips
    row_half = row_index((stride, 1))
    group = 1 if depth % 128 == 0 else 128 // (depth & -depth)
    for start in range(0, chips, group):
        pieces = [taken[chip].astype(F32)[:, 0:depth] for chip in range(start, start + group)]
        joined = jnp.concatenate(pieces, axis=1) if group > 1 else pieces[0]
        span = slice(start * depth, (start + group) * depth)
        columns_out[:, span] = joined.astype(BF16)
        longer = jnp.concatenate([joined, jnp.zeros((stride, joined.shape[1]), F32)], axis=0)
        low = jnp.where(row_half < half, longer[0:stride], 0.0)
        high = jnp.where(row_half < half, longer[half : half + stride], 0.0)
        halves_out[:, span] = jnp.concatenate([low, high], axis=0).astype(BF16)
    weight = columns_out[...]
    embed_b = embed[...]
    embed_f = embed_b.astype(F32)
    modulation_a = modulation[0]
    modulation_b = jnp.where(critic, modulation[1], modulation_a)
    scaled_a = (embed_f * modulation_a[0:1, :]).astype(BF16)
    scaled_b = (embed_f * modulation_b[0:1, :]).astype(BF16)
    first = dot(weight, jnp.concatenate([embed_b, scaled_a], axis=0), NT)
    second = dot(weight, jnp.concatenate([scaled_b, scaled_b], axis=0), NT)
    shifts = []
    for pair in (modulation_a, modulation_b):
        shift = pair[1:2, :]
        high = rounded(shift)
        shifts += [high, shift - high]
    shifts.append(jnp.zeros((4, width), F32))
    offsets = dot(jnp.concatenate(shifts, axis=0).astype(BF16), weight, NT)
    lines = []
    gap = jnp.zeros((1, CHANNELS - block), F32)
    for offset in (offsets[0:1, 0:block] + offsets[1:2, 0:block], offsets[2:3, 0:block] + offsets[3:4, 0:block]):
        high = rounded(offset)
        lines.append(jnp.concatenate([high, gap, offset - high, gap], axis=1))
    low_lanes = lane_index((half, 128)) < CHANNELS
    folded = jnp.where(low_lanes, second[0:half], second[half:block])
    spare = out.shape[1] - block - half - 2
    parts = [first[0:block], folded] + lines
    if spare:
        parts.append(jnp.zeros((spare, 128), F32))
    whole = jnp.concatenate(parts, axis=0).astype(BF16)
    for chip in range(chips):
        out[chip] = whole


def token_rows(packs, sample, start, stop):
    return jnp.concatenate([pack[sample, :, start:stop] for pack in packs], axis=0)


def tail_column(packs, sample, which):
    tail = token_rows(packs, sample, 256, 384).astype(F32)
    at = 3 * which
    return tail[:, at : at + 1] + tail[:, at + 1 : at + 2] + tail[:, at + 2 : at + 3]


def forward(which, packs, matrices, offsets, output_weight, keep, velocity):
    heads = output_weight.shape[0] // HEAD_DIM
    low_lanes = lane_index((1, 128)) < CHANNELS
    rows, scales, levels = [], [], []
    for sample in range(2):
        inputs = token_rows(packs, sample, 0, 128).astype(F32)
        turned = pltpu.roll(inputs, CHANNELS, 1)
        level = tail_column(packs, sample, 2 + which)
        plain, scaled = (turned, inputs) if which else (inputs, turned)
        rows.append(jnp.where(low_lanes, plain, scaled * level).astype(BF16))
        scales.append(tail_column(packs, sample, which))
        levels.append(level[0:1])
    tokens = rows[0].shape[0]
    inputs = jnp.concatenate(rows, axis=0)
    totals = [jnp.zeros((tokens, CHANNELS), F32), jnp.zeros((tokens, CHANNELS), F32)]
    for head in range(heads):
        at = head * 3 * HEAD_DIM
        product = dot(inputs, matrices[at : at + 3 * HEAD_DIM, :], NT)
        offset = offsets[which : which + 1, at : at + 3 * HEAD_DIM]
        for sample in range(2):
            qkv = product[sample * tokens : (sample + 1) * tokens] * scales[sample] + offset * levels[sample]
            qkv = qkv.astype(BF16)
            if keep is not None:
                keep[sample, :, at : at + 3 * HEAD_DIM] = qkv
            query = qkv[:, 0:HEAD_DIM]
            key = qkv[:, HEAD_DIM : 2 * HEAD_DIM]
            value = qkv[:, 2 * HEAD_DIM :]
            scores = dot(query, key, NT) * (HEAD_DIM**-0.5)
            top = jnp.max(scores, axis=-1, keepdims=True)
            powers = jnp.exp(scores - top)
            probs = powers / jnp.sum(powers, axis=-1, keepdims=True)
            mixed = dot(probs.astype(BF16), value).astype(BF16)
            totals[sample] = totals[sample] + dot(mixed, output_weight[head * HEAD_DIM : (head + 1) * HEAD_DIM, :])
    velocity[...] = jnp.concatenate(totals, axis=1)


def second_pass_kernel(
    block, taken, here, there, output_weight, matrices, offsets, keep, velocity, crossing, stacked, stacked_two
):
    chips = taken.shape[0]
    half = block // 2
    low_lanes = lane_index((half, 128)) < CHANNELS
    lines = [[], []]
    for chip in range(chips):
        piece = taken[chip].astype(F32)
        at = chip * block
        stacked[at : at + block, :] = piece[0:block]
        folded = piece[block : block + half]
        turned = pltpu.roll(folded, CHANNELS, 1)
        stacked_two[at : at + half, :] = jnp.where(low_lanes, piece[0:half], turned)
        stacked_two[at + half : at + block, :] = jnp.where(low_lanes, piece[half:block], folded)
        for which in range(2):
            line = piece[block + half + which : block + half + which + 1]
            lines[which].append((line + pltpu.roll(line, CHANNELS, 1))[:, 0:block])
    matrices[...] = stacked[...].astype(BF16)
    joined = [jnp.concatenate(line, axis=1) for line in lines]
    offsets[...] = jnp.concatenate(joined + [jnp.zeros((6, offsets.shape[1]), F32)], axis=0)
    forward(1, (here, there), stacked_two[...].astype(BF16), offsets, output_weight, keep, velocity)
    crossing[...] = pltpu.roll(velocity[...], CHANNELS, 1)


def first_pass_kernel(matrices, offsets, here, there, output_weight, velocity):
    forward(0, (here, there), matrices, offsets, output_weight, None, velocity)


def probs_kernel(kept, out):
    heads = out.shape[0] // 2
    for unit in range(2 * heads):
        at = unit // 2 * 3 * HEAD_DIM
        qkv = kept[unit % 2, :, at : at + 2 * HEAD_DIM]
        scores = dot(qkv[:, HEAD_DIM:], qkv[:, 0:HEAD_DIM], NT) * (HEAD_DIM**-0.5)
        top = jnp.max(scores, axis=0, keepdims=True)
        powers = jnp.exp(scores - top)
        out[unit] = powers / jnp.sum(powers, axis=0, keepdims=True)


def swap_tokens(value):
    half = value.shape[0] // 2
    return jnp.concatenate([value[half:], value[:half]], axis=0)


def backward_kernel(block, kept, probs_turned, here, there, vel_here, vel_there, output_weight, out, gathered, summed):
    critic = on_critic()
    packs = (here, there)
    heads = output_weight.shape[0] // HEAD_DIM
    velocity = vel_here[...] + swap_tokens(vel_there[...])
    lane = lane_index((1, 128))
    grads, rows, levels = [], [], []
    for sample in range(2):
        known = token_rows(packs, sample, 128, 256).astype(F32)
        known = known[:, 0:CHANNELS] + known[:, CHANNELS:]
        total = velocity[:, sample * CHANNELS : (sample + 1) * CHANNELS]
        grads.append(jnp.where(critic, total - known, known).astype(BF16))
        inputs = token_rows(packs, sample, 0, 128).astype(F32)
        inputs = jnp.where(lane < CHANNELS, pltpu.roll(inputs, CHANNELS, 1), inputs)
        level = tail_column(packs, sample, 3)
        levels.append(level[0:1])
        scaled = inputs * (tail_column(packs, sample, 1) * level)
        rows.append(scaled.T.astype(BF16))
    for head in range(heads):
        at = head * 3 * HEAD_DIM
        total, ends = None, None
        for sample in range(2):
            qkv = kept[sample, :, at : at + 3 * HEAD_DIM]
            query = qkv[:, 0:HEAD_DIM]
            key = qkv[:, HEAD_DIM : 2 * HEAD_DIM]
            value = qkv[:, 2 * HEAD_DIM :]
            grad_mixed = dot(grads[sample], output_weight[head * HEAD_DIM : (head + 1) * HEAD_DIM, :], NT).astype(BF16)
            probs = probs_turned[2 * head + sample]
            grad_value = dot(probs.astype(BF16), grad_mixed)
            grad_probs = dot(value, grad_mixed, NT)
            inner = jnp.sum(grad_probs * probs, axis=0, keepdims=True)
            grad_scores = (probs * (grad_probs - inner) * (HEAD_DIM**-0.5)).astype(BF16)
            grad_key = dot(grad_scores, query)
            grad_query = dot(grad_scores, key, TN)
            grad = jnp.concatenate([grad_query, grad_key, grad_value], axis=1).astype(BF16)
            term = dot(rows[sample], grad)
            end = jnp.sum(grad.astype(F32), axis=0, keepdims=True) * levels[sample]
            total = term if total is None else total + term
            ends = end if ends is None else ends + end
        gathered[at : at + 3 * HEAD_DIM, :] = total.T
        summed[:, at : at + 3 * HEAD_DIM] = ends
    columns = heads * 3 * HEAD_DIM
    gathered[columns:, :] = jnp.zeros((gathered.shape[0] - columns, 128), F32)
    chips, height = out.shape[0], out.shape[1]
    half = block // 2
    row = row_index((height, 128))
    low_lanes = lane_index((height, 128)) < CHANNELS
    pad = jnp.zeros((1, 128 - block), F32) if block < 128 else None
    for chip in range(chips):
        at = chip * block
        piece = jnp.where(low_lanes, gathered[at : at + height, :], gathered[at + half : at + half + height, :])
        line = summed[:, at : at + block]
        high = rounded(line)
        pair = [high, line - high]
        if pad is not None:
            pair = [jnp.concatenate([part, pad], axis=1) for part in pair]
        piece = jnp.where(row < half, piece, jnp.where(row == half, pair[0], jnp.where(row == half + 1, pair[1], 0.0)))
        out[chip] = piece.astype(BF16)


def closing_kernel(block, factor, taken, weight, embed, kept, sent):
    second = on_second_core()
    total = taken[0].astype(F32)
    for chip in range(1, taken.shape[0]):
        total = total + taken[chip].astype(F32)
    half = block // 2
    height = total.shape[0]
    row = row_index((height, 128))
    ends = total[half : half + 1] + total[half + 1 : half + 2]
    turned = jnp.where(row < half, total, 0.0).T
    lane = lane_index((1, 128))
    ends_low = jnp.where(lane < half, ends, 0.0)[:, 0:height]
    ends_high = jnp.where(lane < half, pltpu.roll(ends, 128 - half, 1), 0.0)[:, 0:height]
    lower = jnp.concatenate([turned[0:CHANNELS], ends_low, jnp.zeros((7, height), F32)], axis=0)
    upper = jnp.concatenate([turned[CHANNELS:], ends_high, jnp.zeros((7, height), F32)], axis=0)
    joined = jnp.concatenate([lower, upper], axis=1)
    high = joined.astype(BF16)
    low = (joined - high.astype(F32)).astype(BF16)
    middle = embed.shape[1] // 2
    step = middle // 3
    parts = []
    for start in range(0, 2 * middle, step):
        columns = weight[:, start : start + step]
        product = dot(high, columns) + dot(low, columns)
        scale = jnp.sum(product[:CHANNELS] * embed[:, start : start + step].astype(F32), axis=0, keepdims=True)
        parts.append(jnp.concatenate([scale, product[CHANNELS : CHANNELS + 1]], axis=0) * factor)
    left = jnp.concatenate(parts[:3], axis=1)
    right = jnp.concatenate(parts[3:], axis=1)
    kept[...] = jnp.where(second, right, left)
    sent[...] = jnp.where(second, left, right)


def call(kernel, out_shapes, inputs, scalars=0, scratch=(), flops=0, moved=0):
    specs = [pl.BlockSpec(memory_space=pltpu.SMEM)] * scalars
    specs += [pl.BlockSpec(memory_space=pltpu.VMEM)] * (len(inputs) - scalars)
    return pl.pallas_call(
        kernel,
        out_shape=out_shapes,
        in_specs=specs,
        out_specs=jax.tree.map(lambda _: pl.BlockSpec(memory_space=pltpu.VMEM), out_shapes),
        scratch_shapes=list(scratch),
        compiler_params=pltpu.CompilerParams(vmem_limit_bytes=28 * 2**20),
        cost_estimate=pl.CostEstimate(flops=flops, bytes_accessed=moved, transcendentals=0),
    )(*inputs)


def struct(shape, dtype):
    return jax.ShapeDtypeStruct(shape, dtype)


def other_core(value):
    return lax.ppermute(value, "fsdp", [(i, i ^ 1) for i in range(lax.axis_size("fsdp"))])


def other_half(value):
    return lax.ppermute(value, "seq", [(0, 1), (1, 0)])


def between_chips(value):
    count = lax.axis_size("fsdp")
    groups = [list(range(core, count, 2)) for core in range(2)]
    return lax.all_to_all(value, "fsdp", 0, 0, tiled=True, axis_index_groups=groups)


def per_device(
    base_latents,
    noise_latents,
    noise_levels,
    replay_latents,
    replay_levels,
    cotangent,
    embed_weight,
    qkv_weight,
    output_weight,
    modulation,
):
    is_critic = on_critic()
    second_core = on_second_core()
    devices = lax.axis_size("fsdp")
    chips = devices // 2
    embed = embed_weight[0]
    weight = qkv_weight[0]
    width = embed.shape[1]
    columns = weight.shape[1] // 2
    block = columns // chips
    height = round_up(block, 8)
    packed = round_up(block + block // 2 + 2, 8)
    folded = round_up(block // 2 + 2, 8)
    padded = round_up(2 * weight.shape[0], 128)
    tokens = base_latents.shape[2]
    heads = columns // (3 * HEAD_DIM)
    out_rows = output_weight.shape[1] // 2
    out_half = jnp.where(second_core, output_weight[0, out_rows:], output_weight[0, :out_rows])

    keep, send = call(
        cut_kernel,
        (struct((weight.shape[0], columns), BF16), struct((weight.shape[0], columns), BF16)),
        (weight,),
    )
    turned = call(
        functools.partial(weight_kernel, chips),
        struct((chips, height, padded), BF16),
        (keep, other_core(send)),
        scratch=[pltpu.VMEM((columns + height - block, padded), F32)],
    )

    own = call(
        pack_kernel,
        struct((tokens, 384), BF16),
        (
            noise_levels,
            replay_levels,
            base_latents[0, 0],
            noise_latents[0, 0],
            replay_latents[0, 0],
            cotangent[0, 0],
            embed,
        ),
        scalars=2,
    )
    here = jnp.stack([own, other_core(own)])
    there = other_half(here)

    matrices, own_columns = call(
        functools.partial(product_kernel, block),
        (struct((chips, packed, 128), BF16), struct((2 * folded, width), BF16)),
        (between_chips(turned), embed, modulation[0]),
        scratch=[pltpu.VMEM((height, width), BF16)],
    )
    whole, offsets, kept, vel_b, vel_crossing = call(
        functools.partial(second_pass_kernel, block),
        (
            struct((columns, 2 * CHANNELS), BF16),
            struct((8, columns), F32),
            struct((2, 2 * tokens, columns), BF16),
            struct((2 * tokens, 2 * CHANNELS), F32),
            struct((2 * tokens, 2 * CHANNELS), F32),
        ),
        (between_chips(matrices), here, there, out_half),
        scratch=[pltpu.VMEM((columns, 2 * CHANNELS), F32), pltpu.VMEM((columns, 2 * CHANNELS), F32)],
    )
    vel_here = vel_b + other_core(vel_crossing)
    vel_there = other_half(vel_here)
    probs = call(probs_kernel, struct((2 * heads, 2 * tokens, 2 * tokens), F32), (kept,), flops=2 * 10**9)
    vel_there, probs = lax.optimization_barrier((vel_there, probs))
    products = call(
        functools.partial(backward_kernel, block),
        struct((chips, folded, 128), BF16),
        (kept, probs, here, there, vel_here, vel_there, out_half),
        scratch=[pltpu.VMEM((columns + 2 * folded, 128), F32), pltpu.VMEM((1, columns), F32)],
    )
    gathered = between_chips(products)

    vel_a = call(
        first_pass_kernel,
        struct((2 * tokens, 2 * CHANNELS), F32),
        (whole, offsets, here, there, out_half),
        flops=4 * 10**9,
    )
    own_a = vel_a[:, :CHANNELS] + other_core(vel_a[:, CHANNELS:])
    gathered, own_a = lax.optimization_barrier((gathered, own_a))
    own_a = own_a[:tokens] + other_half(own_a[tokens:])
    own_b = vel_here[:tokens, :CHANNELS] + vel_there[tokens:, :CHANNELS]
    sample = own[:, :CHANNELS].astype(F32) - noise_levels[0, 0] * own_a
    payload = jnp.where(is_critic, own_b - own_a, sample).T
    crossed = lax.ppermute(payload.astype(BF16), "role", [(0, 1), (1, 0)]).T

    samples = devices * base_latents.shape[1]
    kept_half, sent_half = call(
        functools.partial(closing_kernel, block, 1.0 / (samples * 2 * tokens)),
        (struct((2, width // 2), F32), struct((2, width // 2), F32)),
        (gathered, own_columns, embed),
    )
    total = kept_half + other_core(sent_half)
    total = (total + other_half(total)).astype(BF16)
    spread = between_chips(jnp.broadcast_to(total[None], (chips,) + total.shape))
    total = jnp.sum(spread.astype(F32), axis=0)
    near_total = other_core(total)
    mod_grads = jnp.where(
        second_core,
        jnp.concatenate([near_total, total], axis=1),
        jnp.concatenate([total, near_total], axis=1),
    )
    return (crossed[None, None], mod_grads[None])


def solution(mesh):
    return jax.shard_map(
        per_device,
        mesh=mesh,
        in_specs=(
            P("role", "fsdp", "seq", None),
            P("role", "fsdp", "seq", None),
            P("role", "fsdp"),
            P("role", "fsdp", "seq", None),
            P("role", "fsdp"),
            P("role", "fsdp", "seq", None),
            P("role", None, None),
            P("role", "fsdp", "seq"),
            P("role", "seq", None),
            P("role", None, None, None),
        ),
        out_specs=(P("role", "fsdp", "seq", None), P("role", None, None)),
        check_vma=False,
    )
```

```python
import functools

import jax
import jax.numpy as jnp
from jax import lax
from jax.experimental import pallas as pl
from jax.experimental.pallas import tpu as pltpu
from jax.sharding import PartitionSpec as P

HEAD_DIM = 128
CHANNELS = 64
EPSILON = 1e-06
F32 = jnp.float32
BF16 = jnp.bfloat16
NT = (((1,), (1,)), ((), ()))
NN = (((1,), (0,)), ((), ()))
TN = (((0,), (0,)), ((), ()))


def dot(a, b, dims=NN):
    return lax.dot_general(a, b, dims, preferred_element_type=F32)


def round_up(value, step):
    return (value + step - 1) // step * step


def rounded(value):
    return value.astype(BF16).astype(F32)


def three_parts(value):
    high = rounded(value)
    middle = rounded(value - high)
    return high, middle, rounded(value - high - middle)


def lane_index(shape):
    return lax.broadcasted_iota(jnp.int32, shape, len(shape) - 1)


def row_index(shape):
    return lax.broadcasted_iota(jnp.int32, shape, len(shape) - 2)


def on_second_core():
    return lax.rem(lax.axis_index("fsdp"), 2) == 1


def on_critic():
    return lax.axis_index("role") == 1


def pack_kernel(noise_levels, replay_levels, base, noise, replay, cotangent, embed, modulation, pack, stack):
    critic = on_critic()
    modulation_a = modulation[0]
    modulation_b = jnp.where(critic, modulation[1], modulation_a)
    embed_f = embed[...].astype(F32)
    scaled_b = (embed_f * modulation_b[0:1, :]).astype(BF16)
    stack[0:64, :] = embed[...]
    stack[64:128, :] = (embed_f * modulation_a[0:1, :]).astype(BF16)
    stack[128:192, :] = scaled_b
    stack[192:256, :] = scaled_b
    shifts = []
    for pair in (modulation_a, modulation_b):
        shift = pair[1:2, :]
        high = rounded(shift)
        shifts += [high, shift - high]
    shifts.append(jnp.zeros((12, embed.shape[1]), F32))
    stack[256:272, :] = jnp.concatenate(shifts, axis=0).astype(BF16)
    level = noise_levels[0, 0]
    level_two = jnp.where(critic, level, replay_levels[0, 0])
    base_f = base[...].astype(F32)
    noise_f = noise[...].astype(F32)
    input_a = rounded((1.0 - level) * base_f + level * noise_f)
    input_b = jnp.where(critic, input_a, replay[...].astype(F32))
    known = jnp.where(critic, noise_f - base_f, cotangent[...].astype(F32))
    known_high = rounded(known)
    tokens = input_a.shape[0]
    rows = jnp.concatenate([input_a, input_b], axis=0).astype(BF16)
    total = jnp.zeros((2 * tokens, 1), F32)
    width = embed.shape[1]
    for start in range(0, width, 512):
        embedded = dot(rows, embed[:, start : start + 512])
        total = total + jnp.sum(embedded * embedded, axis=-1, keepdims=True)
    scale = lax.rsqrt(total / width + EPSILON)
    lane = lane_index((tokens, 128))
    tail = jnp.zeros((tokens, 128), F32)
    ones = jnp.ones((tokens, 1), F32)
    for which, column in enumerate((scale[:tokens], scale[tokens:], ones * level, ones * level_two)):
        for part, value in enumerate(three_parts(column)):
            tail = jnp.where(lane == which * 3 + part, value, tail)
    pack[:, 0:64] = input_a.astype(BF16)
    pack[:, 64:128] = input_b.astype(BF16)
    pack[:, 128:192] = known_high.astype(BF16)
    pack[:, 192:256] = (known - known_high).astype(BF16)
    pack[:, 256:384] = tail.astype(BF16)


def cut_kernel(weight, keep):
    columns = keep.shape[1]
    keep[...] = jnp.where(on_second_core(), weight[:, columns:].astype(F32), weight[:, 0:columns].astype(F32)).astype(BF16)


def weight_kernel(chips, keep, received, out, turned):
    second = on_second_core()
    rows, columns = keep.shape
    own = keep[...].astype(F32)
    other = jnp.where(second, received[:, columns:].astype(F32), received[:, 0:columns].astype(F32))
    both = [jnp.where(second, other, own), jnp.where(second, own, other)]
    padded = out.shape[2]
    if padded > 2 * rows:
        both.append(jnp.zeros((padded - 2 * rows, columns), F32))
    turned[0:columns, :] = jnp.concatenate(both, axis=0).T
    turned[columns:, :] = jnp.zeros((turned.shape[0] - columns, padded), F32)
    block = columns // chips
    height = out.shape[1]
    row = row_index((height, padded))
    for chip in range(chips):
        piece = turned[chip * block : chip * block + height, :]
        out[chip] = jnp.where(row < block, piece, 0.0).astype(BF16)


def product_kernel(block, taken, stack, out, halves_out, columns_out):
    chips, height, padded = taken.shape
    half = block // 2
    stride = halves_out.shape[0] // 2
    width = stack.shape[1]
    depth = width // chips
    row_half = row_index((stride, 1))
    group = 1 if depth % 128 == 0 else 128 // (depth & -depth)
    for start in range(0, chips, group):
        pieces = [taken[chip].astype(F32)[:, 0:depth] for chip in range(start, start + group)]
        joined = jnp.concatenate(pieces, axis=1) if group > 1 else pieces[0]
        span = slice(start * depth, (start + group) * depth)
        columns_out[:, span] = joined.astype(BF16)
        longer = jnp.concatenate([joined, jnp.zeros((stride, joined.shape[1]), F32)], axis=0)
        low = jnp.where(row_half < half, longer[0:stride], 0.0)
        high = jnp.where(row_half < half, longer[half : half + stride], 0.0)
        halves_out[:, span] = jnp.concatenate([low, high], axis=0).astype(BF16)
    weight = columns_out[...]
    products = dot(weight, stack[0:256, :], NT)
    first, second = products[:, 0:128], products[:, 128:256]
    offsets = dot(stack[256:272, :], weight, NT)
    lines = []
    gap = jnp.zeros((1, CHANNELS - block), F32)
    for offset in (offsets[0:1, 0:block] + offsets[1:2, 0:block], offsets[2:3, 0:block] + offsets[3:4, 0:block]):
        high = rounded(offset)
        lines.append(jnp.concatenate([high, gap, offset - high, gap], axis=1))
    low_lanes = lane_index((half, 128)) < CHANNELS
    folded = jnp.where(low_lanes, second[0:half], second[half:block])
    spare = out.shape[1] - block - half - 2
    parts = [first[0:block], folded] + lines
    if spare:
        parts.append(jnp.zeros((spare, 128), F32))
    whole = jnp.concatenate(parts, axis=0).astype(BF16)
    for chip in range(chips):
        out[chip] = whole


def token_rows(packs, sample, start, stop):
    return jnp.concatenate([pack[sample, :, start:stop] for pack in packs], axis=0)


def tail_column(packs, sample, which):
    tail = token_rows(packs, sample, 256, 384).astype(F32)
    at = 3 * which
    return tail[:, at : at + 1] + tail[:, at + 1 : at + 2] + tail[:, at + 2 : at + 3]


def forward(which, packs, matrices, offsets, output_turned, keep, keep_turned, probs_out, velocity):
    heads = output_turned.shape[1] // HEAD_DIM
    low_lanes = lane_index((1, 128)) < CHANNELS
    rows, scales, levels, turned_scales = [], [], [], []
    for sample in range(2):
        inputs = token_rows(packs, sample, 0, 128).astype(F32)
        turned = pltpu.roll(inputs, CHANNELS, 1)
        level = tail_column(packs, sample, 2 + which)
        plain, scaled = (turned, inputs) if which else (inputs, turned)
        rows.append(jnp.where(low_lanes, plain, scaled * level))
        scale = tail_column(packs, sample, which)
        scales.append(scale)
        levels.append(level[0:1])
        turned_scales.append(jnp.broadcast_to(scale, (scale.shape[0], 128)).T[0:1])
    tokens = rows[0].shape[0]
    inputs = jnp.concatenate(rows, axis=0)
    turned = inputs.T.astype(BF16)
    inputs = inputs.astype(BF16)
    offset = offsets[which : which + 1, :]
    columns = offset.shape[1]
    offset_turned = jnp.broadcast_to(offset, (128, columns)).T[:, 0:1]
    units = []
    for head in range(heads):
        at = head * 3 * HEAD_DIM
        span = slice(at, at + 3 * HEAD_DIM)
        matrix = matrices[span, :]
        if keep is None:
            product = dot(inputs, matrix[HEAD_DIM : 2 * HEAD_DIM], NT)
        else:
            product = dot(inputs, matrix, NT)
        product_turned = dot(matrix, turned)
        for sample in range(2):
            own = slice(sample * tokens, (sample + 1) * tokens)
            line = offset[:, span] if keep is not None else offset[:, at + HEAD_DIM : at + 2 * HEAD_DIM]
            qkv = (product[own] * scales[sample] + line * levels[sample]).astype(BF16)
            flipped = product_turned[:, own] * turned_scales[sample] + offset_turned[span] * levels[sample]
            flipped = flipped.astype(BF16)
            key = qkv
            if keep is not None:
                keep[sample, :, span] = qkv
                keep_turned[2 * head + sample] = flipped[HEAD_DIM : 2 * HEAD_DIM]
                key = qkv[:, HEAD_DIM : 2 * HEAD_DIM]
            units.append((key, flipped[0:HEAD_DIM], flipped[2 * HEAD_DIM :]))
    totals = [None, None]
    scores = [dot(key, query) * (HEAD_DIM**-0.5) for key, query, _ in units]
    for unit, score in enumerate(scores):
        powers = jnp.exp(score - jnp.max(score, axis=0, keepdims=True))
        probs = powers * (1.0 / jnp.sum(powers, axis=0, keepdims=True))
        if probs_out is not None:
            probs_out[unit] = probs
        mixed = dot(units[unit][2], probs.astype(BF16)).astype(BF16)
        head = unit // 2
        term = dot(output_turned[:, head * HEAD_DIM : (head + 1) * HEAD_DIM], mixed)
        before = totals[unit % 2]
        totals[unit % 2] = term if before is None else before + term
    velocity[...] = jnp.concatenate(totals, axis=0).T


def second_pass_kernel(
    block,
    taken,
    here,
    there,
    output_turned,
    matrices,
    offsets,
    keep,
    keep_turned,
    probs,
    velocity,
    crossing,
    stacked,
    stacked_two,
):
    chips = taken.shape[0]
    half = block // 2
    low_lanes = lane_index((half, 128)) < CHANNELS
    lines = [[], []]
    for chip in range(chips):
        piece = taken[chip].astype(F32)
        at = chip * block
        stacked[at : at + block, :] = piece[0:block]
        folded = piece[block : block + half]
        turned = pltpu.roll(folded, CHANNELS, 1)
        stacked_two[at : at + half, :] = jnp.where(low_lanes, piece[0:half], turned)
        stacked_two[at + half : at + block, :] = jnp.where(low_lanes, piece[half:block], folded)
        for which in range(2):
            line = piece[block + half + which : block + half + which + 1]
            lines[which].append((line + pltpu.roll(line, CHANNELS, 1))[:, 0:block])
    matrices[...] = stacked[...].astype(BF16)
    joined = [jnp.concatenate(line, axis=1) for line in lines]
    offsets[...] = jnp.concatenate(joined + [jnp.zeros((6, offsets.shape[1]), F32)], axis=0)
    both = stacked_two[...].astype(BF16)
    forward(1, (here, there), both, offsets, output_turned, keep, keep_turned, probs, velocity)
    crossing[...] = pltpu.roll(velocity[...], CHANNELS, 1)


def first_pass_kernel(matrices, offsets, here, there, output_turned, velocity):
    forward(0, (here, there), matrices, offsets, output_turned, None, None, None, velocity)


def swap_tokens(value):
    half = value.shape[0] // 2
    return jnp.concatenate([value[half:], value[:half]], axis=0)


def backward_kernel(
    block, kept, keys_turned, probs_turned, here, there, vel_here, vel_there, output_turned, out, gathered, summed
):
    critic = on_critic()
    packs = (here, there)
    heads = output_turned.shape[1] // HEAD_DIM
    velocity = vel_here[...] + swap_tokens(vel_there[...])
    lane = lane_index((1, 128))
    known = []
    for sample in range(2):
        part = token_rows(packs, sample, 128, 256).astype(F32)
        known.append(part[:, 0:CHANNELS] + part[:, CHANNELS:])
    known = jnp.concatenate(known, axis=1)
    grad_velocity = jnp.where(critic, velocity - known, known)
    grads_turned = grad_velocity.T.astype(BF16)
    grads = grad_velocity.astype(BF16)
    inputs, rows, levels = [], [], []
    for sample in range(2):
        packed = token_rows(packs, sample, 0, 128).astype(F32)
        packed = jnp.where(lane < CHANNELS, pltpu.roll(packed, CHANNELS, 1), packed)
        level = tail_column(packs, sample, 3)
        levels.append(level[0:1])
        scaled = packed * (tail_column(packs, sample, 1) * level)
        inputs.append(scaled.astype(BF16))
        rows.append(scaled.T.astype(BF16))
    grad_mixed, grad_probs = [], []
    for unit in range(2 * heads):
        head, sample = unit // 2, unit % 2
        weight = output_turned[:, head * HEAD_DIM : (head + 1) * HEAD_DIM]
        lanes = slice(sample * CHANNELS, (sample + 1) * CHANNELS)
        grad_mixed.append(dot(grads[:, lanes], weight).astype(BF16))
        turned = dot(weight, grads_turned[lanes], TN).astype(BF16)
        value = kept[sample, :, head * 3 * HEAD_DIM + 2 * HEAD_DIM : (head + 1) * 3 * HEAD_DIM]
        grad_probs.append(dot(value, turned))
    for head in range(heads):
        at = head * 3 * HEAD_DIM
        query_total, rest_total = None, None
        ends = []
        for sample in range(2):
            unit = 2 * head + sample
            probs = probs_turned[unit]
            grad = grad_probs[unit]
            inner = jnp.sum(grad * probs, axis=0, keepdims=True)
            grad_scores = (probs * (grad - inner) * (HEAD_DIM**-0.5)).astype(BF16)
            grad_value = dot(probs.astype(BF16), grad_mixed[unit])
            grad_key = dot(grad_scores, kept[sample, :, at : at + HEAD_DIM])
            grad_query = dot(keys_turned[unit], grad_scores).astype(BF16)
            rest = jnp.concatenate([grad_key, grad_value], axis=1).astype(BF16)
            query_term = dot(grad_query, inputs[sample])
            rest_term = dot(rows[sample], rest)
            query_total = query_term if query_total is None else query_total + query_term
            rest_total = rest_term if rest_total is None else rest_total + rest_term
            turned_sum = jnp.sum(grad_query.astype(F32), axis=1, keepdims=True)
            turned_sum = jnp.broadcast_to(turned_sum, (HEAD_DIM, 128)).T[0:1]
            rest_sum = jnp.sum(rest.astype(F32), axis=0, keepdims=True)
            ends.append(jnp.concatenate([turned_sum, rest_sum], axis=1) * levels[sample])
        gathered[at : at + HEAD_DIM, :] = query_total
        gathered[at + HEAD_DIM : at + 3 * HEAD_DIM, :] = rest_total.T
        summed[:, at : at + 3 * HEAD_DIM] = ends[0] + ends[1]
    columns = heads * 3 * HEAD_DIM
    gathered[columns:, :] = jnp.zeros((gathered.shape[0] - columns, 128), F32)
    chips, height = out.shape[0], out.shape[1]
    half = block // 2
    row = row_index((height, 128))
    low_lanes = lane_index((height, 128)) < CHANNELS
    pad = jnp.zeros((1, 128 - block), F32) if block < 128 else None
    for chip in range(chips):
        at = chip * block
        piece = jnp.where(low_lanes, gathered[at : at + height, :], gathered[at + half : at + half + height, :])
        line = summed[:, at : at + block]
        high = rounded(line)
        pair = [high, line - high]
        if pad is not None:
            pair = [jnp.concatenate([part, pad], axis=1) for part in pair]
        piece = jnp.where(row < half, piece, jnp.where(row == half, pair[0], jnp.where(row == half + 1, pair[1], 0.0)))
        out[chip] = piece.astype(BF16)


def closing_kernel(block, factor, taken, weight, embed, kept, sent):
    second = on_second_core()
    total = taken[0].astype(F32)
    for chip in range(1, taken.shape[0]):
        total = total + taken[chip].astype(F32)
    half = block // 2
    height = total.shape[0]
    row = row_index((height, 128))
    ends = total[half : half + 1] + total[half + 1 : half + 2]
    turned = jnp.where(row < half, total, 0.0).T
    lane = lane_index((1, 128))
    ends_low = jnp.where(lane < half, ends, 0.0)[:, 0:height]
    ends_high = jnp.where(lane < half, pltpu.roll(ends, 128 - half, 1), 0.0)[:, 0:height]
    lower = jnp.concatenate([turned[0:CHANNELS], ends_low, jnp.zeros((7, height), F32)], axis=0)
    upper = jnp.concatenate([turned[CHANNELS:], ends_high, jnp.zeros((7, height), F32)], axis=0)
    joined = jnp.concatenate([lower, upper], axis=1)
    high = joined.astype(BF16)
    low = (joined - high.astype(F32)).astype(BF16)
    middle = embed.shape[1] // 2
    step = middle // 3
    parts = []
    for start in range(0, 2 * middle, step):
        columns = weight[:, start : start + step]
        product = dot(high, columns) + dot(low, columns)
        scale = jnp.sum(product[:CHANNELS] * embed[:, start : start + step].astype(F32), axis=0, keepdims=True)
        parts.append(jnp.concatenate([scale, product[CHANNELS : CHANNELS + 1]], axis=0) * factor)
    left = jnp.concatenate(parts[:3], axis=1)
    right = jnp.concatenate(parts[3:], axis=1)
    kept[...] = jnp.where(second, right, left)
    sent[...] = jnp.where(second, left, right)


def call(kernel, out_shapes, inputs, scalars=0, scratch=(), flops=0, moved=0):
    specs = [pl.BlockSpec(memory_space=pltpu.SMEM)] * scalars
    specs += [pl.BlockSpec(memory_space=pltpu.VMEM)] * (len(inputs) - scalars)
    return pl.pallas_call(
        kernel,
        out_shape=out_shapes,
        in_specs=specs,
        out_specs=jax.tree.map(lambda _: pl.BlockSpec(memory_space=pltpu.VMEM), out_shapes),
        scratch_shapes=list(scratch),
        compiler_params=pltpu.CompilerParams(vmem_limit_bytes=28 * 2**20),
        cost_estimate=pl.CostEstimate(flops=flops, bytes_accessed=moved, transcendentals=0),
    )(*inputs)


def struct(shape, dtype):
    return jax.ShapeDtypeStruct(shape, dtype)


def other_core(value):
    return lax.ppermute(value, "fsdp", [(i, i ^ 1) for i in range(lax.axis_size("fsdp"))])


def other_half(value):
    return lax.ppermute(value, "seq", [(0, 1), (1, 0)])


def between_chips(value):
    count = lax.axis_size("fsdp")
    groups = [list(range(core, count, 2)) for core in range(2)]
    return lax.all_to_all(value, "fsdp", 0, 0, tiled=True, axis_index_groups=groups)


def per_device(
    base_latents,
    noise_latents,
    noise_levels,
    replay_latents,
    replay_levels,
    cotangent,
    embed_weight,
    qkv_weight,
    output_weight,
    modulation,
):
    is_critic = on_critic()
    second_core = on_second_core()
    devices = lax.axis_size("fsdp")
    chips = devices // 2
    embed = embed_weight[0]
    weight = qkv_weight[0]
    width = embed.shape[1]
    columns = weight.shape[1] // 2
    block = columns // chips
    height = round_up(block, 8)
    packed = round_up(block + block // 2 + 2, 8)
    folded = round_up(block // 2 + 2, 8)
    padded = round_up(2 * weight.shape[0], 128)
    tokens = base_latents.shape[2]
    heads = columns // (3 * HEAD_DIM)
    out_columns = output_weight.shape[1] // 2
    output_turned = output_weight[0].T
    output_turned = jnp.where(second_core, output_turned[:, out_columns:], output_turned[:, :out_columns])

    received = other_core(weight)
    keep = call(cut_kernel, struct((weight.shape[0], columns), BF16), (weight,))
    turned = call(
        functools.partial(weight_kernel, chips),
        struct((chips, height, padded), BF16),
        (keep, received),
        scratch=[pltpu.VMEM((columns + height - block, padded), F32)],
    )
    turned, first_levels = lax.optimization_barrier((turned, noise_levels))
    taken = between_chips(turned)

    own, stack = call(
        pack_kernel,
        (struct((tokens, 384), BF16), struct((272, width), BF16)),
        (
            first_levels,
            replay_levels,
            base_latents[0, 0],
            noise_latents[0, 0],
            replay_latents[0, 0],
            cotangent[0, 0],
            embed,
            modulation[0],
        ),
        scalars=2,
    )
    here = jnp.stack([own, other_core(own)])
    taken, here = lax.optimization_barrier((taken, here))
    there = other_half(here)

    matrices, own_columns = call(
        functools.partial(product_kernel, block),
        (struct((chips, packed, 128), BF16), struct((2 * folded, width), BF16)),
        (taken, stack),
        scratch=[pltpu.VMEM((height, width), BF16)],
    )
    whole, offsets, kept, keys_turned, probs, vel_b, vel_crossing = call(
        functools.partial(second_pass_kernel, block),
        (
            struct((columns, 2 * CHANNELS), BF16),
            struct((8, columns), F32),
            struct((2, 2 * tokens, columns), BF16),
            struct((2 * heads, HEAD_DIM, 2 * tokens), BF16),
            struct((2 * heads, 2 * tokens, 2 * tokens), F32),
            struct((2 * tokens, 2 * CHANNELS), F32),
            struct((2 * tokens, 2 * CHANNELS), F32),
        ),
        (between_chips(matrices), here, there, output_turned),
        scratch=[pltpu.VMEM((columns, 2 * CHANNELS), F32), pltpu.VMEM((columns, 2 * CHANNELS), F32)],
    )
    vel_here = vel_b + other_core(vel_crossing)
    vel_there = other_half(vel_here)
    vel_a = call(
        first_pass_kernel,
        struct((2 * tokens, 2 * CHANNELS), F32),
        (whole, offsets, here, there, output_turned),
        flops=4 * 10**9,
    )
    vel_there, vel_a = lax.optimization_barrier((vel_there, vel_a))
    products = call(
        functools.partial(backward_kernel, block),
        struct((chips, folded, 128), BF16),
        (kept, keys_turned, probs, here, there, vel_here, vel_there, output_turned),
        scratch=[pltpu.VMEM((columns + 2 * folded, 128), F32), pltpu.VMEM((1, columns), F32)],
    )
    gathered = between_chips(products)

    own_a = vel_a[:, :CHANNELS] + other_core(vel_a[:, CHANNELS:])
    own_a = own_a[:tokens] + other_half(own_a[tokens:])
    own_b = vel_here[:tokens, :CHANNELS] + vel_there[tokens:, :CHANNELS]
    sample = own[:, :CHANNELS].astype(F32) - noise_levels[0, 0] * own_a
    payload = jnp.where(is_critic, own_b - own_a, sample).T.astype(BF16)
    gathered, payload = lax.optimization_barrier((gathered, payload))
    crossed = lax.ppermute(payload, "role", [(0, 1), (1, 0)]).T

    samples = devices * base_latents.shape[1]
    kept_half, sent_half = call(
        functools.partial(closing_kernel, block, 1.0 / (samples * 2 * tokens)),
        (struct((2, width // 2), F32), struct((2, width // 2), F32)),
        (gathered, own_columns, embed),
    )
    total = kept_half + other_core(sent_half)
    total = (total + other_half(total)).astype(BF16)
    spread = between_chips(jnp.broadcast_to(total[None], (chips,) + total.shape))
    total = jnp.sum(spread.astype(F32), axis=0)
    near_total = other_core(total)
    mod_grads = jnp.where(
        second_core,
        jnp.concatenate([near_total, total], axis=1),
        jnp.concatenate([total, near_total], axis=1),
    )
    return (crossed[None, None], mod_grads[None])


def solution(mesh):
    return jax.shard_map(
        per_device,
        mesh=mesh,
        in_specs=(
            P("role", "fsdp", "seq", None),
            P("role", "fsdp", "seq", None),
            P("role", "fsdp"),
            P("role", "fsdp", "seq", None),
            P("role", "fsdp"),
            P("role", "fsdp", "seq", None),
            P("role", None, None),
            P("role", "fsdp", "seq"),
            P("role", "seq", None),
            P("role", None, None, None),
        ),
        out_specs=(P("role", "fsdp", "seq", None), P("role", None, None)),
        check_vma=False,
    )
```

```python
import functools

import jax
import jax.numpy as jnp
from jax import lax
from jax.experimental import pallas as pl
from jax.experimental.pallas import tpu as pltpu
from jax.sharding import PartitionSpec as P

HEAD_DIM = 128
CHANNELS = 64
EPSILON = 1e-06
F32 = jnp.float32
BF16 = jnp.bfloat16
NT = (((1,), (1,)), ((), ()))
NN = (((1,), (0,)), ((), ()))
TN = (((0,), (0,)), ((), ()))


def dot(a, b, dims=NN):
    return lax.dot_general(a, b, dims, preferred_element_type=F32)


def round_up(value, step):
    return (value + step - 1) // step * step


def rounded(value):
    return value.astype(BF16).astype(F32)


def three_parts(value):
    high = rounded(value)
    middle = rounded(value - high)
    return high, middle, rounded(value - high - middle)


def lane_index(shape):
    return lax.broadcasted_iota(jnp.int32, shape, len(shape) - 1)


def row_index(shape):
    return lax.broadcasted_iota(jnp.int32, shape, len(shape) - 2)


def on_second_core():
    return lax.rem(lax.axis_index("fsdp"), 2) == 1


def on_critic():
    return lax.axis_index("role") == 1


def pack_kernel(noise_levels, replay_levels, base, noise, replay, cotangent, embed, modulation, after, pack, stack):
    critic = on_critic()
    modulation_a = modulation[0]
    modulation_b = jnp.where(critic, modulation[1], modulation_a)
    embed_f = embed[...].astype(F32)
    scaled_b = (embed_f * modulation_b[0:1, :]).astype(BF16)
    stack[0:64, :] = embed[...]
    stack[64:128, :] = (embed_f * modulation_a[0:1, :]).astype(BF16)
    stack[128:192, :] = scaled_b
    stack[192:256, :] = scaled_b
    shifts = []
    for pair in (modulation_a, modulation_b):
        shift = pair[1:2, :]
        high = rounded(shift)
        shifts += [high, shift - high]
    shifts.append(jnp.zeros((12, embed.shape[1]), F32))
    stack[256:272, :] = jnp.concatenate(shifts, axis=0).astype(BF16)
    level = noise_levels[0, 0]
    level_two = jnp.where(critic, level, replay_levels[0, 0])
    base_f = base[...].astype(F32)
    noise_f = noise[...].astype(F32)
    input_a = rounded((1.0 - level) * base_f + level * noise_f)
    input_b = jnp.where(critic, input_a, replay[...].astype(F32))
    known = jnp.where(critic, noise_f - base_f, cotangent[...].astype(F32))
    known_high = rounded(known)
    tokens = input_a.shape[0]
    rows = jnp.concatenate([input_a, input_b], axis=0).astype(BF16)
    total = jnp.zeros((2 * tokens, 1), F32)
    width = embed.shape[1]
    for start in range(0, width, 512):
        embedded = dot(rows, embed[:, start : start + 512])
        total = total + jnp.sum(embedded * embedded, axis=-1, keepdims=True)
    scale = lax.rsqrt(total / width + EPSILON)
    lane = lane_index((tokens, 128))
    tail = jnp.zeros((tokens, 128), F32)
    ones = jnp.ones((tokens, 1), F32)
    for which, column in enumerate((scale[:tokens], scale[tokens:], ones * level, ones * level_two)):
        for part, value in enumerate(three_parts(column)):
            tail = jnp.where(lane == which * 3 + part, value, tail)
    pack[:, 0:64] = input_a.astype(BF16)
    pack[:, 64:128] = input_b.astype(BF16)
    pack[:, 128:192] = known_high.astype(BF16)
    pack[:, 192:256] = (known - known_high).astype(BF16)
    pack[:, 256:384] = tail.astype(BF16)


def turn_rows(rows, padded, second):
    count, columns = rows.shape
    empty = jnp.zeros((count, columns), F32)
    parts = [jnp.where(second, empty, rows), jnp.where(second, rows, empty)]
    if padded > 2 * count:
        parts.append(jnp.zeros((padded - 2 * count, columns), F32))
    return jnp.concatenate(parts, axis=0).T


def half_columns(weight, second):
    columns = weight.shape[1] // 2
    start = pl.multiple_of(jnp.where(second, columns, 0), 128)
    return weight[:, pl.ds(start, columns)].astype(F32)


def own_rows_kernel(weight, out):
    second = on_second_core()
    out[...] = turn_rows(half_columns(weight, second), out.shape[1], second)


def weight_kernel(chips, own, received, out, turned, blocks, copied):
    second = on_second_core()
    columns, padded = own.shape
    turned[0:columns, :] = own[...] + turn_rows(half_columns(received, second), padded, jnp.logical_not(second))
    turned[columns:, :] = jnp.zeros((turned.shape[0] - columns, padded), F32)
    block = columns // chips
    height = out.shape[1]
    row = row_index((height, padded))
    group = 8
    copies = []
    for chip in range(chips):
        piece = turned[chip * block : chip * block + height, :]
        blocks[chip] = jnp.where(row < block, piece, 0.0).astype(BF16)
        if chip % group == group - 1:
            span = pl.ds(chip + 1 - group, group)
            copies.append(pltpu.make_async_copy(blocks.at[span], out.at[span], copied.at[len(copies)]))
            copies[-1].start()
    for copy in copies:
        copy.wait()


def product_kernel(block, taken, stack, after, out, halves_out, columns_out):
    chips, height, padded = taken.shape
    half = block // 2
    stride = halves_out.shape[0] // 2
    width = stack.shape[1]
    depth = width // chips
    row_half = row_index((stride, 1))
    group = 1 if depth % 128 == 0 else 128 // (depth & -depth)
    for start in range(0, chips, group):
        pieces = [taken[chip].astype(F32)[:, 0:depth] for chip in range(start, start + group)]
        joined = jnp.concatenate(pieces, axis=1) if group > 1 else pieces[0]
        span = slice(start * depth, (start + group) * depth)
        columns_out[:, span] = joined.astype(BF16)
        longer = jnp.concatenate([joined, jnp.zeros((stride, joined.shape[1]), F32)], axis=0)
        low = jnp.where(row_half < half, longer[0:stride], 0.0)
        high = jnp.where(row_half < half, longer[half : half + stride], 0.0)
        halves_out[:, span] = jnp.concatenate([low, high], axis=0).astype(BF16)
    weight = columns_out[...]
    products = dot(weight, stack[0:256, :], NT)
    first, second = products[:, 0:128], products[:, 128:256]
    offsets = dot(stack[256:272, :], weight, NT)
    lines = []
    gap = jnp.zeros((1, CHANNELS - block), F32)
    for offset in (offsets[0:1, 0:block] + offsets[1:2, 0:block], offsets[2:3, 0:block] + offsets[3:4, 0:block]):
        high = rounded(offset)
        lines.append(jnp.concatenate([high, gap, offset - high, gap], axis=1))
    low_lanes = lane_index((half, 128)) < CHANNELS
    folded = jnp.where(low_lanes, second[0:half], second[half:block])
    spare = out.shape[1] - block - half - 2
    parts = [first[0:block], folded] + lines
    if spare:
        parts.append(jnp.zeros((spare, 128), F32))
    whole = jnp.concatenate(parts, axis=0).astype(BF16)
    for chip in range(chips):
        out[chip] = whole


def token_rows(packs, sample, start, stop):
    return jnp.concatenate([pack[sample, :, start:stop] for pack in packs], axis=0)


def tail_column(packs, sample, which):
    tail = token_rows(packs, sample, 256, 384).astype(F32)
    at = 3 * which
    return tail[:, at : at + 1] + tail[:, at + 1 : at + 2] + tail[:, at + 2 : at + 3]


def forward(which, packs, matrices, offsets, output_turned, keep, keep_turned, probs_out, velocity):
    heads = output_turned.shape[1] // HEAD_DIM
    low_lanes = lane_index((1, 128)) < CHANNELS
    rows, scales, levels, turned_scales = [], [], [], []
    for sample in range(2):
        inputs = token_rows(packs, sample, 0, 128).astype(F32)
        turned = pltpu.roll(inputs, CHANNELS, 1)
        level = tail_column(packs, sample, 2 + which)
        plain, scaled = (turned, inputs) if which else (inputs, turned)
        rows.append(jnp.where(low_lanes, plain, scaled * level))
        scale = tail_column(packs, sample, which)
        scales.append(scale)
        levels.append(level[0:1])
        turned_scales.append(jnp.broadcast_to(scale, (scale.shape[0], 128)).T[0:1])
    tokens = rows[0].shape[0]
    inputs = jnp.concatenate(rows, axis=0)
    turned = inputs.T.astype(BF16)
    inputs = inputs.astype(BF16)
    offset = offsets[which : which + 1, :]
    columns = offset.shape[1]
    offset_turned = jnp.broadcast_to(offset, (128, columns)).T[:, 0:1]
    units = []
    for head in range(heads):
        at = head * 3 * HEAD_DIM
        span = slice(at, at + 3 * HEAD_DIM)
        matrix = matrices[span, :]
        if keep is None:
            product = dot(inputs, matrix[HEAD_DIM : 2 * HEAD_DIM], NT)
        else:
            product = dot(inputs, matrix, NT)
        product_turned = dot(matrix, turned)
        for sample in range(2):
            own = slice(sample * tokens, (sample + 1) * tokens)
            line = offset[:, span] if keep is not None else offset[:, at + HEAD_DIM : at + 2 * HEAD_DIM]
            qkv = (product[own] * scales[sample] + line * levels[sample]).astype(BF16)
            flipped = product_turned[:, own] * turned_scales[sample] + offset_turned[span] * levels[sample]
            flipped = flipped.astype(BF16)
            key = qkv
            if keep is not None:
                keep[sample, :, span] = qkv
                keep_turned[2 * head + sample] = flipped[HEAD_DIM : 2 * HEAD_DIM]
                key = qkv[:, HEAD_DIM : 2 * HEAD_DIM]
            units.append((key, flipped[0:HEAD_DIM], flipped[2 * HEAD_DIM :]))
    totals = [None, None]
    scores = [dot(key, query) * (HEAD_DIM**-0.5) for key, query, _ in units]
    for unit, score in enumerate(scores):
        powers = jnp.exp(score - jnp.max(score, axis=0, keepdims=True))
        probs = powers * (1.0 / jnp.sum(powers, axis=0, keepdims=True))
        if probs_out is not None:
            probs_out[unit] = probs
        mixed = dot(units[unit][2], probs.astype(BF16)).astype(BF16)
        head = unit // 2
        term = dot(output_turned[:, head * HEAD_DIM : (head + 1) * HEAD_DIM], mixed)
        before = totals[unit % 2]
        totals[unit % 2] = term if before is None else before + term
    velocity[...] = jnp.concatenate(totals, axis=0).T


def second_pass_kernel(
    block,
    taken,
    here,
    there,
    output_turned,
    matrices,
    offsets,
    keep,
    keep_turned,
    probs,
    velocity,
    crossing,
    stacked,
    stacked_two,
):
    chips = taken.shape[0]
    half = block // 2
    low_lanes = lane_index((half, 128)) < CHANNELS
    lines = [[], []]
    for chip in range(chips):
        piece = taken[chip].astype(F32)
        at = chip * block
        stacked[at : at + block, :] = piece[0:block]
        folded = piece[block : block + half]
        turned = pltpu.roll(folded, CHANNELS, 1)
        stacked_two[at : at + half, :] = jnp.where(low_lanes, piece[0:half], turned)
        stacked_two[at + half : at + block, :] = jnp.where(low_lanes, piece[half:block], folded)
        for which in range(2):
            line = piece[block + half + which : block + half + which + 1]
            lines[which].append((line + pltpu.roll(line, CHANNELS, 1))[:, 0:block])
    matrices[...] = stacked[...].astype(BF16)
    joined = [jnp.concatenate(line, axis=1) for line in lines]
    offsets[...] = jnp.concatenate(joined + [jnp.zeros((6, offsets.shape[1]), F32)], axis=0)
    both = stacked_two[...].astype(BF16)
    forward(1, (here, there), both, offsets, output_turned, keep, keep_turned, probs, velocity)
    crossing[...] = pltpu.roll(velocity[...], CHANNELS, 1)


def first_pass_kernel(matrices, offsets, here, there, output_turned, after, velocity, crossing):
    forward(0, (here, there), matrices, offsets, output_turned, None, None, None, velocity)
    crossing[...] = pltpu.roll(velocity[...], CHANNELS, 1)


def swap_tokens(value):
    half = value.shape[0] // 2
    return jnp.concatenate([value[half:], value[:half]], axis=0)


def backward_kernel(
    block,
    kept,
    keys_turned,
    probs_turned,
    here,
    there,
    vel_here,
    vel_there,
    output_turned,
    after,
    out,
    gathered,
    summed,
    blocks,
    copied,
):
    critic = on_critic()
    packs = (here, there)
    heads = output_turned.shape[1] // HEAD_DIM
    velocity = vel_here[...] + swap_tokens(vel_there[...])
    lane = lane_index((1, 128))
    known = []
    for sample in range(2):
        part = token_rows(packs, sample, 128, 256).astype(F32)
        known.append(part[:, 0:CHANNELS] + part[:, CHANNELS:])
    known = jnp.concatenate(known, axis=1)
    grad_velocity = jnp.where(critic, velocity - known, known)
    grads_turned = grad_velocity.T.astype(BF16)
    grads = grad_velocity.astype(BF16)
    inputs, rows, levels = [], [], []
    for sample in range(2):
        packed = token_rows(packs, sample, 0, 128).astype(F32)
        packed = jnp.where(lane < CHANNELS, pltpu.roll(packed, CHANNELS, 1), packed)
        level = tail_column(packs, sample, 3)
        levels.append(level[0:1])
        scaled = packed * (tail_column(packs, sample, 1) * level)
        inputs.append(scaled.astype(BF16))
        rows.append(scaled.T.astype(BF16))
    grad_mixed, grad_probs = [], []
    for unit in range(2 * heads):
        head, sample = unit // 2, unit % 2
        weight = output_turned[:, head * HEAD_DIM : (head + 1) * HEAD_DIM]
        lanes = slice(sample * CHANNELS, (sample + 1) * CHANNELS)
        grad_mixed.append(dot(grads[:, lanes], weight).astype(BF16))
        turned = dot(weight, grads_turned[lanes], TN).astype(BF16)
        value = kept[sample, :, head * 3 * HEAD_DIM + 2 * HEAD_DIM : (head + 1) * 3 * HEAD_DIM]
        grad_probs.append(dot(value, turned))
    columns = heads * 3 * HEAD_DIM
    gathered[columns:, :] = jnp.zeros((gathered.shape[0] - columns, 128), F32)
    height = out.shape[1]
    half = block // 2
    row = row_index((height, 128))
    low_lanes = lane_index((height, 128)) < CHANNELS
    pad = jnp.zeros((1, 128 - block), F32) if block < 128 else None
    copies = []
    for head in range(heads):
        at = head * 3 * HEAD_DIM
        query_total, rest_total = None, None
        ends = []
        for sample in range(2):
            unit = 2 * head + sample
            probs = probs_turned[unit]
            grad = grad_probs[unit]
            inner = jnp.sum(grad * probs, axis=0, keepdims=True)
            grad_scores = (probs * (grad - inner) * (HEAD_DIM**-0.5)).astype(BF16)
            grad_value = dot(probs.astype(BF16), grad_mixed[unit])
            grad_key = dot(grad_scores, kept[sample, :, at : at + HEAD_DIM])
            grad_query = dot(keys_turned[unit], grad_scores).astype(BF16)
            rest = jnp.concatenate([grad_key, grad_value], axis=1).astype(BF16)
            query_term = dot(grad_query, inputs[sample])
            rest_term = dot(rows[sample], rest)
            query_total = query_term if query_total is None else query_total + query_term
            rest_total = rest_term if rest_total is None else rest_total + rest_term
            turned_sum = jnp.sum(grad_query.astype(F32), axis=1, keepdims=True)
            turned_sum = jnp.broadcast_to(turned_sum, (HEAD_DIM, 128)).T[0:1]
            rest_sum = jnp.sum(rest.astype(F32), axis=0, keepdims=True)
            ends.append(jnp.concatenate([turned_sum, rest_sum], axis=1) * levels[sample])
        gathered[at : at + HEAD_DIM, :] = query_total
        gathered[at + HEAD_DIM : at + 3 * HEAD_DIM, :] = rest_total.T
        summed[:, at : at + 3 * HEAD_DIM] = ends[0] + ends[1]
        start = columns * head // heads // block
        stop = columns * (head + 1) // heads // block
        for chip in range(start, stop):
            base = chip * block
            piece = jnp.where(low_lanes, gathered[base : base + height, :], gathered[base + half : base + half + height, :])
            line = summed[:, base : base + block]
            high = rounded(line)
            pair = [high, line - high]
            if pad is not None:
                pair = [jnp.concatenate([part, pad], axis=1) for part in pair]
            tail = jnp.where(row == half, pair[0], jnp.where(row == half + 1, pair[1], 0.0))
            blocks[chip] = jnp.where(row < half, piece, tail).astype(BF16)
        span = pl.ds(start, stop - start)
        copies.append(pltpu.make_async_copy(blocks.at[span], out.at[span], copied.at[head]))
        copies[-1].start()
    for copy in copies:
        copy.wait()


def closing_kernel(block, factor, taken, weight, embed, after, kept, sent):
    second = on_second_core()
    total = taken[0].astype(F32)
    for chip in range(1, taken.shape[0]):
        total = total + taken[chip].astype(F32)
    half = block // 2
    height = total.shape[0]
    row = row_index((height, 128))
    ends = total[half : half + 1] + total[half + 1 : half + 2]
    turned = jnp.where(row < half, total, 0.0).T
    lane = lane_index((1, 128))
    ends_low = jnp.where(lane < half, ends, 0.0)[:, 0:height]
    ends_high = jnp.where(lane < half, pltpu.roll(ends, 128 - half, 1), 0.0)[:, 0:height]
    lower = jnp.concatenate([turned[0:CHANNELS], ends_low, jnp.zeros((7, height), F32)], axis=0)
    upper = jnp.concatenate([turned[CHANNELS:], ends_high, jnp.zeros((7, height), F32)], axis=0)
    joined = jnp.concatenate([lower, upper], axis=1)
    high = joined.astype(BF16)
    low = (joined - high.astype(F32)).astype(BF16)
    middle = embed.shape[1] // 2
    step = middle // 3
    parts = []
    for start in range(0, 2 * middle, step):
        columns = weight[:, start : start + step]
        product = dot(high, columns) + dot(low, columns)
        scale = jnp.sum(product[:CHANNELS] * embed[:, start : start + step].astype(F32), axis=0, keepdims=True)
        parts.append(jnp.concatenate([scale, product[CHANNELS : CHANNELS + 1]], axis=0) * factor)
    sides = []
    for side in (parts[:3], parts[3:]):
        lines = [part[which : which + 1, i : i + 128] for which in range(2) for part in side for i in range(0, step, 128)]
        sides.append(jnp.concatenate(lines, axis=0))
    kept[...] = jnp.where(second, sides[1], sides[0])
    sent[...] = jnp.where(second, sides[0], sides[1])


def payload_kernel(noise_levels, own, a_here, a_there, b_here, b_there, out):
    tokens = own.shape[0]
    own_a = a_here[0:tokens, 0:CHANNELS] + a_there[...]
    own_b = b_here[0:tokens, 0:CHANNELS] + b_there[tokens:, 0:CHANNELS]
    sample = own[:, 0:CHANNELS].astype(F32) - noise_levels[0, 0] * own_a
    out[...] = jnp.where(on_critic(), own_b - own_a, sample).T.astype(BF16)


def spread_kernel(total, other, crossed, out, crossed_out):
    line = (total[...] + other[...]).astype(BF16)
    for chip in range(out.shape[0]):
        out[chip] = line
    crossed_out[...] = crossed[...]


def join_kernel(total, near, out):
    second = on_second_core()
    count = total.shape[0] // 2
    left = jnp.where(second, near[...], total[...])
    right = jnp.where(second, total[...], near[...])
    for which in range(2):
        for side, half in enumerate((left, right)):
            for i in range(count):
                at = (side * count + i) * 128
                out[which : which + 1, at : at + 128] = half[which * count + i : which * count + i + 1, :]


def call(kernel, out_shapes, inputs, scalars=0, scratch=(), flops=0, after=(), far_out=False):
    specs = [pl.BlockSpec(memory_space=pltpu.SMEM)] * scalars
    specs += [pl.BlockSpec(memory_space=pltpu.VMEM)] * (len(inputs) - scalars)
    specs += [pl.BlockSpec(memory_space=pl.ANY)] * len(after)
    space = pl.ANY if far_out else pltpu.VMEM
    return pl.pallas_call(
        kernel,
        out_shape=out_shapes,
        in_specs=specs,
        out_specs=jax.tree.map(lambda _: pl.BlockSpec(memory_space=space), out_shapes),
        scratch_shapes=list(scratch),
        compiler_params=pltpu.CompilerParams(vmem_limit_bytes=28 * 2**20),
        cost_estimate=pl.CostEstimate(flops=flops, bytes_accessed=0, transcendentals=0),
    )(*inputs, *after)


def struct(shape, dtype):
    return jax.ShapeDtypeStruct(shape, dtype)


def other_core(value):
    return lax.ppermute(value, "fsdp", [(i, i ^ 1) for i in range(lax.axis_size("fsdp"))])


def other_half(value):
    return lax.ppermute(value, "seq", [(0, 1), (1, 0)])


def between_chips(value):
    count = lax.axis_size("fsdp")
    groups = [list(range(core, count, 2)) for core in range(2)]
    return lax.all_to_all(value, "fsdp", 0, 0, tiled=True, axis_index_groups=groups)


def per_device(
    base_latents,
    noise_latents,
    noise_levels,
    replay_latents,
    replay_levels,
    cotangent,
    embed_weight,
    qkv_weight,
    output_weight,
    modulation,
):
    second_core = on_second_core()
    devices = lax.axis_size("fsdp")
    chips = devices // 2
    embed = embed_weight[0]
    weight = qkv_weight[0]
    width = embed.shape[1]
    columns = weight.shape[1] // 2
    block = columns // chips
    height = round_up(block, 8)
    packed = round_up(block + block // 2 + 2, 8)
    folded = round_up(block // 2 + 2, 8)
    padded = round_up(2 * weight.shape[0], 128)
    tokens = base_latents.shape[2]
    heads = columns // (3 * HEAD_DIM)
    out_columns = output_weight.shape[1] // 2
    output_turned = output_weight[0].T
    output_turned = jnp.where(second_core, output_turned[:, out_columns:], output_turned[:, :out_columns])

    received = other_core(weight)
    own_turned = call(own_rows_kernel, struct((columns, padded), F32), (weight,))
    turned = call(
        functools.partial(weight_kernel, chips),
        struct((chips, height, padded), BF16),
        (own_turned, received),
        scratch=[
            pltpu.VMEM((columns + height - block, padded), F32),
            pltpu.VMEM((chips, height, padded), BF16),
            pltpu.SemaphoreType.DMA((chips // 8,)),
        ],
        far_out=True,
    )
    taken = between_chips(turned)

    own, stack = call(
        pack_kernel,
        (struct((tokens, 384), BF16), struct((272, width), BF16)),
        (
            noise_levels,
            replay_levels,
            base_latents[0, 0],
            noise_latents[0, 0],
            replay_latents[0, 0],
            cotangent[0, 0],
            embed,
            modulation[0],
        ),
        scalars=2,
        after=(turned,),
    )
    here = jnp.stack([own, other_core(own)])
    there = other_half(here)

    matrices, own_columns = call(
        functools.partial(product_kernel, block),
        (struct((chips, packed, 128), BF16), struct((2 * folded, width), BF16)),
        (taken, stack),
        scratch=[pltpu.VMEM((height, width), BF16)],
        after=(there,),
    )
    whole, offsets, kept, keys_turned, probs, vel_b, vel_crossing = call(
        functools.partial(second_pass_kernel, block),
        (
            struct((columns, 2 * CHANNELS), BF16),
            struct((8, columns), F32),
            struct((2, 2 * tokens, columns), BF16),
            struct((2 * heads, HEAD_DIM, 2 * tokens), BF16),
            struct((2 * heads, 2 * tokens, 2 * tokens), F32),
            struct((2 * tokens, 2 * CHANNELS), F32),
            struct((2 * tokens, 2 * CHANNELS), F32),
        ),
        (between_chips(matrices), here, there, output_turned),
        scratch=[pltpu.VMEM((columns, 2 * CHANNELS), F32), pltpu.VMEM((columns, 2 * CHANNELS), F32)],
    )
    vel_here = vel_b + other_core(vel_crossing)
    vel_there = other_half(vel_here)
    vel_a, vel_a_crossing = call(
        first_pass_kernel,
        (struct((2 * tokens, 2 * CHANNELS), F32), struct((2 * tokens, 2 * CHANNELS), F32)),
        (whole, offsets, here, there, output_turned),
        flops=4 * 10**9,
        after=(vel_here,),
    )
    vel_a_here = vel_a + other_core(vel_a_crossing)
    products = call(
        functools.partial(backward_kernel, block),
        struct((chips, folded, 128), BF16),
        (kept, keys_turned, probs, here, there, vel_here, vel_there, output_turned),
        scratch=[
            pltpu.VMEM((columns + 2 * folded, 128), F32),
            pltpu.VMEM((1, columns), F32),
            pltpu.VMEM((chips, folded, 128), BF16),
            pltpu.SemaphoreType.DMA((heads,)),
        ],
        after=(vel_a,),
        far_out=True,
    )

    payload = call(
        payload_kernel,
        struct((CHANNELS, tokens), BF16),
        (noise_levels, own, vel_a_here, other_half(vel_a_here[tokens:, :CHANNELS]), vel_here, vel_there),
        scalars=1,
    )
    crossed = lax.ppermute(payload, "role", [(0, 1), (1, 0)])

    samples = devices * base_latents.shape[1]
    lines = width // 128
    kept_half, sent_half = call(
        functools.partial(closing_kernel, block, 1.0 / (samples * 2 * tokens)),
        (struct((lines, 128), F32), struct((lines, 128), F32)),
        (between_chips(products), own_columns, embed),
        after=(payload,),
    )
    total = kept_half + other_core(sent_half)
    spread, crossed = call(
        spread_kernel,
        (struct((chips, lines, 128), BF16), struct(crossed.shape, BF16)),
        (total, other_half(total), crossed),
    )
    total = jnp.sum(between_chips(spread).astype(F32), axis=0)
    mod_grads = call(join_kernel, struct((2, width), F32), (total, other_core(total)))
    return (crossed.T[None, None], mod_grads[None])


def solution(mesh):
    return jax.shard_map(
        per_device,
        mesh=mesh,
        in_specs=(
            P("role", "fsdp", "seq", None),
            P("role", "fsdp", "seq", None),
            P("role", "fsdp"),
            P("role", "fsdp", "seq", None),
            P("role", "fsdp"),
            P("role", "fsdp", "seq", None),
            P("role", None, None),
            P("role", "fsdp", "seq"),
            P("role", "seq", None),
            P("role", None, None, None),
        ),
        out_specs=(P("role", "fsdp", "seq", None), P("role", None, None)),
        check_vma=False,
    )
```

```python
import functools

import jax
import jax.numpy as jnp
from jax import lax
from jax.experimental import pallas as pl
from jax.experimental.pallas import tpu as pltpu
from jax.sharding import PartitionSpec as P

HEAD_DIM = 128
CHANNELS = 64
EPSILON = 1e-06
F32 = jnp.float32
BF16 = jnp.bfloat16
NT = (((1,), (1,)), ((), ()))
NN = (((1,), (0,)), ((), ()))
TN = (((0,), (0,)), ((), ()))


def dot(a, b, dims=NN):
    return lax.dot_general(a, b, dims, preferred_element_type=F32)


def round_up(value, step):
    return (value + step - 1) // step * step


def rounded(value):
    return value.astype(BF16).astype(F32)


def three_parts(value):
    high = rounded(value)
    middle = rounded(value - high)
    return high, middle, rounded(value - high - middle)


def lane_index(shape):
    return lax.broadcasted_iota(jnp.int32, shape, len(shape) - 1)


def row_index(shape):
    return lax.broadcasted_iota(jnp.int32, shape, len(shape) - 2)


def on_second_core():
    return lax.rem(lax.axis_index("fsdp"), 2) == 1


def on_critic():
    return lax.axis_index("role") == 1


def pack_kernel(noise_levels, replay_levels, base, noise, replay, cotangent, embed, modulation, after, pack, stack):
    critic = on_critic()
    modulation_a = modulation[0]
    modulation_b = jnp.where(critic, modulation[1], modulation_a)
    embed_f = embed[...].astype(F32)
    scaled_b = (embed_f * modulation_b[0:1, :]).astype(BF16)
    stack[0:64, :] = embed[...]
    stack[64:128, :] = (embed_f * modulation_a[0:1, :]).astype(BF16)
    stack[128:192, :] = scaled_b
    stack[192:256, :] = scaled_b
    shifts = []
    for pair in (modulation_a, modulation_b):
        shift = pair[1:2, :]
        high = rounded(shift)
        shifts += [high, shift - high]
    shifts.append(jnp.zeros((12, embed.shape[1]), F32))
    stack[256:272, :] = jnp.concatenate(shifts, axis=0).astype(BF16)
    level = noise_levels[0, 0]
    level_two = jnp.where(critic, level, replay_levels[0, 0])
    base_f = base[...].astype(F32)
    noise_f = noise[...].astype(F32)
    input_a = rounded((1.0 - level) * base_f + level * noise_f)
    input_b = jnp.where(critic, input_a, replay[...].astype(F32))
    known = jnp.where(critic, noise_f - base_f, cotangent[...].astype(F32))
    known_high = rounded(known)
    tokens = input_a.shape[0]
    rows = jnp.concatenate([input_a, input_b], axis=0).astype(BF16)
    total = jnp.zeros((2 * tokens, 1), F32)
    width = embed.shape[1]
    for start in range(0, width, 512):
        embedded = dot(rows, embed[:, start : start + 512])
        total = total + jnp.sum(embedded * embedded, axis=-1, keepdims=True)
    scale = lax.rsqrt(total / width + EPSILON)
    lane = lane_index((tokens, 128))
    tail = jnp.zeros((tokens, 128), F32)
    ones = jnp.ones((tokens, 1), F32)
    for which, column in enumerate((scale[:tokens], scale[tokens:], ones * level, ones * level_two)):
        for part, value in enumerate(three_parts(column)):
            tail = jnp.where(lane == which * 3 + part, value, tail)
    pack[:, 0:64] = input_a.astype(BF16)
    pack[:, 64:128] = input_b.astype(BF16)
    pack[:, 128:192] = known_high.astype(BF16)
    pack[:, 192:256] = (known - known_high).astype(BF16)
    pack[:, 256:384] = tail.astype(BF16)


def turn_rows(rows, padded, second):
    count, columns = rows.shape
    empty = jnp.zeros((count, columns), F32)
    parts = [jnp.where(second, empty, rows), jnp.where(second, rows, empty)]
    if padded > 2 * count:
        parts.append(jnp.zeros((padded - 2 * count, columns), F32))
    return jnp.concatenate(parts, axis=0).T


def half_columns(weight, second):
    columns = weight.shape[1] // 2
    start = pl.multiple_of(jnp.where(second, columns, 0), 128)
    return weight[:, pl.ds(start, columns)].astype(F32)


def own_rows_kernel(weight, out):
    second = on_second_core()
    out[...] = turn_rows(half_columns(weight, second), out.shape[1], second)


def weight_kernel(chips, own, received, out, turned, blocks, copied):
    second = on_second_core()
    columns, padded = own.shape
    turned[0:columns, :] = own[...] + turn_rows(half_columns(received, second), padded, jnp.logical_not(second))
    block = columns // chips
    height = out.shape[1]
    spare = padded // 4
    upper_lanes = lane_index((16, padded)) >= padded - spare
    group = 8
    copies = []
    for chip in range(chips):
        piece = turned[chip * block : chip * block + height, :]
        last = turned[chip * block + height : (chip + 1) * block, :]
        lines = [pltpu.roll(last, padded - spare * (part + 1), 1) for part in range(3)]
        lines.append(jnp.zeros_like(last))
        top = jnp.where(upper_lanes, jnp.concatenate(lines, axis=0), piece[0:16])
        blocks[chip] = jnp.concatenate([top, piece[16:]], axis=0).astype(BF16)
        if chip % group == group - 1:
            span = pl.ds(chip + 1 - group, group)
            copies.append(pltpu.make_async_copy(blocks.at[span], out.at[span], copied.at[len(copies)]))
            copies[-1].start()
    for copy in copies:
        copy.wait()


def product_kernel(block, taken, stack, out, columns_out):
    chips, height, padded = taken.shape
    half = block // 2
    width = stack.shape[1]
    depth = width // chips
    group = 128 // (depth & -depth)
    spare = padded - depth
    lane = lane_index((4, padded))
    for start in range(0, chips, group):
        mains, lasts = [], []
        for chip in range(start, start + group):
            piece = taken[chip].astype(F32)
            mains.append(piece[:, 0:depth])
            top, next_top = piece[0:8], piece[8:16]
            low = pltpu.roll(top, spare, 1)[0:4]
            middle = pltpu.roll(top, 2 * spare, 1)[4:8]
            high = pltpu.roll(next_top, 3 * spare, 1)[0:4]
            lasts.append(jnp.where(lane < spare, low, jnp.where(lane < 2 * spare, middle, high))[:, 0:depth])
        last = jnp.concatenate(lasts, axis=1)
        joined = jnp.concatenate([jnp.concatenate(mains, axis=1), last, jnp.zeros_like(last)], axis=0)
        span = slice(start * depth, (start + group) * depth)
        columns_out[:, span] = joined.astype(BF16)
    weight = columns_out[...]
    products = dot(weight, stack[0:256, :], NT)
    first, second = products[:, 0:128], products[:, 128:256]
    offsets = dot(stack[256:272, :], weight, NT)
    lines = []
    gap = jnp.zeros((1, CHANNELS - block), F32)
    for offset in (offsets[0:1, 0:block] + offsets[1:2, 0:block], offsets[2:3, 0:block] + offsets[3:4, 0:block]):
        high = rounded(offset)
        lines.append(jnp.concatenate([high, gap, offset - high, gap], axis=1))
    low_lanes = lane_index((half, 128)) < CHANNELS
    folded = jnp.where(low_lanes, second[0:half], second[half:block])
    spare = out.shape[1] - block - half - 2
    parts = [first[0:block], folded] + lines
    if spare:
        parts.append(jnp.zeros((spare, 128), F32))
    whole = jnp.concatenate(parts, axis=0).astype(BF16)
    for chip in range(chips):
        out[chip] = whole


def token_rows(packs, sample, start, stop):
    return jnp.concatenate([pack[sample, :, start:stop] for pack in packs], axis=0)


def tail_column(packs, sample, which):
    tail = token_rows(packs, sample, 256, 384).astype(F32)
    at = 3 * which
    return tail[:, at : at + 1] + tail[:, at + 1 : at + 2] + tail[:, at + 2 : at + 3]


def forward(which, packs, matrices, offsets, output_turned, keep, keep_turned, probs_out, velocity):
    heads = output_turned.shape[1] // HEAD_DIM
    low_lanes = lane_index((1, 128)) < CHANNELS
    rows, scales, levels, turned_scales = [], [], [], []
    for sample in range(2):
        inputs = token_rows(packs, sample, 0, 128).astype(F32)
        turned = pltpu.roll(inputs, CHANNELS, 1)
        level = tail_column(packs, sample, 2 + which)
        plain, scaled = (turned, inputs) if which else (inputs, turned)
        rows.append(jnp.where(low_lanes, plain, scaled * level))
        scale = tail_column(packs, sample, which)
        scales.append(scale)
        levels.append(level[0:1])
        turned_scales.append(jnp.broadcast_to(scale, (scale.shape[0], 128)).T[0:1])
    tokens = rows[0].shape[0]
    inputs = jnp.concatenate(rows, axis=0)
    turned = inputs.T.astype(BF16)
    inputs = inputs.astype(BF16)
    offset = offsets[which : which + 1, :]
    columns = offset.shape[1]
    offset_turned = jnp.broadcast_to(offset, (128, columns)).T[:, 0:1]
    units = []
    for head in range(heads):
        at = head * 3 * HEAD_DIM
        span = slice(at, at + 3 * HEAD_DIM)
        matrix = matrices[span, :]
        if keep is None:
            product = dot(inputs, matrix[HEAD_DIM : 2 * HEAD_DIM], NT)
        else:
            product = dot(inputs, matrix, NT)
        product_turned = dot(matrix, turned)
        for sample in range(2):
            own = slice(sample * tokens, (sample + 1) * tokens)
            line = offset[:, span] if keep is not None else offset[:, at + HEAD_DIM : at + 2 * HEAD_DIM]
            qkv = (product[own] * scales[sample] + line * levels[sample]).astype(BF16)
            flipped = product_turned[:, own] * turned_scales[sample] + offset_turned[span] * levels[sample]
            flipped = flipped.astype(BF16)
            key = qkv
            if keep is not None:
                keep[sample, :, span] = qkv
                keep_turned[2 * head + sample] = flipped[HEAD_DIM : 2 * HEAD_DIM]
                key = qkv[:, HEAD_DIM : 2 * HEAD_DIM]
            units.append((key, flipped[0:HEAD_DIM], flipped[2 * HEAD_DIM :]))
    totals = [None, None]
    scores = [dot(key, query) * (HEAD_DIM**-0.5) for key, query, _ in units]
    for unit, score in enumerate(scores):
        powers = jnp.exp(score - jnp.max(score, axis=0, keepdims=True))
        probs = powers * (1.0 / jnp.sum(powers, axis=0, keepdims=True))
        if probs_out is not None:
            probs_out[unit] = probs
        mixed = dot(units[unit][2], probs.astype(BF16)).astype(BF16)
        head = unit // 2
        term = dot(output_turned[:, head * HEAD_DIM : (head + 1) * HEAD_DIM], mixed)
        before = totals[unit % 2]
        totals[unit % 2] = term if before is None else before + term
    velocity[...] = jnp.concatenate(totals, axis=0).T


def second_pass_kernel(
    block,
    taken,
    here,
    there,
    output_turned,
    matrices,
    offsets,
    keep,
    keep_turned,
    probs,
    velocity,
    crossing,
    stacked,
    stacked_two,
):
    chips = taken.shape[0]
    half = block // 2
    low_lanes = lane_index((half, 128)) < CHANNELS
    lines = [[], []]
    for chip in range(chips):
        piece = taken[chip].astype(F32)
        at = chip * block
        stacked[at : at + block, :] = piece[0:block]
        folded = piece[block : block + half]
        turned = pltpu.roll(folded, CHANNELS, 1)
        stacked_two[at : at + half, :] = jnp.where(low_lanes, piece[0:half], turned)
        stacked_two[at + half : at + block, :] = jnp.where(low_lanes, piece[half:block], folded)
        for which in range(2):
            line = piece[block + half + which : block + half + which + 1]
            lines[which].append((line + pltpu.roll(line, CHANNELS, 1))[:, 0:block])
    matrices[...] = stacked[...].astype(BF16)
    joined = [jnp.concatenate(line, axis=1) for line in lines]
    offsets[...] = jnp.concatenate(joined + [jnp.zeros((6, offsets.shape[1]), F32)], axis=0)
    both = stacked_two[...].astype(BF16)
    forward(1, (here, there), both, offsets, output_turned, keep, keep_turned, probs, velocity)
    crossing[...] = pltpu.roll(velocity[...], CHANNELS, 1)


def first_pass_kernel(matrices, offsets, here, there, output_turned, after, velocity, crossing):
    forward(0, (here, there), matrices, offsets, output_turned, None, None, None, velocity)
    crossing[...] = pltpu.roll(velocity[...], CHANNELS, 1)


def swap_tokens(value):
    half = value.shape[0] // 2
    return jnp.concatenate([value[half:], value[:half]], axis=0)


def backward_kernel(
    block,
    kept,
    keys_turned,
    probs_turned,
    here,
    there,
    vel_here,
    vel_there,
    output_turned,
    after,
    out,
    gathered,
    summed,
    blocks,
    copied,
):
    critic = on_critic()
    packs = (here, there)
    heads = output_turned.shape[1] // HEAD_DIM
    velocity = vel_here[...] + swap_tokens(vel_there[...])
    lane = lane_index((1, 128))
    known = []
    for sample in range(2):
        part = token_rows(packs, sample, 128, 256).astype(F32)
        known.append(part[:, 0:CHANNELS] + part[:, CHANNELS:])
    known = jnp.concatenate(known, axis=1)
    grad_velocity = jnp.where(critic, velocity - known, known)
    grads_turned = grad_velocity.T.astype(BF16)
    grads = grad_velocity.astype(BF16)
    inputs, rows, levels = [], [], []
    for sample in range(2):
        packed = token_rows(packs, sample, 0, 128).astype(F32)
        packed = jnp.where(lane < CHANNELS, pltpu.roll(packed, CHANNELS, 1), packed)
        level = tail_column(packs, sample, 3)
        levels.append(level[0:1])
        scaled = packed * (tail_column(packs, sample, 1) * level)
        inputs.append(scaled.astype(BF16))
        rows.append(scaled.T.astype(BF16))
    grad_mixed, grad_probs = [], []
    for unit in range(2 * heads):
        head, sample = unit // 2, unit % 2
        weight = output_turned[:, head * HEAD_DIM : (head + 1) * HEAD_DIM]
        lanes = slice(sample * CHANNELS, (sample + 1) * CHANNELS)
        grad_mixed.append(dot(grads[:, lanes], weight).astype(BF16))
        turned = dot(weight, grads_turned[lanes], TN).astype(BF16)
        value = kept[sample, :, head * 3 * HEAD_DIM + 2 * HEAD_DIM : (head + 1) * 3 * HEAD_DIM]
        grad_probs.append(dot(value, turned))
    columns = heads * 3 * HEAD_DIM
    gathered[columns:, :] = jnp.zeros((gathered.shape[0] - columns, 128), F32)
    height = out.shape[1]
    half = block // 2
    row = row_index((height, 128))
    low_lanes = lane_index((height, 128)) < CHANNELS
    pad = jnp.zeros((1, 128 - block), F32) if block < 128 else None
    copies = []
    for head in range(heads):
        at = head * 3 * HEAD_DIM
        query_total, rest_total = None, None
        ends = []
        for sample in range(2):
            unit = 2 * head + sample
            probs = probs_turned[unit]
            grad = grad_probs[unit]
            inner = jnp.sum(grad * probs, axis=0, keepdims=True)
            grad_scores = (probs * (grad - inner) * (HEAD_DIM**-0.5)).astype(BF16)
            grad_value = dot(probs.astype(BF16), grad_mixed[unit])
            grad_key = dot(grad_scores, kept[sample, :, at : at + HEAD_DIM])
            grad_query = dot(keys_turned[unit], grad_scores).astype(BF16)
            rest = jnp.concatenate([grad_key, grad_value], axis=1).astype(BF16)
            query_term = dot(grad_query, inputs[sample])
            rest_term = dot(rows[sample], rest)
            query_total = query_term if query_total is None else query_total + query_term
            rest_total = rest_term if rest_total is None else rest_total + rest_term
            turned_sum = jnp.sum(grad_query.astype(F32), axis=1, keepdims=True)
            turned_sum = jnp.broadcast_to(turned_sum, (HEAD_DIM, 128)).T[0:1]
            rest_sum = jnp.sum(rest.astype(F32), axis=0, keepdims=True)
            ends.append(jnp.concatenate([turned_sum, rest_sum], axis=1) * levels[sample])
        gathered[at : at + HEAD_DIM, :] = query_total
        gathered[at + HEAD_DIM : at + 3 * HEAD_DIM, :] = rest_total.T
        summed[:, at : at + 3 * HEAD_DIM] = ends[0] + ends[1]
        start = columns * head // heads // block
        stop = columns * (head + 1) // heads // block
        for chip in range(start, stop):
            base = chip * block
            piece = jnp.where(low_lanes, gathered[base : base + height, :], gathered[base + half : base + half + height, :])
            line = summed[:, base : base + block]
            high = rounded(line)
            pair = [high, line - high]
            if pad is not None:
                pair = [jnp.concatenate([part, pad], axis=1) for part in pair]
            tail = jnp.where(row == half, pair[0], jnp.where(row == half + 1, pair[1], 0.0))
            blocks[chip] = jnp.where(row < half, piece, tail).astype(BF16)
        span = pl.ds(start, stop - start)
        copies.append(pltpu.make_async_copy(blocks.at[span], out.at[span], copied.at[head]))
        copies[-1].start()
    for copy in copies:
        copy.wait()


def closing_kernel(block, factor, taken, weight, embed, after, kept, sent):
    second = on_second_core()
    total = taken[0].astype(F32)
    for chip in range(1, taken.shape[0]):
        total = total + taken[chip].astype(F32)
    half = block // 2
    height = total.shape[0]
    row = row_index((height, 128))
    ends = total[half : half + 1] + total[half + 1 : half + 2]
    lines = [jnp.where(row < half, total, 0.0), jnp.zeros((128 - height, 128), F32)]
    turned = jnp.concatenate(lines, axis=0).T
    products = turned[0:CHANNELS] + pltpu.roll(turned[CHANNELS:], half, 1)
    joined = jnp.concatenate([products, ends, jnp.zeros((7, 128), F32)], axis=0)[:, 0 : weight.shape[0]]
    high = joined.astype(BF16)
    low = (joined - high.astype(F32)).astype(BF16)
    middle = embed.shape[1] // 2
    step = middle // 3
    parts = []
    for start in range(0, 2 * middle, step):
        columns = weight[:, start : start + step]
        product = dot(high, columns) + dot(low, columns)
        scale = jnp.sum(product[:CHANNELS] * embed[:, start : start + step].astype(F32), axis=0, keepdims=True)
        parts.append(jnp.concatenate([scale, product[CHANNELS : CHANNELS + 1]], axis=0) * factor)
    sides = []
    for side in (parts[:3], parts[3:]):
        lines = [part[which : which + 1, i : i + 128] for which in range(2) for part in side for i in range(0, step, 128)]
        sides.append(jnp.concatenate(lines, axis=0))
    kept[...] = jnp.where(second, sides[1], sides[0])
    sent[...] = jnp.where(second, sides[0], sides[1])


def payload_kernel(noise_levels, own, a_here, a_there, b_here, b_there, out):
    tokens = own.shape[0]
    own_a = a_here[0:tokens, 0:CHANNELS] + a_there[...]
    own_b = b_here[0:tokens, 0:CHANNELS] + b_there[tokens:, 0:CHANNELS]
    sample = own[:, 0:CHANNELS].astype(F32) - noise_levels[0, 0] * own_a
    out[...] = jnp.where(on_critic(), own_b - own_a, sample).T.astype(BF16)


def spread_kernel(total, other, out):
    line = (total[...] + other[...]).astype(BF16)
    for chip in range(out.shape[0]):
        out[chip] = line


def join_kernel(total, near, crossed, out, crossed_out):
    crossed_out[...] = crossed[...]
    second = on_second_core()
    count = total.shape[0] // 2
    left = jnp.where(second, near[...], total[...])
    right = jnp.where(second, total[...], near[...])
    for which in range(2):
        for side, half in enumerate((left, right)):
            for i in range(count):
                at = (side * count + i) * 128
                out[which : which + 1, at : at + 128] = half[which * count + i : which * count + i + 1, :]


def call(kernel, out_shapes, inputs, scalars=0, scratch=(), flops=0, after=(), far_out=False):
    specs = [pl.BlockSpec(memory_space=pltpu.SMEM)] * scalars
    specs += [pl.BlockSpec(memory_space=pltpu.VMEM)] * (len(inputs) - scalars)
    specs += [pl.BlockSpec(memory_space=pl.ANY)] * len(after)
    space = pl.ANY if far_out else pltpu.VMEM
    return pl.pallas_call(
        kernel,
        out_shape=out_shapes,
        in_specs=specs,
        out_specs=jax.tree.map(lambda _: pl.BlockSpec(memory_space=space), out_shapes),
        scratch_shapes=list(scratch),
        compiler_params=pltpu.CompilerParams(vmem_limit_bytes=28 * 2**20),
        cost_estimate=pl.CostEstimate(flops=flops, bytes_accessed=0, transcendentals=0),
    )(*inputs, *after)


def struct(shape, dtype):
    return jax.ShapeDtypeStruct(shape, dtype)


def other_core(value):
    return lax.ppermute(value, "fsdp", [(i, i ^ 1) for i in range(lax.axis_size("fsdp"))])


def other_half(value):
    return lax.ppermute(value, "seq", [(0, 1), (1, 0)])


def between_chips(value):
    count = lax.axis_size("fsdp")
    groups = [list(range(core, count, 2)) for core in range(2)]
    return lax.all_to_all(value, "fsdp", 0, 0, tiled=True, axis_index_groups=groups)


def per_device(
    base_latents,
    noise_latents,
    noise_levels,
    replay_latents,
    replay_levels,
    cotangent,
    embed_weight,
    qkv_weight,
    output_weight,
    modulation,
):
    second_core = on_second_core()
    devices = lax.axis_size("fsdp")
    chips = devices // 2
    embed = embed_weight[0]
    weight = qkv_weight[0]
    width = embed.shape[1]
    columns = weight.shape[1] // 2
    block = columns // chips
    height = block - 4
    packed = round_up(block + block // 2 + 2, 8)
    folded = round_up(block // 2 + 2, 8)
    padded = round_up(2 * weight.shape[0], 128)
    tokens = base_latents.shape[2]
    heads = columns // (3 * HEAD_DIM)
    out_columns = output_weight.shape[1] // 2
    output_turned = output_weight[0].T
    output_turned = jnp.where(second_core, output_turned[:, out_columns:], output_turned[:, :out_columns])

    received = other_core(weight)
    own_turned = call(own_rows_kernel, struct((columns, padded), F32), (weight,))
    turned = call(
        functools.partial(weight_kernel, chips),
        struct((chips, height, padded), BF16),
        (own_turned, received),
        scratch=[
            pltpu.VMEM((columns, padded), F32),
            pltpu.VMEM((chips, height, padded), BF16),
            pltpu.SemaphoreType.DMA((chips // 8,)),
        ],
        far_out=True,
    )
    taken = between_chips(turned)

    own, stack = call(
        pack_kernel,
        (struct((tokens, 384), BF16), struct((272, width), BF16)),
        (
            noise_levels,
            replay_levels,
            base_latents[0, 0],
            noise_latents[0, 0],
            replay_latents[0, 0],
            cotangent[0, 0],
            embed,
            modulation[0],
        ),
        scalars=2,
        after=(turned,),
    )
    here = jnp.stack([own, other_core(own)])
    there = other_half(here)

    matrices, own_columns = call(
        functools.partial(product_kernel, block),
        (struct((chips, packed, 128), BF16), struct((height + 8, width), BF16)),
        (taken, stack),
    )
    whole, offsets, kept, keys_turned, probs, vel_b, vel_crossing = call(
        functools.partial(second_pass_kernel, block),
        (
            struct((columns, 2 * CHANNELS), BF16),
            struct((8, columns), F32),
            struct((2, 2 * tokens, columns), BF16),
            struct((2 * heads, HEAD_DIM, 2 * tokens), BF16),
            struct((2 * heads, 2 * tokens, 2 * tokens), F32),
            struct((2 * tokens, 2 * CHANNELS), F32),
            struct((2 * tokens, 2 * CHANNELS), F32),
        ),
        (between_chips(matrices), here, there, output_turned),
        scratch=[pltpu.VMEM((columns, 2 * CHANNELS), F32), pltpu.VMEM((columns, 2 * CHANNELS), F32)],
    )
    vel_here = vel_b + other_core(vel_crossing)
    vel_there = other_half(vel_here)
    vel_a, vel_a_crossing = call(
        first_pass_kernel,
        (struct((2 * tokens, 2 * CHANNELS), F32), struct((2 * tokens, 2 * CHANNELS), F32)),
        (whole, offsets, here, there, output_turned),
        flops=4 * 10**9,
        after=(vel_here,),
    )
    vel_a_here = vel_a + other_core(vel_a_crossing)
    products = call(
        functools.partial(backward_kernel, block),
        struct((chips, folded, 128), BF16),
        (kept, keys_turned, probs, here, there, vel_here, vel_there, output_turned),
        scratch=[
            pltpu.VMEM((columns + 2 * folded, 128), F32),
            pltpu.VMEM((1, columns), F32),
            pltpu.VMEM((chips, folded, 128), BF16),
            pltpu.SemaphoreType.DMA((heads,)),
        ],
        after=(vel_a,),
        far_out=True,
    )

    payload = call(
        payload_kernel,
        struct((CHANNELS, tokens), BF16),
        (noise_levels, own, vel_a_here, other_half(vel_a_here[tokens:, :CHANNELS]), vel_here, vel_there),
        scalars=1,
    )
    crossed = lax.ppermute(payload, "role", [(0, 1), (1, 0)])

    samples = devices * base_latents.shape[1]
    lines = width // 128
    kept_half, sent_half = call(
        functools.partial(closing_kernel, block, 1.0 / (samples * 2 * tokens)),
        (struct((lines, 128), F32), struct((lines, 128), F32)),
        (between_chips(products), own_columns, embed),
        after=(payload,),
    )
    total = kept_half + other_core(sent_half)
    spread = call(spread_kernel, struct((chips, lines, 128), BF16), (total, other_half(total)))
    total = jnp.sum(between_chips(spread).astype(F32), axis=0)
    mod_grads, crossed = call(
        join_kernel,
        (struct((2, width), F32), struct(crossed.shape, BF16)),
        (total, other_core(total), crossed),
    )
    return (crossed.T[None, None], mod_grads[None])


def solution(mesh):
    return jax.shard_map(
        per_device,
        mesh=mesh,
        in_specs=(
            P("role", "fsdp", "seq", None),
            P("role", "fsdp", "seq", None),
            P("role", "fsdp"),
            P("role", "fsdp", "seq", None),
            P("role", "fsdp"),
            P("role", "fsdp", "seq", None),
            P("role", None, None),
            P("role", "fsdp", "seq"),
            P("role", "seq", None),
            P("role", None, None, None),
        ),
        out_specs=(P("role", "fsdp", "seq", None), P("role", None, None)),
        check_vma=False,
    )
```

```python
import functools

import jax
import jax.numpy as jnp
from jax import lax
from jax.experimental import pallas as pl
from jax.experimental.pallas import tpu as pltpu
from jax.sharding import PartitionSpec as P

HEAD_DIM = 128
CHANNELS = 64
EPSILON = 1e-06
F32 = jnp.float32
BF16 = jnp.bfloat16
NT = (((1,), (1,)), ((), ()))
NN = (((1,), (0,)), ((), ()))
TN = (((0,), (0,)), ((), ()))


def dot(a, b, dims=NN):
    return lax.dot_general(a, b, dims, preferred_element_type=F32)


def round_up(value, step):
    return (value + step - 1) // step * step


def rounded(value):
    return value.astype(BF16).astype(F32)


def three_parts(value):
    high = rounded(value)
    middle = rounded(value - high)
    return high, middle, rounded(value - high - middle)


def lane_index(shape):
    return lax.broadcasted_iota(jnp.int32, shape, len(shape) - 1)


def row_index(shape):
    return lax.broadcasted_iota(jnp.int32, shape, len(shape) - 2)


def on_second_core():
    return lax.rem(lax.axis_index("fsdp"), 2) == 1


def on_critic():
    return lax.axis_index("role") == 1


def stack_kernel(embed, modulation, after, stack):
    modulation_a = modulation[0]
    modulation_b = jnp.where(on_critic(), modulation[1], modulation_a)
    embed_f = embed[...].astype(F32)
    stack[0:64, :] = embed[...]
    stack[64:128, :] = (embed_f * modulation_a[0:1, :]).astype(BF16)
    stack[128:192, :] = (embed_f * modulation_b[0:1, :]).astype(BF16)
    shifts = []
    for pair in (modulation_a, modulation_b):
        shift = pair[1:2, :]
        high = rounded(shift)
        shifts += [high, shift - high]
    shifts.append(jnp.zeros((60, embed.shape[1]), F32))
    stack[192:256, :] = jnp.concatenate(shifts, axis=0).astype(BF16)


def pack_kernel(noise_levels, replay_levels, base, noise, replay, cotangent, embed, after, pack):
    critic = on_critic()
    level = noise_levels[0, 0]
    level_two = jnp.where(critic, level, replay_levels[0, 0])
    base_f = base[...].astype(F32)
    noise_f = noise[...].astype(F32)
    input_a = rounded((1.0 - level) * base_f + level * noise_f)
    input_b = jnp.where(critic, input_a, replay[...].astype(F32))
    known = jnp.where(critic, noise_f - base_f, cotangent[...].astype(F32))
    known_high = rounded(known)
    tokens = input_a.shape[0]
    rows = jnp.concatenate([input_a, input_b], axis=0).astype(BF16)
    total = jnp.zeros((2 * tokens, 1), F32)
    width = embed.shape[1]
    for start in range(0, width, 512):
        embedded = dot(rows, embed[:, start : start + 512])
        total = total + jnp.sum(embedded * embedded, axis=-1, keepdims=True)
    scale = lax.rsqrt(total / width + EPSILON)
    lane = lane_index((tokens, 128))
    tail = jnp.zeros((tokens, 128), F32)
    ones = jnp.ones((tokens, 1), F32)
    for which, column in enumerate((scale[:tokens], scale[tokens:], ones * level, ones * level_two)):
        for part, value in enumerate(three_parts(column)):
            tail = jnp.where(lane == which * 3 + part, value, tail)
    pack[:, 0:64] = input_a.astype(BF16)
    pack[:, 64:128] = input_b.astype(BF16)
    pack[:, 128:192] = known_high.astype(BF16)
    pack[:, 192:256] = (known - known_high).astype(BF16)
    pack[:, 256:384] = tail.astype(BF16)


def turn_rows(rows, padded, second):
    count, columns = rows.shape
    empty = jnp.zeros((count, columns), F32)
    parts = [jnp.where(second, empty, rows), jnp.where(second, rows, empty)]
    if padded > 2 * count:
        parts.append(jnp.zeros((padded - 2 * count, columns), F32))
    return jnp.concatenate(parts, axis=0).T


def half_columns(weight, second):
    columns = weight.shape[1] // 2
    start = pl.multiple_of(jnp.where(second, columns, 0), 128)
    return weight[:, pl.ds(start, columns)].astype(F32)


def own_rows_kernel(weight, out):
    second = on_second_core()
    out[...] = turn_rows(half_columns(weight, second), out.shape[1], second)


def weight_kernel(chips, own, received, out, turned):
    second = on_second_core()
    columns, padded = own.shape
    turned[0:columns, :] = own[...] + turn_rows(half_columns(received, second), padded, jnp.logical_not(second))
    block = columns // chips
    height = out.shape[1]
    spare = padded // 4
    upper_lanes = lane_index((16, padded)) >= padded - spare
    for chip in range(chips):
        piece = turned[chip * block : chip * block + height, :]
        last = turned[chip * block + height : (chip + 1) * block, :]
        lines = [pltpu.roll(last, padded - spare * (part + 1), 1) for part in range(3)]
        lines.append(jnp.zeros_like(last))
        top = jnp.where(upper_lanes, jnp.concatenate(lines, axis=0), piece[0:16])
        out[chip] = jnp.concatenate([top, piece[16:]], axis=0).astype(BF16)


def product_kernel(block, taken, stack, after, out, columns_out):
    chips, height, padded = taken.shape
    half = block // 2
    width = stack.shape[1]
    depth = width // chips
    group = 128 // (depth & -depth)
    spare = padded - depth
    lane = lane_index((4, padded))
    for start in range(0, chips, group):
        mains, lasts = [], []
        for chip in range(start, start + group):
            piece = taken[chip].astype(F32)
            mains.append(piece[:, 0:depth])
            top, next_top = piece[0:8], piece[8:16]
            low = pltpu.roll(top, spare, 1)[0:4]
            middle = pltpu.roll(top, 2 * spare, 1)[4:8]
            high = pltpu.roll(next_top, 3 * spare, 1)[0:4]
            lasts.append(jnp.where(lane < spare, low, jnp.where(lane < 2 * spare, middle, high))[:, 0:depth])
        last = jnp.concatenate(lasts, axis=1)
        joined = jnp.concatenate([jnp.concatenate(mains, axis=1), last, jnp.zeros_like(last)], axis=0)
        span = slice(start * depth, (start + group) * depth)
        columns_out[:, span] = joined.astype(BF16)
    weight = columns_out[...]
    products = dot(weight, stack[...], NT)
    first, second = products[:, 0:128], products[:, 128:256]
    tall = jnp.concatenate([second, jnp.zeros((128 - second.shape[0], 128), F32)], axis=0).T
    lines = []
    gap = jnp.zeros((1, CHANNELS - block), F32)
    for at in (CHANNELS, CHANNELS + 2):
        offset = tall[at : at + 1, 0:block] + tall[at + 1 : at + 2, 0:block]
        high = rounded(offset)
        lines.append(jnp.concatenate([high, gap, offset - high, gap], axis=1))
    low_lanes = lane_index((half, 128)) < CHANNELS
    folded = jnp.where(low_lanes, second[0:half], pltpu.roll(second, CHANNELS, 1)[half:block])
    spare = out.shape[1] - block - half - 2
    parts = [first[0:block], folded] + lines
    if spare:
        parts.append(jnp.zeros((spare, 128), F32))
    whole = jnp.concatenate(parts, axis=0).astype(BF16)
    for chip in range(chips):
        out[chip] = whole


def token_rows(packs, sample, start, stop):
    return jnp.concatenate([pack[sample, :, start:stop] for pack in packs], axis=0)


def tail_column(packs, sample, which):
    tail = token_rows(packs, sample, 256, 384).astype(F32)
    at = 3 * which
    return tail[:, at : at + 1] + tail[:, at + 1 : at + 2] + tail[:, at + 2 : at + 3]


def scaled_rows(which, packs):
    low_lanes = lane_index((1, 128)) < CHANNELS
    rows, scales, levels = [], [], []
    for sample in range(2):
        inputs = token_rows(packs, sample, 0, 128).astype(F32)
        turned = pltpu.roll(inputs, CHANNELS, 1)
        level = tail_column(packs, sample, 2 + which)
        plain, scaled = (turned, inputs) if which else (inputs, turned)
        rows.append(jnp.where(low_lanes, plain, scaled * level))
        scales.append(tail_column(packs, sample, which))
        levels.append(level[0:1])
    return jnp.concatenate(rows, axis=0), scales, levels


def forward(which, packs, matrices, offsets, output_turned, keys_out, probs_out, velocity, crossing):
    heads = output_turned.shape[1] // HEAD_DIM
    inputs, scales, levels = scaled_rows(which, packs)
    tokens = inputs.shape[0] // 2
    turned_scales = [jnp.broadcast_to(scale, (tokens, 128)).T[0:1] for scale in scales]
    turned = inputs.T.astype(BF16)
    inputs = inputs.astype(BF16)
    offset = offsets[which : which + 1, :]
    offset_turned = jnp.broadcast_to(offset, (128, offset.shape[1])).T[:, 0:1]
    units = []
    for head in range(heads):
        at = head * 3 * HEAD_DIM
        span = slice(at, at + 3 * HEAD_DIM)
        matrix = matrices[span, :]
        product = dot(inputs, matrix[HEAD_DIM : 2 * HEAD_DIM], NT)
        product_turned = dot(matrix, turned)
        line = offset[:, at + HEAD_DIM : at + 2 * HEAD_DIM]
        for sample in range(2):
            own = slice(sample * tokens, (sample + 1) * tokens)
            key = (product[own] * scales[sample] + line * levels[sample]).astype(BF16)
            flipped = product_turned[:, own] * turned_scales[sample] + offset_turned[span] * levels[sample]
            flipped = flipped.astype(BF16)
            if keys_out is not None:
                keys_out[2 * head + sample] = flipped[HEAD_DIM : 2 * HEAD_DIM]
            units.append((key, flipped[0:HEAD_DIM], flipped[2 * HEAD_DIM :]))
    totals = [None, None]
    scores = [dot(key, query) * (HEAD_DIM**-0.5) for key, query, _ in units]
    for unit, score in enumerate(scores):
        powers = jnp.exp(score - jnp.max(score, axis=0, keepdims=True))
        probs = powers * (1.0 / jnp.sum(powers, axis=0, keepdims=True))
        if probs_out is not None:
            probs_out[unit] = probs
        mixed = dot(units[unit][2], probs.astype(BF16)).astype(BF16)
        head = unit // 2
        term = dot(output_turned[:, head * HEAD_DIM : (head + 1) * HEAD_DIM], mixed)
        before = totals[unit % 2]
        totals[unit % 2] = term if before is None else before + term
    whole = jnp.concatenate(totals, axis=0).T
    velocity[...] = whole
    crossing[...] = pltpu.roll(whole, CHANNELS, 1)


def second_pass_kernel(
    block, taken, here, there, output_turned, matrices, offsets, keys_turned, probs, velocity, crossing, stacked
):
    chips = taken.shape[0]
    half = block // 2
    low_lanes = lane_index((half, 128)) < CHANNELS
    lines = [[], []]
    for chip in range(chips):
        piece = taken[chip].astype(F32)
        at = chip * block
        folded = piece[block : block + half]
        turned = pltpu.roll(folded, CHANNELS, 1)
        stacked[at : at + half, :] = jnp.where(low_lanes, piece[0:half], turned)
        stacked[at + half : at + block, :] = jnp.where(low_lanes, piece[half:block], folded)
        for which in range(2):
            line = piece[block + half + which : block + half + which + 1]
            lines[which].append((line + pltpu.roll(line, CHANNELS, 1))[:, 0:block])
    joined = [jnp.concatenate(line, axis=1) for line in lines]
    offsets[...] = jnp.concatenate(joined + [jnp.zeros((6, offsets.shape[1]), F32)], axis=0)
    matrices[...] = stacked[...].astype(BF16)
    forward(1, (here, there), matrices[...], offsets, output_turned, keys_turned, probs, velocity, crossing)


def first_pass_kernel(
    block, taken, matrices, offsets, here, there, output_turned, after, velocity, crossing, kept, scaled_out, rows_out, stacked
):
    packs = (here, there)
    for chip in range(taken.shape[0]):
        stacked[chip * block : (chip + 1) * block, :] = taken[chip].astype(F32)[0:block]
    forward(0, packs, stacked[...].astype(BF16), offsets, output_turned, None, None, velocity, crossing)
    inputs, scales, levels = scaled_rows(1, packs)
    tokens = inputs.shape[0] // 2
    low_lanes = lane_index((1, 128)) < CHANNELS
    for sample in range(2):
        plain = inputs[sample * tokens : (sample + 1) * tokens]
        plain = jnp.where(low_lanes, plain, pltpu.roll(plain, CHANNELS, 1))
        scaled = plain * (scales[sample] * levels[sample])
        scaled_out[sample] = scaled.astype(BF16)
        rows_out[sample] = scaled.T.astype(BF16)
    inputs = inputs.astype(BF16)
    for head in range(output_turned.shape[1] // HEAD_DIM):
        for place, part in enumerate((0, 2)):
            at = (3 * head + part) * HEAD_DIM
            to = (2 * head + place) * HEAD_DIM
            product = dot(inputs, matrices[at : at + HEAD_DIM, :], NT)
            line = offsets[1:2, at : at + HEAD_DIM]
            for sample in range(2):
                own = product[sample * tokens : (sample + 1) * tokens]
                kept[sample, :, to : to + HEAD_DIM] = (own * scales[sample] + line * levels[sample]).astype(BF16)


def swap_tokens(value):
    half = value.shape[0] // 2
    return jnp.concatenate([value[half:], value[:half]], axis=0)


def backward_kernel(
    block,
    kept,
    scaled,
    rows,
    keys_turned,
    probs_turned,
    here,
    there,
    vel_here,
    vel_there,
    output_turned,
    out,
    gathered,
    summed,
):
    critic = on_critic()
    packs = (here, there)
    heads = output_turned.shape[1] // HEAD_DIM
    velocity = vel_here[...] + swap_tokens(vel_there[...].astype(F32))
    known, levels = [], []
    for sample in range(2):
        part = token_rows(packs, sample, 128, 256).astype(F32)
        known.append(part[:, 0:CHANNELS] + part[:, CHANNELS:])
        levels.append(tail_column((here,), sample, 3)[0:1])
    known = jnp.concatenate(known, axis=1)
    grad_velocity = jnp.where(critic, velocity - known, known)
    grads_turned = grad_velocity.T.astype(BF16)
    grads = grad_velocity.astype(BF16)
    grad_mixed, grad_probs = [], []
    for unit in range(2 * heads):
        head, sample = unit // 2, unit % 2
        weight = output_turned[:, head * HEAD_DIM : (head + 1) * HEAD_DIM]
        lanes = slice(sample * CHANNELS, (sample + 1) * CHANNELS)
        grad_mixed.append(dot(grads[:, lanes], weight).astype(BF16))
        turned = dot(weight, grads_turned[lanes], TN).astype(BF16)
        value = kept[sample, :, (2 * head + 1) * HEAD_DIM : (2 * head + 2) * HEAD_DIM]
        grad_probs.append(dot(value, turned))
    columns = heads * 3 * HEAD_DIM
    gathered[columns:, :] = jnp.zeros((gathered.shape[0] - columns, 128), F32)
    height = out.shape[1]
    half = block // 2
    row = row_index((height, 128))
    low_lanes = lane_index((height, 128)) < CHANNELS
    pad = jnp.zeros((1, 128 - block), F32) if block < 128 else None
    for head in range(heads):
        at = head * 3 * HEAD_DIM
        query_total, rest_total = None, None
        ends = []
        for sample in range(2):
            unit = 2 * head + sample
            probs = probs_turned[unit]
            grad = grad_probs[unit]
            inner = jnp.sum(grad * probs, axis=0, keepdims=True)
            grad_scores = (probs * (grad - inner) * (HEAD_DIM**-0.5)).astype(BF16)
            grad_value = dot(probs.astype(BF16), grad_mixed[unit])
            grad_key = dot(grad_scores, kept[sample, :, 2 * head * HEAD_DIM : (2 * head + 1) * HEAD_DIM])
            grad_query = dot(keys_turned[unit], grad_scores).astype(BF16)
            rest = jnp.concatenate([grad_key, grad_value], axis=1).astype(BF16)
            query_term = dot(grad_query, scaled[sample])
            rest_term = dot(rows[sample], rest)
            query_total = query_term if query_total is None else query_total + query_term
            rest_total = rest_term if rest_total is None else rest_total + rest_term
            turned_sum = jnp.sum(grad_query.astype(F32), axis=1, keepdims=True)
            turned_sum = jnp.broadcast_to(turned_sum, (HEAD_DIM, 128)).T[0:1]
            rest_sum = jnp.sum(rest.astype(F32), axis=0, keepdims=True)
            ends.append(jnp.concatenate([turned_sum, rest_sum], axis=1) * levels[sample])
        gathered[at : at + HEAD_DIM, :] = query_total
        gathered[at + HEAD_DIM : at + 3 * HEAD_DIM, :] = rest_total.T
        summed[:, at : at + 3 * HEAD_DIM] = ends[0] + ends[1]
        start = columns * head // heads // block
        stop = columns * (head + 1) // heads // block
        for chip in range(start, stop):
            base = chip * block
            piece = jnp.where(low_lanes, gathered[base : base + height, :], gathered[base + half : base + half + height, :])
            line = summed[:, base : base + block]
            high = rounded(line)
            pair = [high, line - high]
            if pad is not None:
                pair = [jnp.concatenate([part, pad], axis=1) for part in pair]
            tail = jnp.where(row == half, pair[0], jnp.where(row == half + 1, pair[1], 0.0))
            out[chip] = jnp.where(row < half, piece, tail).astype(BF16)


def closing_kernel(block, factor, taken, weight, embed, after, kept, sent):
    second = on_second_core()
    total = taken[0].astype(F32)
    for chip in range(1, taken.shape[0]):
        total = total + taken[chip].astype(F32)
    half = block // 2
    height = total.shape[0]
    row = row_index((height, 128))
    ends = total[half : half + 1] + total[half + 1 : half + 2]
    lines = [jnp.where(row < half, total, 0.0), jnp.zeros((128 - height, 128), F32)]
    turned = jnp.concatenate(lines, axis=0).T
    products = turned[0:CHANNELS] + pltpu.roll(turned[CHANNELS:], half, 1)
    joined = jnp.concatenate([products, ends, jnp.zeros((7, 128), F32)], axis=0)[:, 0 : weight.shape[0]]
    high = joined.astype(BF16)
    low = (joined - high.astype(F32)).astype(BF16)
    middle = embed.shape[1] // 2
    step = middle // 3
    parts = []
    for start in range(0, 2 * middle, step):
        columns = weight[:, start : start + step]
        product = dot(high, columns) + dot(low, columns)
        scale = jnp.sum(product[:CHANNELS] * embed[:, start : start + step].astype(F32), axis=0, keepdims=True)
        parts.append(jnp.concatenate([scale, product[CHANNELS : CHANNELS + 1]], axis=0) * factor)
    sides = []
    for side in (parts[:3], parts[3:]):
        lines = [part[which : which + 1, i : i + 128] for which in range(2) for part in side for i in range(0, step, 128)]
        sides.append(jnp.concatenate(lines, axis=0))
    kept[...] = jnp.where(second, sides[1], sides[0])
    sent[...] = jnp.where(second, sides[0], sides[1])


def payload_kernel(noise_levels, own, a_here, b_here, there, out):
    tokens = own.shape[0]
    own_a = a_here[0:tokens, 0:CHANNELS] + there[:, 0:CHANNELS]
    own_b = b_here[0:tokens, 0:CHANNELS] + there[:, CHANNELS:]
    sample = own[:, 0:CHANNELS].astype(F32) - noise_levels[0, 0] * own_a
    out[...] = jnp.where(on_critic(), own_b - own_a, sample).T.astype(BF16)


def spread_kernel(total, other, out):
    line = (total[...] + other[...]).astype(BF16)
    for chip in range(out.shape[0]):
        out[chip] = line


def join_kernel(total, near, crossed, out, crossed_out):
    crossed_out[...] = crossed[...]
    second = on_second_core()
    count = total.shape[0] // 2
    left = jnp.where(second, near[...], total[...])
    right = jnp.where(second, total[...], near[...])
    for which in range(2):
        for side, half in enumerate((left, right)):
            for i in range(count):
                at = (side * count + i) * 128
                out[which : which + 1, at : at + 128] = half[which * count + i : which * count + i + 1, :]


def call(kernel, out_shapes, inputs, scalars=0, scratch=(), flops=0, after=()):
    specs = [pl.BlockSpec(memory_space=pltpu.SMEM)] * scalars
    specs += [pl.BlockSpec(memory_space=pltpu.VMEM)] * (len(inputs) - scalars)
    specs += [pl.BlockSpec(memory_space=pl.ANY)] * len(after)
    return pl.pallas_call(
        kernel,
        out_shape=out_shapes,
        in_specs=specs,
        out_specs=jax.tree.map(lambda _: pl.BlockSpec(memory_space=pltpu.VMEM), out_shapes),
        scratch_shapes=list(scratch),
        compiler_params=pltpu.CompilerParams(vmem_limit_bytes=28 * 2**20),
        cost_estimate=pl.CostEstimate(flops=flops, bytes_accessed=0, transcendentals=0),
    )(*inputs, *after)


def struct(shape, dtype):
    return jax.ShapeDtypeStruct(shape, dtype)


def other_core(value):
    return lax.ppermute(value, "fsdp", [(i, i ^ 1) for i in range(lax.axis_size("fsdp"))])


def other_half(value):
    return lax.ppermute(value, "seq", [(0, 1), (1, 0)])


def between_chips(value):
    count = lax.axis_size("fsdp")
    groups = [list(range(core, count, 2)) for core in range(2)]
    return lax.all_to_all(value, "fsdp", 0, 0, tiled=True, axis_index_groups=groups)


def per_device(
    base_latents,
    noise_latents,
    noise_levels,
    replay_latents,
    replay_levels,
    cotangent,
    embed_weight,
    qkv_weight,
    output_weight,
    modulation,
):
    second_core = on_second_core()
    devices = lax.axis_size("fsdp")
    chips = devices // 2
    embed = embed_weight[0]
    weight = qkv_weight[0]
    width = embed.shape[1]
    columns = weight.shape[1] // 2
    block = columns // chips
    height = block - 4
    packed = round_up(block + block // 2 + 2, 8)
    folded = round_up(block // 2 + 2, 8)
    padded = round_up(2 * weight.shape[0], 128)
    tokens = base_latents.shape[2]
    heads = columns // (3 * HEAD_DIM)
    out_columns = output_weight.shape[1] // 2
    output_turned = output_weight[0].T
    output_turned = jnp.where(second_core, output_turned[:, out_columns:], output_turned[:, :out_columns])

    received = other_core(weight)
    own_turned = call(own_rows_kernel, struct((columns, padded), F32), (weight,))
    turned = call(
        functools.partial(weight_kernel, chips),
        struct((chips, height, padded), BF16),
        (own_turned, received),
        scratch=[pltpu.VMEM((columns, padded), F32)],
    )
    taken = between_chips(turned)
    stack = call(stack_kernel, struct((256, width), BF16), (embed, modulation[0]), after=(turned,))

    own = call(
        pack_kernel,
        struct((tokens, 384), BF16),
        (
            noise_levels,
            replay_levels,
            base_latents[0, 0],
            noise_latents[0, 0],
            replay_latents[0, 0],
            cotangent[0, 0],
            embed,
        ),
        scalars=2,
        after=(turned,),
    )
    matrices, own_columns = call(
        functools.partial(product_kernel, block),
        (struct((chips, packed, 128), BF16), struct((height + 8, width), BF16)),
        (taken, stack),
        after=(own,),
    )
    here = jnp.stack([own, other_core(own)])
    there = other_half(here)

    taken = between_chips(matrices)
    whole, offsets, keys_turned, probs, vel_b, vel_crossing = call(
        functools.partial(second_pass_kernel, block),
        (
            struct((columns, 2 * CHANNELS), BF16),
            struct((8, columns), F32),
            struct((2 * heads, HEAD_DIM, 2 * tokens), BF16),
            struct((2 * heads, 2 * tokens, 2 * tokens), F32),
            struct((2 * tokens, 2 * CHANNELS), F32),
            struct((2 * tokens, 2 * CHANNELS), F32),
        ),
        (taken, here, there, output_turned),
        scratch=[pltpu.VMEM((columns, 2 * CHANNELS), F32)],
    )
    vel_here = vel_b + other_core(vel_crossing)
    vel_there = other_half(vel_here.astype(BF16))
    vel_a, vel_a_crossing, kept, scaled, rows = call(
        functools.partial(first_pass_kernel, block),
        (
            struct((2 * tokens, 2 * CHANNELS), F32),
            struct((2 * tokens, 2 * CHANNELS), F32),
            struct((2, 2 * tokens, 2 * heads * HEAD_DIM), BF16),
            struct((2, 2 * tokens, 2 * CHANNELS), BF16),
            struct((2, 2 * CHANNELS, 2 * tokens), BF16),
        ),
        (taken, whole, offsets, here, there, output_turned),
        scratch=[pltpu.VMEM((columns, 2 * CHANNELS), F32)],
        flops=4 * 10**9,
        after=(vel_here,),
    )
    products = call(
        functools.partial(backward_kernel, block),
        struct((chips, folded, 128), BF16),
        (kept, scaled, rows, keys_turned, probs, here, there, vel_here, vel_there, output_turned),
        scratch=[pltpu.VMEM((columns + 2 * folded, 128), F32), pltpu.VMEM((1, columns), F32)],
    )

    vel_a_here = vel_a + other_core(vel_a_crossing)
    both_there = other_half(jnp.concatenate([vel_a_here[tokens:, :CHANNELS], vel_here[tokens:, :CHANNELS]], axis=1))
    payload = call(
        payload_kernel,
        struct((CHANNELS, tokens), BF16),
        (noise_levels, own, vel_a_here, vel_here, both_there),
        scalars=1,
    )
    crossed = lax.ppermute(payload, "role", [(0, 1), (1, 0)])

    samples = devices * base_latents.shape[1]
    lines = width // 128
    kept_half, sent_half = call(
        functools.partial(closing_kernel, block, 1.0 / (samples * 2 * tokens)),
        (struct((lines, 128), F32), struct((lines, 128), F32)),
        (between_chips(products), own_columns, embed),
        after=(payload,),
    )
    total = kept_half + other_core(sent_half)
    spread = call(spread_kernel, struct((chips, lines, 128), BF16), (total, other_half(total)))
    total = jnp.sum(between_chips(spread).astype(F32), axis=0)
    mod_grads, crossed = call(
        join_kernel,
        (struct((2, width), F32), struct(crossed.shape, BF16)),
        (total, other_core(total), crossed),
    )
    return (crossed.T[None, None], mod_grads[None])


def solution(mesh):
    return jax.shard_map(
        per_device,
        mesh=mesh,
        in_specs=(
            P("role", "fsdp", "seq", None),
            P("role", "fsdp", "seq", None),
            P("role", "fsdp"),
            P("role", "fsdp", "seq", None),
            P("role", "fsdp"),
            P("role", "fsdp", "seq", None),
            P("role", None, None),
            P("role", "fsdp", "seq"),
            P("role", "seq", None),
            P("role", None, None, None),
        ),
        out_specs=(P("role", "fsdp", "seq", None), P("role", None, None)),
        check_vma=False,
    )
```

```python
import functools

import jax
import jax.numpy as jnp
from jax import lax
from jax.experimental import pallas as pl
from jax.experimental.pallas import tpu as pltpu
from jax.sharding import PartitionSpec as P

HEAD_DIM = 128
CHANNELS = 64
EPSILON = 1e-06
F32 = jnp.float32
BF16 = jnp.bfloat16
NT = (((1,), (1,)), ((), ()))
NN = (((1,), (0,)), ((), ()))
TN = (((0,), (0,)), ((), ()))


def dot(a, b, dims=NN):
    return lax.dot_general(a, b, dims, preferred_element_type=F32)


def round_up(value, step):
    return (value + step - 1) // step * step


def rounded(value):
    return value.astype(BF16).astype(F32)


def three_parts(value):
    high = rounded(value)
    middle = rounded(value - high)
    return high, middle, rounded(value - high - middle)


def lane_index(shape):
    return lax.broadcasted_iota(jnp.int32, shape, len(shape) - 1)


def row_index(shape):
    return lax.broadcasted_iota(jnp.int32, shape, len(shape) - 2)


def on_second_core():
    return lax.rem(lax.axis_index("fsdp"), 2) == 1


def on_critic():
    return lax.axis_index("role") == 1


def stack_kernel(embed, modulation, after, stack):
    modulation_a = modulation[0]
    modulation_b = jnp.where(on_critic(), modulation[1], modulation_a)
    embed_f = embed[...].astype(F32)
    stack[0:64, :] = embed[...]
    stack[64:128, :] = (embed_f * modulation_a[0:1, :]).astype(BF16)
    stack[128:192, :] = (embed_f * modulation_b[0:1, :]).astype(BF16)
    shifts = []
    for pair in (modulation_a, modulation_b):
        shift = pair[1:2, :]
        high = rounded(shift)
        shifts += [high, shift - high]
    shifts.append(jnp.zeros((60, embed.shape[1]), F32))
    stack[192:256, :] = jnp.concatenate(shifts, axis=0).astype(BF16)


def pack_kernel(noise_levels, replay_levels, base, noise, replay, cotangent, embed, after, pack):
    critic = on_critic()
    level = noise_levels[0, 0]
    level_two = jnp.where(critic, level, replay_levels[0, 0])
    base_f = base[...].astype(F32)
    noise_f = noise[...].astype(F32)
    input_a = rounded((1.0 - level) * base_f + level * noise_f)
    input_b = jnp.where(critic, input_a, replay[...].astype(F32))
    known = jnp.where(critic, noise_f - base_f, cotangent[...].astype(F32))
    known_high = rounded(known)
    tokens = input_a.shape[0]
    rows = jnp.concatenate([input_a, input_b], axis=0).astype(BF16)
    total = jnp.zeros((2 * tokens, 1), F32)
    width = embed.shape[1]
    for start in range(0, width, 512):
        embedded = dot(rows, embed[:, start : start + 512])
        total = total + jnp.sum(embedded * embedded, axis=-1, keepdims=True)
    scale = lax.rsqrt(total / width + EPSILON)
    lane = lane_index((tokens, 128))
    tail = jnp.zeros((tokens, 128), F32)
    ones = jnp.ones((tokens, 1), F32)
    for which, column in enumerate((scale[:tokens], scale[tokens:], ones * level, ones * level_two)):
        for part, value in enumerate(three_parts(column)):
            tail = jnp.where(lane == which * 3 + part, value, tail)
    pack[:, 0:64] = input_a.astype(BF16)
    pack[:, 64:128] = input_b.astype(BF16)
    pack[:, 128:192] = known_high.astype(BF16)
    pack[:, 192:256] = (known - known_high).astype(BF16)
    pack[:, 256:384] = tail.astype(BF16)


def turn_rows(rows, padded, second):
    count, columns = rows.shape
    empty = jnp.zeros((count, columns), F32)
    parts = [jnp.where(second, empty, rows), jnp.where(second, rows, empty)]
    if padded > 2 * count:
        parts.append(jnp.zeros((padded - 2 * count, columns), F32))
    return jnp.concatenate(parts, axis=0).T


def half_columns(weight, second):
    columns = weight.shape[1] // 2
    start = pl.multiple_of(jnp.where(second, columns, 0), 128)
    return weight[:, pl.ds(start, columns)].astype(F32)


def own_rows_kernel(weight, out):
    second = on_second_core()
    out[...] = turn_rows(half_columns(weight, second), out.shape[1], second)


def weight_kernel(chips, own, received, out, turned):
    second = on_second_core()
    columns, padded = own.shape
    turned[0:columns, :] = own[...] + turn_rows(half_columns(received, second), padded, jnp.logical_not(second))
    block = columns // chips
    height = out.shape[1]
    spare = padded // 4
    upper_lanes = lane_index((16, padded)) >= padded - spare
    for chip in range(chips):
        piece = turned[chip * block : chip * block + height, :]
        last = turned[chip * block + height : (chip + 1) * block, :]
        lines = [pltpu.roll(last, padded - spare * (part + 1), 1) for part in range(3)]
        lines.append(jnp.zeros_like(last))
        top = jnp.where(upper_lanes, jnp.concatenate(lines, axis=0), piece[0:16])
        out[chip] = jnp.concatenate([top, piece[16:]], axis=0).astype(BF16)


def product_kernel(block, taken, stack, after, out, columns_out):
    chips, height, padded = taken.shape
    half = block // 2
    width = stack.shape[1]
    depth = width // chips
    group = 128 // (depth & -depth)
    spare = padded - depth
    lane = lane_index((4, padded))
    for start in range(0, chips, group):
        mains, lasts = [], []
        for chip in range(start, start + group):
            piece = taken[chip].astype(F32)
            mains.append(piece[:, 0:depth])
            top, next_top = piece[0:8], piece[8:16]
            low = pltpu.roll(top, spare, 1)[0:4]
            middle = pltpu.roll(top, 2 * spare, 1)[4:8]
            high = pltpu.roll(next_top, 3 * spare, 1)[0:4]
            lasts.append(jnp.where(lane < spare, low, jnp.where(lane < 2 * spare, middle, high))[:, 0:depth])
        last = jnp.concatenate(lasts, axis=1)
        joined = jnp.concatenate([jnp.concatenate(mains, axis=1), last, jnp.zeros_like(last)], axis=0)
        span = slice(start * depth, (start + group) * depth)
        columns_out[:, span] = joined.astype(BF16)
    weight = columns_out[...]
    products = dot(weight, stack[...], NT)
    first, second = products[:, 0:128], products[:, 128:256]
    tall = jnp.concatenate([second, jnp.zeros((128 - second.shape[0], 128), F32)], axis=0).T
    lines = []
    gap = jnp.zeros((1, CHANNELS - block), F32)
    for at in (CHANNELS, CHANNELS + 2):
        offset = tall[at : at + 1, 0:block] + tall[at + 1 : at + 2, 0:block]
        high = rounded(offset)
        lines.append(jnp.concatenate([high, gap, offset - high, gap], axis=1))
    low_lanes = lane_index((half, 128)) < CHANNELS
    folded = jnp.where(low_lanes, second[0:half], pltpu.roll(second, CHANNELS, 1)[half:block])
    spare = out.shape[1] - block - half - 2
    parts = [first[0:block], folded] + lines
    if spare:
        parts.append(jnp.zeros((spare, 128), F32))
    whole = jnp.concatenate(parts, axis=0).astype(BF16)
    for chip in range(chips):
        out[chip] = whole


def token_rows(packs, sample, start, stop):
    return jnp.concatenate([pack[sample, :, start:stop] for pack in packs], axis=0)


def tail_column(packs, sample, which):
    tail = token_rows(packs, sample, 256, 384).astype(F32)
    at = 3 * which
    return tail[:, at : at + 1] + tail[:, at + 1 : at + 2] + tail[:, at + 2 : at + 3]


def fill_rows(which, packs, rows, turned, scale, lines):
    low_lanes = lane_index((1, 128)) < CHANNELS
    lines[...] = jnp.zeros_like(lines)
    for sample in range(2):
        inputs = token_rows(packs, sample, 0, 128).astype(F32)
        tokens = inputs.shape[0]
        own = slice(sample * tokens, (sample + 1) * tokens)
        flipped = pltpu.roll(inputs, CHANNELS, 1)
        level = jnp.broadcast_to(tail_column(packs, sample, 2 + which), inputs.shape)
        norm = jnp.broadcast_to(tail_column(packs, sample, which), inputs.shape)
        plain, scaled_part = (flipped, inputs) if which else (inputs, flipped)
        both = jnp.where(low_lanes, plain, scaled_part * level)
        rows[own, :] = both.astype(BF16)
        turned[:, own] = both.T.astype(BF16)
        scale[own, :] = norm
        lines[0:1, own] = norm.T[0:1]
        lines[1:2, own] = level.T[0:1]


def tokens_kernel(here, there, rows, turned, scale, lines, known, scaled, scaled_turned):
    packs = (here, there)
    fill_rows(1, packs, rows, turned, scale, lines)
    low_lanes = lane_index((1, 128)) < CHANNELS
    parts = []
    for sample in range(2):
        inputs = token_rows(packs, sample, 0, 128).astype(F32)
        whole = jnp.where(low_lanes, pltpu.roll(inputs, CHANNELS, 1), inputs)
        whole = whole * (tail_column(packs, sample, 1) * tail_column(packs, sample, 3))
        scaled[sample] = whole.astype(BF16)
        scaled_turned[sample] = whole.T.astype(BF16)
        part = token_rows(packs, sample, 128, 256).astype(F32)
        parts.append(part[:, 0:CHANNELS] + part[:, CHANNELS:])
    known[...] = jnp.concatenate(parts, axis=1)


def sample_level(lines, sample):
    at = sample * (lines.shape[1] // 2)
    return lines[1:2, at : at + 1]


def forward(which, rows, turned, scale, lines, matrices, offsets, output_turned, keys_out, probs_out, velocity, crossing):
    heads = output_turned.shape[1] // HEAD_DIM
    tokens = rows.shape[0] // 2
    inputs = rows[...]
    inputs_turned = turned[...]
    levels = [sample_level(lines, sample) for sample in range(2)]
    offset = offsets[which : which + 1, :]
    offset_turned = jnp.broadcast_to(offset, (128, offset.shape[1])).T[:, 0:1]
    units = []
    for head in range(heads):
        at = head * 3 * HEAD_DIM
        span = slice(at, at + 3 * HEAD_DIM)
        matrix = matrices[span, :]
        product = dot(inputs, matrix[HEAD_DIM : 2 * HEAD_DIM], NT)
        product_turned = dot(matrix, inputs_turned)
        line = offset[:, at + HEAD_DIM : at + 2 * HEAD_DIM]
        for sample in range(2):
            own = slice(sample * tokens, (sample + 1) * tokens)
            key = (product[own] * scale[own, :] + line * levels[sample]).astype(BF16)
            norms = lines[0:1, own]
            flipped = product_turned[:, own] * norms + offset_turned[span] * levels[sample]
            flipped = flipped.astype(BF16)
            if keys_out is not None:
                keys_out[2 * head + sample] = flipped[HEAD_DIM : 2 * HEAD_DIM]
            units.append((key, flipped[0:HEAD_DIM], flipped[2 * HEAD_DIM :]))
    totals = [None, None]
    scores = [dot(key, query) * (HEAD_DIM**-0.5) for key, query, _ in units]
    for unit, score in enumerate(scores):
        powers = jnp.exp(score - jnp.max(score, axis=0, keepdims=True))
        probs = powers * (1.0 / jnp.sum(powers, axis=0, keepdims=True))
        if probs_out is not None:
            probs_out[unit] = probs
        mixed = dot(units[unit][2], probs.astype(BF16)).astype(BF16)
        head = unit // 2
        term = dot(output_turned[:, head * HEAD_DIM : (head + 1) * HEAD_DIM], mixed)
        before = totals[unit % 2]
        totals[unit % 2] = term if before is None else before + term
    whole = jnp.concatenate(totals, axis=0).T
    velocity[...] = whole
    if crossing is not None:
        crossing[...] = pltpu.roll(whole, CHANNELS, 1)


def second_pass_kernel(
    block,
    taken,
    rows,
    turned,
    scale,
    lines_in,
    output_turned,
    matrices,
    offsets,
    keys_turned,
    probs,
    velocity,
    crossing,
    stacked,
):
    chips = taken.shape[0]
    half = block // 2
    low_lanes = lane_index((half, 128)) < CHANNELS
    lines = [[], []]
    for chip in range(chips):
        piece = taken[chip].astype(F32)
        at = chip * block
        folded = piece[block : block + half]
        moved = pltpu.roll(folded, CHANNELS, 1)
        stacked[at : at + half, :] = jnp.where(low_lanes, piece[0:half], moved)
        stacked[at + half : at + block, :] = jnp.where(low_lanes, piece[half:block], folded)
        for which in range(2):
            line = piece[block + half + which : block + half + which + 1]
            lines[which].append((line + pltpu.roll(line, CHANNELS, 1))[:, 0:block])
    joined = [jnp.concatenate(line, axis=1) for line in lines]
    offsets[...] = jnp.concatenate(joined + [jnp.zeros((6, offsets.shape[1]), F32)], axis=0)
    matrices[...] = stacked[...].astype(BF16)
    forward(
        1,
        rows,
        turned,
        scale,
        lines_in,
        matrices[...],
        offsets,
        output_turned,
        keys_turned,
        probs,
        velocity,
        crossing,
    )


def first_pass_kernel(
    block,
    taken,
    matrices,
    offsets,
    here,
    there,
    rows_b,
    scale_b,
    lines,
    output_turned,
    after,
    velocity,
    kept,
    stacked,
    rows,
    turned,
    scale,
    lines_a,
):
    fill_rows(0, (here, there), rows, turned, scale, lines_a)
    for chip in range(taken.shape[0]):
        stacked[chip * block : (chip + 1) * block, :] = taken[chip].astype(F32)[0:block]
    forward(
        0,
        rows,
        turned,
        scale,
        lines_a,
        stacked[...].astype(BF16),
        offsets,
        output_turned,
        None,
        None,
        velocity,
        None,
    )
    inputs = rows_b[...]
    tokens = inputs.shape[0] // 2
    for head in range(output_turned.shape[1] // HEAD_DIM):
        for place, part in enumerate((0, 2)):
            at = (3 * head + part) * HEAD_DIM
            to = (2 * head + place) * HEAD_DIM
            product = dot(inputs, matrices[at : at + HEAD_DIM, :], NT)
            line = offsets[1:2, at : at + HEAD_DIM]
            for sample in range(2):
                own = slice(sample * tokens, (sample + 1) * tokens)
                value = product[own] * scale_b[own, :] + line * sample_level(lines, sample)
                kept[sample, :, to : to + HEAD_DIM] = value.astype(BF16)


def swap_tokens(value):
    half = value.shape[0] // 2
    return jnp.concatenate([value[half:], value[:half]], axis=0)


def backward_kernel(
    block,
    kept,
    scaled,
    rows,
    keys_turned,
    probs_turned,
    lines,
    known,
    vel_here,
    vel_there,
    output_turned,
    vel_a,
    out,
    first,
    crossing,
    gathered,
    summed,
):
    critic = on_critic()
    first[...] = vel_a[...]
    crossing[...] = pltpu.roll(vel_a[...], CHANNELS, 1)
    heads = output_turned.shape[1] // HEAD_DIM
    velocity = vel_here[...] + swap_tokens(vel_there[...].astype(F32))
    level_rows = []
    for sample in range(2):
        tokens = lines.shape[1] // 2
        level = lines[1:2, sample * tokens : (sample + 1) * tokens]
        high = rounded(level)
        level_rows.append(jnp.concatenate([high, level - high, jnp.zeros((14, tokens), F32)], axis=0).astype(BF16))
    known = known[...]
    grad_velocity = jnp.where(critic, velocity - known, known)
    grads_turned = grad_velocity.T.astype(BF16)
    grads = grad_velocity.astype(BF16)
    grad_mixed, grad_probs = [], []
    for unit in range(2 * heads):
        head, sample = unit // 2, unit % 2
        weight = output_turned[:, head * HEAD_DIM : (head + 1) * HEAD_DIM]
        lanes = slice(sample * CHANNELS, (sample + 1) * CHANNELS)
        grad_mixed.append(dot(grads[:, lanes], weight).astype(BF16))
        turned = dot(weight, grads_turned[lanes], TN).astype(BF16)
        value = kept[sample, :, (2 * head + 1) * HEAD_DIM : (2 * head + 2) * HEAD_DIM]
        grad_probs.append(dot(value, turned))
    columns = heads * 3 * HEAD_DIM
    gathered[columns:, :] = jnp.zeros((gathered.shape[0] - columns, 128), F32)
    height = out.shape[1]
    half = block // 2
    row = row_index((height, 128))
    low_lanes = lane_index((height, 128)) < CHANNELS
    pad = jnp.zeros((1, 128 - block), F32) if block < 128 else None
    for head in range(heads):
        at = head * 3 * HEAD_DIM
        query_total, rest_total = None, None
        ends = []
        for sample in range(2):
            unit = 2 * head + sample
            probs = probs_turned[unit]
            grad = grad_probs[unit]
            inner = jnp.sum(grad * probs, axis=0, keepdims=True)
            grad_scores = (probs * (grad - inner) * (HEAD_DIM**-0.5)).astype(BF16)
            grad_value = dot(probs.astype(BF16), grad_mixed[unit])
            grad_key = dot(grad_scores, kept[sample, :, 2 * head * HEAD_DIM : (2 * head + 1) * HEAD_DIM])
            grad_query = dot(keys_turned[unit], grad_scores).astype(BF16)
            rest = jnp.concatenate([grad_key, grad_value], axis=1).astype(BF16)
            query_term = dot(grad_query, scaled[sample])
            rest_term = dot(jnp.concatenate([rows[sample], level_rows[sample]], axis=0), rest)
            query_total = query_term if query_total is None else query_total + query_term
            rest_total = rest_term if rest_total is None else rest_total + rest_term
            ends.append(dot(level_rows[sample], grad_query, NT))
        ends = jnp.concatenate([ends[0] + ends[1], rest_total[128:]], axis=1)
        gathered[at : at + HEAD_DIM, :] = query_total
        gathered[at + HEAD_DIM : at + 3 * HEAD_DIM, :] = rest_total[0:128].T
        summed[:, at : at + 3 * HEAD_DIM] = ends[0:1] + ends[1:2]
        start = columns * head // heads // block
        stop = columns * (head + 1) // heads // block
        for chip in range(start, stop):
            base = chip * block
            piece = jnp.where(low_lanes, gathered[base : base + height, :], gathered[base + half : base + half + height, :])
            line = summed[:, base : base + block]
            high = rounded(line)
            pair = [high, line - high]
            if pad is not None:
                pair = [jnp.concatenate([part, pad], axis=1) for part in pair]
            tail = jnp.where(row == half, pair[0], jnp.where(row == half + 1, pair[1], 0.0))
            out[chip] = jnp.where(row < half, piece, tail).astype(BF16)


def closing_kernel(block, factor, taken, weight, embed, after, kept, sent):
    second = on_second_core()
    total = taken[0].astype(F32)
    for chip in range(1, taken.shape[0]):
        total = total + taken[chip].astype(F32)
    half = block // 2
    height = total.shape[0]
    row = row_index((height, 128))
    ends = total[half : half + 1] + total[half + 1 : half + 2]
    lines = [jnp.where(row < half, total, 0.0), jnp.zeros((128 - height, 128), F32)]
    turned = jnp.concatenate(lines, axis=0).T
    products = turned[0:CHANNELS] + pltpu.roll(turned[CHANNELS:], half, 1)
    joined = jnp.concatenate([products, ends, jnp.zeros((7, 128), F32)], axis=0)[:, 0 : weight.shape[0]]
    high = joined.astype(BF16)
    low = (joined - high.astype(F32)).astype(BF16)
    middle = embed.shape[1] // 2
    step = middle // 3
    parts = []
    for start in range(0, 2 * middle, step):
        columns = weight[:, start : start + step]
        product = dot(high, columns) + dot(low, columns)
        scale = jnp.sum(product[:CHANNELS] * embed[:, start : start + step].astype(F32), axis=0, keepdims=True)
        parts.append(jnp.concatenate([scale, product[CHANNELS : CHANNELS + 1]], axis=0) * factor)
    sides = []
    for side in (parts[:3], parts[3:]):
        lines = [part[which : which + 1, i : i + 128] for which in range(2) for part in side for i in range(0, step, 128)]
        sides.append(jnp.concatenate(lines, axis=0))
    kept[...] = jnp.where(second, sides[1], sides[0])
    sent[...] = jnp.where(second, sides[0], sides[1])


def payload_kernel(noise_levels, own, a_here, b_here, there, out):
    tokens = own.shape[0]
    own_a = a_here[0:tokens, 0:CHANNELS] + there[:, 0:CHANNELS]
    own_b = b_here[0:tokens, 0:CHANNELS] + there[:, CHANNELS:]
    sample = own[:, 0:CHANNELS].astype(F32) - noise_levels[0, 0] * own_a
    out[...] = jnp.where(on_critic(), own_b - own_a, sample).T.astype(BF16)


def spread_kernel(total, other, out):
    line = (total[...] + other[...]).astype(BF16)
    for chip in range(out.shape[0]):
        out[chip] = line


def join_kernel(total, near, crossed, out, crossed_out):
    crossed_out[...] = crossed[...]
    second = on_second_core()
    count = total.shape[0] // 2
    left = jnp.where(second, near[...], total[...])
    right = jnp.where(second, total[...], near[...])
    for which in range(2):
        for side, half in enumerate((left, right)):
            for i in range(count):
                at = (side * count + i) * 128
                out[which : which + 1, at : at + 128] = half[which * count + i : which * count + i + 1, :]


def call(kernel, out_shapes, inputs, scalars=0, scratch=(), flops=0, after=()):
    specs = [pl.BlockSpec(memory_space=pltpu.SMEM)] * scalars
    specs += [pl.BlockSpec(memory_space=pltpu.VMEM)] * (len(inputs) - scalars)
    specs += [pl.BlockSpec(memory_space=pl.ANY)] * len(after)
    return pl.pallas_call(
        kernel,
        out_shape=out_shapes,
        in_specs=specs,
        out_specs=jax.tree.map(lambda _: pl.BlockSpec(memory_space=pltpu.VMEM), out_shapes),
        scratch_shapes=list(scratch),
        compiler_params=pltpu.CompilerParams(vmem_limit_bytes=28 * 2**20),
        cost_estimate=pl.CostEstimate(flops=flops, bytes_accessed=0, transcendentals=0),
    )(*inputs, *after)


def struct(shape, dtype):
    return jax.ShapeDtypeStruct(shape, dtype)


def other_core(value):
    return lax.ppermute(value, "fsdp", [(i, i ^ 1) for i in range(lax.axis_size("fsdp"))])


def other_half(value):
    return lax.ppermute(value, "seq", [(0, 1), (1, 0)])


def between_chips(value):
    count = lax.axis_size("fsdp")
    groups = [list(range(core, count, 2)) for core in range(2)]
    return lax.all_to_all(value, "fsdp", 0, 0, tiled=True, axis_index_groups=groups)


def per_device(
    base_latents,
    noise_latents,
    noise_levels,
    replay_latents,
    replay_levels,
    cotangent,
    embed_weight,
    qkv_weight,
    output_weight,
    modulation,
):
    second_core = on_second_core()
    devices = lax.axis_size("fsdp")
    chips = devices // 2
    embed = embed_weight[0]
    weight = qkv_weight[0]
    width = embed.shape[1]
    columns = weight.shape[1] // 2
    block = columns // chips
    height = block - 4
    packed = round_up(block + block // 2 + 2, 8)
    folded = round_up(block // 2 + 2, 8)
    padded = round_up(2 * weight.shape[0], 128)
    tokens = base_latents.shape[2]
    heads = columns // (3 * HEAD_DIM)
    out_columns = output_weight.shape[1] // 2
    output_turned = output_weight[0].T
    output_turned = jnp.where(second_core, output_turned[:, out_columns:], output_turned[:, :out_columns])

    received = other_core(weight)
    own_turned = call(own_rows_kernel, struct((columns, padded), F32), (weight,))
    turned = call(
        functools.partial(weight_kernel, chips),
        struct((chips, height, padded), BF16),
        (own_turned, received),
        scratch=[pltpu.VMEM((columns, padded), F32)],
    )
    taken = between_chips(turned)
    stack = call(stack_kernel, struct((256, width), BF16), (embed, modulation[0]), after=(turned,))

    own = call(
        pack_kernel,
        struct((tokens, 384), BF16),
        (
            noise_levels,
            replay_levels,
            base_latents[0, 0],
            noise_latents[0, 0],
            replay_latents[0, 0],
            cotangent[0, 0],
            embed,
        ),
        scalars=2,
        after=(turned,),
    )
    matrices, own_columns = call(
        functools.partial(product_kernel, block),
        (struct((chips, packed, 128), BF16), struct((height + 8, width), BF16)),
        (taken, stack),
        after=(own,),
    )
    here = jnp.stack([own, other_core(own)])
    there = other_half(here)

    rows, rows_turned, scale, lines, known, scaled, scaled_turned = call(
        tokens_kernel,
        (
            struct((4 * tokens, 2 * CHANNELS), BF16),
            struct((2 * CHANNELS, 4 * tokens), BF16),
            struct((4 * tokens, 2 * CHANNELS), F32),
            struct((8, 4 * tokens), F32),
            struct((2 * tokens, 2 * CHANNELS), F32),
            struct((2, 2 * tokens, 2 * CHANNELS), BF16),
            struct((2, 2 * CHANNELS, 2 * tokens), BF16),
        ),
        (here, there),
    )
    taken = between_chips(matrices)
    whole, offsets, keys_turned, probs, vel_b, vel_crossing = call(
        functools.partial(second_pass_kernel, block),
        (
            struct((columns, 2 * CHANNELS), BF16),
            struct((8, columns), F32),
            struct((2 * heads, HEAD_DIM, 2 * tokens), BF16),
            struct((2 * heads, 2 * tokens, 2 * tokens), F32),
            struct((2 * tokens, 2 * CHANNELS), F32),
            struct((2 * tokens, 2 * CHANNELS), F32),
        ),
        (taken, rows, rows_turned, scale, lines, output_turned),
        scratch=[pltpu.VMEM((columns, 2 * CHANNELS), F32)],
    )
    vel_here = vel_b + other_core(vel_crossing)
    vel_there = other_half(vel_here.astype(BF16))
    vel_a, kept = call(
        functools.partial(first_pass_kernel, block),
        (struct((2 * tokens, 2 * CHANNELS), F32), struct((2, 2 * tokens, 2 * heads * HEAD_DIM), BF16)),
        (taken, whole, offsets, here, there, rows, scale, lines, output_turned),
        scratch=[
            pltpu.VMEM((columns, 2 * CHANNELS), F32),
            pltpu.VMEM((4 * tokens, 2 * CHANNELS), BF16),
            pltpu.VMEM((2 * CHANNELS, 4 * tokens), BF16),
            pltpu.VMEM((4 * tokens, 2 * CHANNELS), F32),
            pltpu.VMEM((8, 4 * tokens), F32),
        ],
        flops=4 * 10**9,
        after=(vel_here,),
    )
    products, vel_a, vel_crossing = call(
        functools.partial(backward_kernel, block),
        (
            struct((chips, folded, 128), BF16),
            struct((2 * tokens, 2 * CHANNELS), F32),
            struct((2 * tokens, 2 * CHANNELS), F32),
        ),
        (kept, scaled, scaled_turned, keys_turned, probs, lines, known, vel_here, vel_there, output_turned, vel_a),
        scratch=[pltpu.VMEM((columns + 2 * folded, 128), F32), pltpu.VMEM((1, columns), F32)],
    )

    vel_a_here = vel_a + other_core(vel_crossing)
    both_there = other_half(jnp.concatenate([vel_a_here[tokens:, :CHANNELS], vel_here[tokens:, :CHANNELS]], axis=1))
    payload = call(
        payload_kernel,
        struct((CHANNELS, tokens), BF16),
        (noise_levels, own, vel_a_here, vel_here, both_there),
        scalars=1,
    )
    crossed = lax.ppermute(payload, "role", [(0, 1), (1, 0)])

    samples = devices * base_latents.shape[1]
    height = width // 128
    kept_half, sent_half = call(
        functools.partial(closing_kernel, block, 1.0 / (samples * 2 * tokens)),
        (struct((height, 128), F32), struct((height, 128), F32)),
        (between_chips(products), own_columns, embed),
        after=(payload,),
    )
    total = kept_half + other_core(sent_half)
    spread = call(spread_kernel, struct((chips, height, 128), BF16), (total, other_half(total)))
    total = jnp.sum(between_chips(spread).astype(F32), axis=0)
    mod_grads, crossed = call(
        join_kernel,
        (struct((2, width), F32), struct(crossed.shape, BF16)),
        (total, other_core(total), crossed),
    )
    return (crossed.T[None, None], mod_grads[None])


def solution(mesh):
    return jax.shard_map(
        per_device,
        mesh=mesh,
        in_specs=(
            P("role", "fsdp", "seq", None),
            P("role", "fsdp", "seq", None),
            P("role", "fsdp"),
            P("role", "fsdp", "seq", None),
            P("role", "fsdp"),
            P("role", "fsdp", "seq", None),
            P("role", None, None),
            P("role", "fsdp", "seq"),
            P("role", "seq", None),
            P("role", None, None, None),
        ),
        out_specs=(P("role", "fsdp", "seq", None), P("role", None, None)),
        check_vma=False,
    )
```

```python
import functools

import jax
import jax.numpy as jnp
from jax import lax
from jax.experimental import pallas as pl
from jax.experimental.pallas import tpu as pltpu
from jax.sharding import PartitionSpec as P

HEAD_DIM = 128
CHANNELS = 64
EPSILON = 1e-06
F32 = jnp.float32
BF16 = jnp.bfloat16
NT = (((1,), (1,)), ((), ()))
NN = (((1,), (0,)), ((), ()))
TN = (((0,), (0,)), ((), ()))


def dot(a, b, dims=NN):
    return lax.dot_general(a, b, dims, preferred_element_type=F32)


def round_up(value, step):
    return (value + step - 1) // step * step


def rounded(value):
    return value.astype(BF16).astype(F32)


def three_parts(value):
    high = rounded(value)
    middle = rounded(value - high)
    return high, middle, rounded(value - high - middle)


def lane_index(shape):
    return lax.broadcasted_iota(jnp.int32, shape, len(shape) - 1)


def row_index(shape):
    return lax.broadcasted_iota(jnp.int32, shape, len(shape) - 2)


def on_second_core():
    return lax.rem(lax.axis_index("fsdp"), 2) == 1


def on_critic():
    return lax.axis_index("role") == 1


def stack_kernel(embed, modulation, after, stack):
    modulation_a = modulation[0]
    modulation_b = jnp.where(on_critic(), modulation[1], modulation_a)
    embed_f = embed[...].astype(F32)
    stack[0:64, :] = embed[...]
    stack[64:128, :] = (embed_f * modulation_a[0:1, :]).astype(BF16)
    stack[128:192, :] = (embed_f * modulation_b[0:1, :]).astype(BF16)
    shifts = []
    for pair in (modulation_a, modulation_b):
        shift = pair[1:2, :]
        high = rounded(shift)
        shifts += [high, shift - high]
    shifts.append(jnp.zeros((60, embed.shape[1]), F32))
    stack[192:256, :] = jnp.concatenate(shifts, axis=0).astype(BF16)


def pack_kernel(noise_levels, replay_levels, base, noise, replay, cotangent, embed, after, pack):
    critic = on_critic()
    level = noise_levels[0, 0]
    level_two = jnp.where(critic, level, replay_levels[0, 0])
    base_f = base[...].astype(F32)
    noise_f = noise[...].astype(F32)
    input_a = rounded((1.0 - level) * base_f + level * noise_f)
    input_b = jnp.where(critic, input_a, replay[...].astype(F32))
    known = jnp.where(critic, noise_f - base_f, cotangent[...].astype(F32))
    known_high = rounded(known)
    tokens = input_a.shape[0]
    rows = jnp.concatenate([input_a, input_b], axis=0).astype(BF16)
    total = jnp.zeros((2 * tokens, 1), F32)
    width = embed.shape[1]
    for start in range(0, width, 512):
        embedded = dot(rows, embed[:, start : start + 512])
        total = total + jnp.sum(embedded * embedded, axis=-1, keepdims=True)
    scale = lax.rsqrt(total / width + EPSILON)
    lane = lane_index((tokens, 128))
    tail = jnp.zeros((tokens, 128), F32)
    ones = jnp.ones((tokens, 1), F32)
    for which, column in enumerate((scale[:tokens], scale[tokens:], ones * level, ones * level_two)):
        for part, value in enumerate(three_parts(column)):
            tail = jnp.where(lane == which * 3 + part, value, tail)
    pack[:, 0:64] = input_a.astype(BF16)
    pack[:, 64:128] = input_b.astype(BF16)
    pack[:, 128:192] = known_high.astype(BF16)
    pack[:, 192:256] = (known - known_high).astype(BF16)
    pack[:, 256:384] = tail.astype(BF16)


def turn_rows(rows, padded, second):
    count, columns = rows.shape
    empty = jnp.zeros((count, columns), F32)
    parts = [jnp.where(second, empty, rows), jnp.where(second, rows, empty)]
    if padded > 2 * count:
        parts.append(jnp.zeros((padded - 2 * count, columns), F32))
    return jnp.concatenate(parts, axis=0).T


def half_columns(weight, second):
    columns = weight.shape[1] // 2
    start = pl.multiple_of(jnp.where(second, columns, 0), 128)
    return weight[:, pl.ds(start, columns)].astype(F32)


def own_rows_kernel(weight, out):
    second = on_second_core()
    out[...] = turn_rows(half_columns(weight, second), out.shape[1], second)


def weight_kernel(chips, own, received, out, turned):
    second = on_second_core()
    columns, padded = own.shape
    turned[0:columns, :] = own[...] + turn_rows(half_columns(received, second), padded, jnp.logical_not(second))
    block = columns // chips
    height = out.shape[1]
    spare = padded // 4
    upper_lanes = lane_index((16, padded)) >= padded - spare
    for chip in range(chips):
        piece = turned[chip * block : chip * block + height, :]
        last = turned[chip * block + height : (chip + 1) * block, :]
        lines = [pltpu.roll(last, padded - spare * (part + 1), 1) for part in range(3)]
        lines.append(jnp.zeros_like(last))
        top = jnp.where(upper_lanes, jnp.concatenate(lines, axis=0), piece[0:16])
        out[chip] = jnp.concatenate([top, piece[16:]], axis=0).astype(BF16)


def product_kernel(block, taken, stack, after, out, columns_out):
    chips, height, padded = taken.shape
    half = block // 2
    width = stack.shape[1]
    depth = width // chips
    group = 128 // (depth & -depth)
    spare = padded - depth
    lane = lane_index((4, padded))
    for start in range(0, chips, group):
        mains, lasts = [], []
        for chip in range(start, start + group):
            piece = taken[chip].astype(F32)
            mains.append(piece[:, 0:depth])
            top, next_top = piece[0:8], piece[8:16]
            low = pltpu.roll(top, spare, 1)[0:4]
            middle = pltpu.roll(top, 2 * spare, 1)[4:8]
            high = pltpu.roll(next_top, 3 * spare, 1)[0:4]
            lasts.append(jnp.where(lane < spare, low, jnp.where(lane < 2 * spare, middle, high))[:, 0:depth])
        last = jnp.concatenate(lasts, axis=1)
        joined = jnp.concatenate([jnp.concatenate(mains, axis=1), last, jnp.zeros_like(last)], axis=0)
        span = slice(start * depth, (start + group) * depth)
        columns_out[:, span] = joined.astype(BF16)
    weight = columns_out[...]
    products = dot(weight, stack[...], NT)
    first, second = products[:, 0:128], products[:, 128:256]
    tall = jnp.concatenate([second, jnp.zeros((128 - second.shape[0], 128), F32)], axis=0).T
    lines = []
    gap = jnp.zeros((1, CHANNELS - block), F32)
    for at in (CHANNELS, CHANNELS + 2):
        offset = tall[at : at + 1, 0:block] + tall[at + 1 : at + 2, 0:block]
        high = rounded(offset)
        lines.append(jnp.concatenate([high, gap, offset - high, gap], axis=1))
    low_lanes = lane_index((half, 128)) < CHANNELS
    folded = jnp.where(low_lanes, second[0:half], pltpu.roll(second, CHANNELS, 1)[half:block])
    spare = out.shape[1] - block - half - 2
    parts = [first[0:block], folded] + lines
    if spare:
        parts.append(jnp.zeros((spare, 128), F32))
    whole = jnp.concatenate(parts, axis=0).astype(BF16)
    for chip in range(chips):
        out[chip] = whole


def token_rows(packs, sample, start, stop):
    return jnp.concatenate([pack[sample, :, start:stop] for pack in packs], axis=0)


def tail_column(packs, sample, which):
    tail = token_rows(packs, sample, 256, 384).astype(F32)
    at = 3 * which
    return tail[:, at : at + 1] + tail[:, at + 1 : at + 2] + tail[:, at + 2 : at + 3]


def fill_rows(which, packs, rows, turned, scale, lines):
    low_lanes = lane_index((1, 128)) < CHANNELS
    lines[...] = jnp.zeros_like(lines)
    for sample in range(2):
        inputs = token_rows(packs, sample, 0, 128).astype(F32)
        tokens = inputs.shape[0]
        own = slice(sample * tokens, (sample + 1) * tokens)
        flipped = pltpu.roll(inputs, CHANNELS, 1)
        level = jnp.broadcast_to(tail_column(packs, sample, 2 + which), inputs.shape)
        norm = jnp.broadcast_to(tail_column(packs, sample, which), inputs.shape)
        plain, scaled_part = (flipped, inputs) if which else (inputs, flipped)
        both = jnp.where(low_lanes, plain, scaled_part * level)
        rows[own, :] = both.astype(BF16)
        turned[:, own] = both.T.astype(BF16)
        scale[own, :] = norm
        lines[0:1, own] = norm.T[0:1]
        lines[1:2, own] = level.T[0:1]


def tokens_kernel(here, there, rows, turned, scale, lines, known, scaled, scaled_turned):
    packs = (here, there)
    fill_rows(1, packs, rows, turned, scale, lines)
    low_lanes = lane_index((1, 128)) < CHANNELS
    parts = []
    for sample in range(2):
        inputs = token_rows(packs, sample, 0, 128).astype(F32)
        whole = jnp.where(low_lanes, pltpu.roll(inputs, CHANNELS, 1), inputs)
        whole = whole * (tail_column(packs, sample, 1) * tail_column(packs, sample, 3))
        scaled[sample] = whole.astype(BF16)
        scaled_turned[sample] = whole.T.astype(BF16)
        part = token_rows(packs, sample, 128, 256).astype(F32)
        parts.append(part[:, 0:CHANNELS] + part[:, CHANNELS:])
    known[...] = jnp.concatenate(parts, axis=1)


def sample_level(lines, sample):
    at = sample * (lines.shape[1] // 2)
    return lines[1:2, at : at + 1]


def forward(which, rows, turned, scale, lines, matrices, offsets, output_turned, keys_out, probs_out, velocity, crossing):
    heads = output_turned.shape[1] // HEAD_DIM
    tokens = rows.shape[0] // 2
    inputs = rows[...]
    inputs_turned = turned[...]
    levels = [sample_level(lines, sample) for sample in range(2)]
    offset = offsets[which : which + 1, :]
    offset_turned = jnp.broadcast_to(offset, (128, offset.shape[1])).T[:, 0:1]
    units = []
    for head in range(heads):
        at = head * 3 * HEAD_DIM
        span = slice(at, at + 3 * HEAD_DIM)
        matrix = matrices[span, :]
        product = dot(inputs, matrix[HEAD_DIM : 2 * HEAD_DIM], NT)
        product_turned = dot(matrix, inputs_turned)
        line = offset[:, at + HEAD_DIM : at + 2 * HEAD_DIM]
        for sample in range(2):
            own = slice(sample * tokens, (sample + 1) * tokens)
            key = (product[own] * scale[own, :] + line * levels[sample]).astype(BF16)
            norms = lines[0:1, own]
            flipped = product_turned[:, own] * norms + offset_turned[span] * levels[sample]
            flipped = flipped.astype(BF16)
            if keys_out is not None:
                keys_out[2 * head + sample] = flipped[HEAD_DIM : 2 * HEAD_DIM]
            units.append((key, flipped[0:HEAD_DIM], flipped[2 * HEAD_DIM :]))
    totals = [None, None]
    scores = [dot(key, query) * (HEAD_DIM**-0.5) for key, query, _ in units]
    for unit, score in enumerate(scores):
        powers = jnp.exp(score - jnp.max(score, axis=0, keepdims=True))
        probs = powers * (1.0 / jnp.sum(powers, axis=0, keepdims=True))
        if probs_out is not None:
            probs_out[unit] = probs
        mixed = dot(units[unit][2], probs.astype(BF16)).astype(BF16)
        head = unit // 2
        term = dot(output_turned[:, head * HEAD_DIM : (head + 1) * HEAD_DIM], mixed)
        before = totals[unit % 2]
        totals[unit % 2] = term if before is None else before + term
    whole = jnp.concatenate(totals, axis=0).T
    velocity[...] = whole
    if crossing is not None:
        crossing[...] = pltpu.roll(whole, CHANNELS, 1)


def second_pass_kernel(
    block,
    taken,
    rows,
    turned,
    scale,
    lines_in,
    output_turned,
    matrices,
    offsets,
    keys_turned,
    probs,
    velocity,
    crossing,
    stacked,
):
    chips = taken.shape[0]
    half = block // 2
    low_lanes = lane_index((half, 128)) < CHANNELS
    lines = [[], []]
    for chip in range(chips):
        piece = taken[chip].astype(F32)
        at = chip * block
        folded = piece[block : block + half]
        moved = pltpu.roll(folded, CHANNELS, 1)
        stacked[at : at + half, :] = jnp.where(low_lanes, piece[0:half], moved)
        stacked[at + half : at + block, :] = jnp.where(low_lanes, piece[half:block], folded)
        for which in range(2):
            line = piece[block + half + which : block + half + which + 1]
            lines[which].append((line + pltpu.roll(line, CHANNELS, 1))[:, 0:block])
    joined = [jnp.concatenate(line, axis=1) for line in lines]
    offsets[...] = jnp.concatenate(joined + [jnp.zeros((6, offsets.shape[1]), F32)], axis=0)
    matrices[...] = stacked[...].astype(BF16)
    forward(
        1,
        rows,
        turned,
        scale,
        lines_in,
        matrices[...],
        offsets,
        output_turned,
        keys_turned,
        probs,
        velocity,
        crossing,
    )


def first_pass_kernel(
    block,
    taken,
    matrices,
    offsets,
    here,
    there,
    rows_b,
    scale_b,
    lines,
    output_turned,
    after,
    velocity,
    kept,
    stacked,
    rows,
    turned,
    scale,
    lines_a,
):
    fill_rows(0, (here, there), rows, turned, scale, lines_a)
    for chip in range(taken.shape[0]):
        stacked[chip * block : (chip + 1) * block, :] = taken[chip].astype(F32)[0:block]
    forward(
        0,
        rows,
        turned,
        scale,
        lines_a,
        stacked[...].astype(BF16),
        offsets,
        output_turned,
        None,
        None,
        velocity,
        None,
    )
    inputs = rows_b[...]
    tokens = inputs.shape[0] // 2
    for head in range(output_turned.shape[1] // HEAD_DIM):
        for place, part in enumerate((0, 2)):
            at = (3 * head + part) * HEAD_DIM
            to = (2 * head + place) * HEAD_DIM
            product = dot(inputs, matrices[at : at + HEAD_DIM, :], NT)
            line = offsets[1:2, at : at + HEAD_DIM]
            for sample in range(2):
                own = slice(sample * tokens, (sample + 1) * tokens)
                value = product[own] * scale_b[own, :] + line * sample_level(lines, sample)
                kept[sample, :, to : to + HEAD_DIM] = value.astype(BF16)


def swap_tokens(value):
    half = value.shape[0] // 2
    return jnp.concatenate([value[half:], value[:half]], axis=0)


def backward_kernel(
    block,
    kept,
    scaled,
    rows,
    keys_turned,
    probs_turned,
    lines,
    known,
    vel_here,
    vel_there,
    output_turned,
    vel_a,
    out,
    first,
    crossing,
    gathered,
    summed,
):
    critic = on_critic()
    first[...] = vel_a[...]
    crossing[...] = pltpu.roll(vel_a[...], CHANNELS, 1)
    heads = output_turned.shape[1] // HEAD_DIM
    velocity = vel_here[...] + swap_tokens(vel_there[...].astype(F32))
    level_rows = []
    for sample in range(2):
        tokens = lines.shape[1] // 2
        level = lines[1:2, sample * tokens : (sample + 1) * tokens]
        high = rounded(level)
        level_rows.append(jnp.concatenate([high, level - high, jnp.zeros((14, tokens), F32)], axis=0).astype(BF16))
    known = known[...]
    grad_velocity = jnp.where(critic, velocity - known, known)
    grads_turned = grad_velocity.T.astype(BF16)
    grads = grad_velocity.astype(BF16)
    grad_mixed, grad_probs = [], []
    for unit in range(2 * heads):
        head, sample = unit // 2, unit % 2
        weight = output_turned[:, head * HEAD_DIM : (head + 1) * HEAD_DIM]
        lanes = slice(sample * CHANNELS, (sample + 1) * CHANNELS)
        grad_mixed.append(dot(grads[:, lanes], weight).astype(BF16))
        turned = dot(weight, grads_turned[lanes], TN).astype(BF16)
        value = kept[sample, :, (2 * head + 1) * HEAD_DIM : (2 * head + 2) * HEAD_DIM]
        grad_probs.append(dot(value, turned))
    columns = heads * 3 * HEAD_DIM
    gathered[columns:, :] = jnp.zeros((gathered.shape[0] - columns, 128), F32)
    height = out.shape[1]
    half = block // 2
    row = row_index((height, 128))
    low_lanes = lane_index((height, 128)) < CHANNELS
    pad = jnp.zeros((1, 128 - block), F32) if block < 128 else None
    for head in range(heads):
        at = head * 3 * HEAD_DIM
        query_total, rest_total = None, None
        ends = []
        for sample in range(2):
            unit = 2 * head + sample
            probs = probs_turned[unit]
            grad = grad_probs[unit]
            inner = jnp.sum(grad * probs, axis=0, keepdims=True)
            grad_scores = (probs * (grad - inner) * (HEAD_DIM**-0.5)).astype(BF16)
            grad_value = dot(probs.astype(BF16), grad_mixed[unit])
            grad_key = dot(grad_scores, kept[sample, :, 2 * head * HEAD_DIM : (2 * head + 1) * HEAD_DIM])
            grad_query = dot(keys_turned[unit], grad_scores).astype(BF16)
            rest = jnp.concatenate([grad_key, grad_value], axis=1).astype(BF16)
            query_term = dot(grad_query, scaled[sample])
            rest_term = dot(jnp.concatenate([rows[sample], level_rows[sample]], axis=0), rest)
            query_total = query_term if query_total is None else query_total + query_term
            rest_total = rest_term if rest_total is None else rest_total + rest_term
            ends.append(dot(level_rows[sample], grad_query, NT))
        ends = jnp.concatenate([ends[0] + ends[1], rest_total[128:]], axis=1)
        gathered[at : at + HEAD_DIM, :] = query_total
        gathered[at + HEAD_DIM : at + 3 * HEAD_DIM, :] = rest_total[0:128].T
        summed[:, at : at + 3 * HEAD_DIM] = ends[0:1] + ends[1:2]
        start = columns * head // heads // block
        stop = columns * (head + 1) // heads // block
        for chip in range(start, stop):
            base = chip * block
            piece = jnp.where(low_lanes, gathered[base : base + height, :], gathered[base + half : base + half + height, :])
            line = summed[:, base : base + block]
            high = rounded(line)
            pair = [high, line - high]
            if pad is not None:
                pair = [jnp.concatenate([part, pad], axis=1) for part in pair]
            tail = jnp.where(row == half, pair[0], jnp.where(row == half + 1, pair[1], 0.0))
            out[chip] = jnp.where(row < half, piece, tail).astype(BF16)


def closing_kernel(block, factor, taken, weight, embed, kept, sent):
    second = on_second_core()
    total = taken[0].astype(F32)
    for chip in range(1, taken.shape[0]):
        total = total + taken[chip].astype(F32)
    half = block // 2
    height = total.shape[0]
    row = row_index((height, 128))
    ends = total[half : half + 1] + total[half + 1 : half + 2]
    lines = [jnp.where(row < half, total, 0.0), jnp.zeros((128 - height, 128), F32)]
    turned = jnp.concatenate(lines, axis=0).T
    products = turned[0:CHANNELS] + pltpu.roll(turned[CHANNELS:], half, 1)
    joined = jnp.concatenate([products, ends, jnp.zeros((7, 128), F32)], axis=0)[:, 0 : weight.shape[0]]
    high = joined.astype(BF16)
    low = (joined - high.astype(F32)).astype(BF16)
    middle = embed.shape[1] // 2
    step = middle // 3
    parts = []
    for start in range(0, 2 * middle, step):
        columns = weight[:, start : start + step]
        product = dot(high, columns) + dot(low, columns)
        scale = jnp.sum(product[:CHANNELS] * embed[:, start : start + step].astype(F32), axis=0, keepdims=True)
        parts.append(jnp.concatenate([scale, product[CHANNELS : CHANNELS + 1]], axis=0) * factor)
    sides = []
    for side in (parts[:3], parts[3:]):
        lines = [part[which : which + 1, i : i + 128] for which in range(2) for part in side for i in range(0, step, 128)]
        sides.append(jnp.concatenate(lines, axis=0))
    kept[...] = jnp.where(second, sides[1], sides[0])
    sent[...] = jnp.where(second, sides[0], sides[1])


def payload_kernel(noise_levels, own, vel_a, vel_b, here, there):
    tokens = own.shape[0]
    velocity = vel_a[:, 0:CHANNELS]
    part = jnp.where(on_critic(), vel_b[:, 0:CHANNELS] - velocity, -noise_levels[0, 0] * velocity)
    sample = jnp.where(on_critic(), 0.0, own[:, 0:CHANNELS].astype(F32))
    here[...] = (sample + part[0:tokens]).T
    there[...] = part[tokens:].T


def spread_kernel(total, other, out):
    line = (total[...] + other[...]).astype(BF16)
    for chip in range(out.shape[0]):
        out[chip] = line


def join_kernel(total, near, crossed_here, crossed_there, out, crossed):
    crossed[...] = (crossed_here[...] + crossed_there[...]).astype(BF16)
    second = on_second_core()
    count = total.shape[0] // 2
    left = jnp.where(second, near[...], total[...])
    right = jnp.where(second, total[...], near[...])
    for which in range(2):
        for side, half in enumerate((left, right)):
            for i in range(count):
                at = (side * count + i) * 128
                out[which : which + 1, at : at + 128] = half[which * count + i : which * count + i + 1, :]


def call(kernel, out_shapes, inputs, scalars=0, scratch=(), flops=0, after=()):
    specs = [pl.BlockSpec(memory_space=pltpu.SMEM)] * scalars
    specs += [pl.BlockSpec(memory_space=pltpu.VMEM)] * (len(inputs) - scalars)
    specs += [pl.BlockSpec(memory_space=pl.ANY)] * len(after)
    return pl.pallas_call(
        kernel,
        out_shape=out_shapes,
        in_specs=specs,
        out_specs=jax.tree.map(lambda _: pl.BlockSpec(memory_space=pltpu.VMEM), out_shapes),
        scratch_shapes=list(scratch),
        compiler_params=pltpu.CompilerParams(vmem_limit_bytes=28 * 2**20),
        cost_estimate=pl.CostEstimate(flops=flops, bytes_accessed=0, transcendentals=0),
    )(*inputs, *after)


def struct(shape, dtype):
    return jax.ShapeDtypeStruct(shape, dtype)


def other_core(value):
    return lax.ppermute(value, "fsdp", [(i, i ^ 1) for i in range(lax.axis_size("fsdp"))])


def other_half(value):
    return lax.ppermute(value, "seq", [(0, 1), (1, 0)])


def between_chips(value):
    count = lax.axis_size("fsdp")
    groups = [list(range(core, count, 2)) for core in range(2)]
    return lax.all_to_all(value, "fsdp", 0, 0, tiled=True, axis_index_groups=groups)


def per_device(
    base_latents,
    noise_latents,
    noise_levels,
    replay_latents,
    replay_levels,
    cotangent,
    embed_weight,
    qkv_weight,
    output_weight,
    modulation,
):
    second_core = on_second_core()
    devices = lax.axis_size("fsdp")
    chips = devices // 2
    embed = embed_weight[0]
    weight = qkv_weight[0]
    width = embed.shape[1]
    columns = weight.shape[1] // 2
    block = columns // chips
    height = block - 4
    packed = round_up(block + block // 2 + 2, 8)
    folded = round_up(block // 2 + 2, 8)
    padded = round_up(2 * weight.shape[0], 128)
    tokens = base_latents.shape[2]
    heads = columns // (3 * HEAD_DIM)
    out_columns = output_weight.shape[1] // 2
    output_turned = output_weight[0].T
    output_turned = jnp.where(second_core, output_turned[:, out_columns:], output_turned[:, :out_columns])

    received = other_core(weight)
    own_turned = call(own_rows_kernel, struct((columns, padded), F32), (weight,))
    turned = call(
        functools.partial(weight_kernel, chips),
        struct((chips, height, padded), BF16),
        (own_turned, received),
        scratch=[pltpu.VMEM((columns, padded), F32)],
    )
    taken = between_chips(turned)
    stack = call(stack_kernel, struct((256, width), BF16), (embed, modulation[0]), after=(turned,))

    own = call(
        pack_kernel,
        struct((tokens, 384), BF16),
        (
            noise_levels,
            replay_levels,
            base_latents[0, 0],
            noise_latents[0, 0],
            replay_latents[0, 0],
            cotangent[0, 0],
            embed,
        ),
        scalars=2,
        after=(turned,),
    )
    matrices, own_columns = call(
        functools.partial(product_kernel, block),
        (struct((chips, packed, 128), BF16), struct((height + 8, width), BF16)),
        (taken, stack),
        after=(own,),
    )
    here = jnp.stack([own, other_core(own)])
    there = other_half(here)

    rows, rows_turned, scale, lines, known, scaled, scaled_turned = call(
        tokens_kernel,
        (
            struct((4 * tokens, 2 * CHANNELS), BF16),
            struct((2 * CHANNELS, 4 * tokens), BF16),
            struct((4 * tokens, 2 * CHANNELS), F32),
            struct((8, 4 * tokens), F32),
            struct((2 * tokens, 2 * CHANNELS), F32),
            struct((2, 2 * tokens, 2 * CHANNELS), BF16),
            struct((2, 2 * CHANNELS, 2 * tokens), BF16),
        ),
        (here, there),
    )
    taken = between_chips(matrices)
    whole, offsets, keys_turned, probs, vel_b, vel_crossing = call(
        functools.partial(second_pass_kernel, block),
        (
            struct((columns, 2 * CHANNELS), BF16),
            struct((8, columns), F32),
            struct((2 * heads, HEAD_DIM, 2 * tokens), BF16),
            struct((2 * heads, 2 * tokens, 2 * tokens), F32),
            struct((2 * tokens, 2 * CHANNELS), F32),
            struct((2 * tokens, 2 * CHANNELS), F32),
        ),
        (taken, rows, rows_turned, scale, lines, output_turned),
        scratch=[pltpu.VMEM((columns, 2 * CHANNELS), F32)],
    )
    vel_here = vel_b + other_core(vel_crossing)
    vel_there = other_half(vel_here.astype(BF16))
    vel_a, kept = call(
        functools.partial(first_pass_kernel, block),
        (struct((2 * tokens, 2 * CHANNELS), F32), struct((2, 2 * tokens, 2 * heads * HEAD_DIM), BF16)),
        (taken, whole, offsets, here, there, rows, scale, lines, output_turned),
        scratch=[
            pltpu.VMEM((columns, 2 * CHANNELS), F32),
            pltpu.VMEM((4 * tokens, 2 * CHANNELS), BF16),
            pltpu.VMEM((2 * CHANNELS, 4 * tokens), BF16),
            pltpu.VMEM((4 * tokens, 2 * CHANNELS), F32),
            pltpu.VMEM((8, 4 * tokens), F32),
        ],
        flops=4 * 10**9,
        after=(vel_here,),
    )
    products, vel_a, vel_crossing = call(
        functools.partial(backward_kernel, block),
        (
            struct((chips, folded, 128), BF16),
            struct((2 * tokens, 2 * CHANNELS), F32),
            struct((2 * tokens, 2 * CHANNELS), F32),
        ),
        (kept, scaled, scaled_turned, keys_turned, probs, lines, known, vel_here, vel_there, output_turned, vel_a),
        scratch=[pltpu.VMEM((columns + 2 * folded, 128), F32), pltpu.VMEM((1, columns), F32)],
    )

    vel_a_here = vel_a + other_core(vel_crossing)
    part_here, part_there = call(
        payload_kernel,
        (struct((CHANNELS, tokens), F32), struct((CHANNELS, tokens), F32)),
        (noise_levels, own, vel_a_here, vel_here),
        scalars=1,
    )
    crossed_here = lax.ppermute(part_here, "role", [(0, 1), (1, 0)])
    crossed_there = lax.ppermute(part_there, ("role", "seq"), [(i, i ^ 3) for i in range(4)])

    samples = devices * base_latents.shape[1]
    height = width // 128
    kept_half, sent_half = call(
        functools.partial(closing_kernel, block, 1.0 / (samples * 2 * tokens)),
        (struct((height, 128), F32), struct((height, 128), F32)),
        (between_chips(products), own_columns, embed),
    )
    total = kept_half + other_core(sent_half)
    spread = call(spread_kernel, struct((chips, height, 128), BF16), (total, other_half(total)))
    total = jnp.sum(between_chips(spread).astype(F32), axis=0)
    mod_grads, crossed = call(
        join_kernel,
        (struct((2, width), F32), struct((CHANNELS, tokens), BF16)),
        (total, other_core(total), crossed_here, crossed_there),
    )
    return (crossed.T[None, None], mod_grads[None])


def solution(mesh):
    return jax.shard_map(
        per_device,
        mesh=mesh,
        in_specs=(
            P("role", "fsdp", "seq", None),
            P("role", "fsdp", "seq", None),
            P("role", "fsdp"),
            P("role", "fsdp", "seq", None),
            P("role", "fsdp"),
            P("role", "fsdp", "seq", None),
            P("role", None, None),
            P("role", "fsdp", "seq"),
            P("role", "seq", None),
            P("role", None, None, None),
        ),
        out_specs=(P("role", "fsdp", "seq", None), P("role", None, None)),
        check_vma=False,
    )
```

```python
import functools

import jax
import jax.numpy as jnp
from jax import lax
from jax.experimental import pallas as pl
from jax.experimental.pallas import tpu as pltpu
from jax.sharding import PartitionSpec as P

HEAD_DIM = 128
CHANNELS = 64
EPSILON = 1e-06
F32 = jnp.float32
BF16 = jnp.bfloat16
NT = (((1,), (1,)), ((), ()))
NN = (((1,), (0,)), ((), ()))
TN = (((0,), (0,)), ((), ()))


def dot(a, b, dims=NN):
    return lax.dot_general(a, b, dims, preferred_element_type=F32)


def round_up(value, step):
    return (value + step - 1) // step * step


def rounded(value):
    return value.astype(BF16).astype(F32)


def three_parts(value):
    high = rounded(value)
    middle = rounded(value - high)
    return high, middle, rounded(value - high - middle)


def lane_index(shape):
    return lax.broadcasted_iota(jnp.int32, shape, len(shape) - 1)


def row_index(shape):
    return lax.broadcasted_iota(jnp.int32, shape, len(shape) - 2)


def on_second_core():
    return lax.rem(lax.axis_index("fsdp"), 2) == 1


def on_critic():
    return lax.axis_index("role") == 1


def stack_kernel(embed, modulation, after, stack):
    modulation_a = modulation[0]
    modulation_b = jnp.where(on_critic(), modulation[1], modulation_a)
    embed_f = embed[...].astype(F32)
    stack[0:64, :] = embed[...]
    stack[64:128, :] = (embed_f * modulation_a[0:1, :]).astype(BF16)
    stack[128:192, :] = (embed_f * modulation_b[0:1, :]).astype(BF16)
    shifts = []
    for pair in (modulation_a, modulation_b):
        shift = pair[1:2, :]
        high = rounded(shift)
        shifts += [high, shift - high]
    shifts.append(jnp.zeros((60, embed.shape[1]), F32))
    stack[192:256, :] = jnp.concatenate(shifts, axis=0).astype(BF16)


def pack_kernel(noise_levels, replay_levels, base, noise, replay, cotangent, embed, after, pack):
    critic = on_critic()
    level = noise_levels[0, 0]
    level_two = jnp.where(critic, level, replay_levels[0, 0])
    base_f = base[...].astype(F32).T
    noise_f = noise[...].astype(F32).T
    input_a = rounded((1.0 - level) * base_f + level * noise_f)
    input_b = jnp.where(critic, input_a, replay[...].astype(F32).T)
    known = jnp.where(critic, noise_f - base_f, cotangent[...].astype(F32).T)
    known_high = rounded(known)
    tokens = input_a.shape[0]
    rows = jnp.concatenate([input_a, input_b], axis=0).astype(BF16)
    total = jnp.zeros((2 * tokens, 1), F32)
    width = embed.shape[1]
    for start in range(0, width, 512):
        embedded = dot(rows, embed[:, start : start + 512])
        total = total + jnp.sum(embedded * embedded, axis=-1, keepdims=True)
    scale = lax.rsqrt(total / width + EPSILON)
    lane = lane_index((tokens, CHANNELS))
    tail = jnp.zeros((tokens, CHANNELS), F32)
    ones = jnp.ones((tokens, 1), F32)
    for which, column in enumerate((scale[:tokens], scale[tokens:], ones * level, ones * level_two)):
        for part, value in enumerate(three_parts(column)):
            tail = jnp.where(lane == which * 3 + part, value, tail)
    pack[:, 0:64] = input_a.astype(BF16)
    pack[:, 64:128] = jnp.where(critic, known - known_high, input_b).astype(BF16)
    pack[:, 128:192] = known_high.astype(BF16)
    pack[:, 192:256] = tail.astype(BF16)


def turn_rows(rows, padded, second):
    count, columns = rows.shape
    empty = jnp.zeros((count, columns), F32)
    parts = [jnp.where(second, empty, rows), jnp.where(second, rows, empty)]
    if padded > 2 * count:
        parts.append(jnp.zeros((padded - 2 * count, columns), F32))
    return jnp.concatenate(parts, axis=0).T


def half_columns(weight, second):
    columns = weight.shape[1] // 2
    start = pl.multiple_of(jnp.where(second, columns, 0), 128)
    return weight[:, pl.ds(start, columns)].astype(F32)


def own_rows_kernel(weight, out):
    second = on_second_core()
    out[...] = turn_rows(half_columns(weight, second), out.shape[1], second)


def weight_kernel(chips, own, received, out, turned):
    second = on_second_core()
    columns, padded = own.shape
    turned[0:columns, :] = own[...] + turn_rows(half_columns(received, second), padded, jnp.logical_not(second))
    block = columns // chips
    height = out.shape[1]
    spare = padded // 4
    upper_lanes = lane_index((16, padded)) >= padded - spare
    for chip in range(chips):
        piece = turned[chip * block : chip * block + height, :]
        last = turned[chip * block + height : (chip + 1) * block, :]
        lines = [pltpu.roll(last, padded - spare * (part + 1), 1) for part in range(3)]
        lines.append(jnp.zeros_like(last))
        top = jnp.where(upper_lanes, jnp.concatenate(lines, axis=0), piece[0:16])
        out[chip] = jnp.concatenate([top, piece[16:]], axis=0).astype(BF16)


def product_kernel(block, taken, stack, out, columns_out):
    chips, height, padded = taken.shape
    half = block // 2
    width = stack.shape[1]
    depth = width // chips
    group = 128 // (depth & -depth)
    spare = padded - depth
    lane = lane_index((4, padded))
    for start in range(0, chips, group):
        mains, lasts = [], []
        for chip in range(start, start + group):
            piece = taken[chip].astype(F32)
            mains.append(piece[:, 0:depth])
            top, next_top = piece[0:8], piece[8:16]
            low = pltpu.roll(top, spare, 1)[0:4]
            middle = pltpu.roll(top, 2 * spare, 1)[4:8]
            high = pltpu.roll(next_top, 3 * spare, 1)[0:4]
            lasts.append(jnp.where(lane < spare, low, jnp.where(lane < 2 * spare, middle, high))[:, 0:depth])
        last = jnp.concatenate(lasts, axis=1)
        joined = jnp.concatenate([jnp.concatenate(mains, axis=1), last, jnp.zeros_like(last)], axis=0)
        span = slice(start * depth, (start + group) * depth)
        columns_out[:, span] = joined.astype(BF16)
    weight = columns_out[...]
    products = dot(weight, stack[...], NT)
    first, second = products[:, 0:128], products[:, 128:256]
    tall = jnp.concatenate([second, jnp.zeros((128 - second.shape[0], 128), F32)], axis=0).T
    lines = []
    gap = jnp.zeros((1, CHANNELS - block), F32)
    for at in (CHANNELS, CHANNELS + 2):
        offset = tall[at : at + 1, 0:block] + tall[at + 1 : at + 2, 0:block]
        high = rounded(offset)
        lines.append(jnp.concatenate([high, gap, offset - high, gap], axis=1))
    low_lanes = lane_index((half, 128)) < CHANNELS
    folded = jnp.where(low_lanes, second[0:half], pltpu.roll(second, CHANNELS, 1)[half:block])
    spare = out.shape[1] - block - half - 2
    parts = [first[0:block], folded] + lines
    if spare:
        parts.append(jnp.zeros((spare, 128), F32))
    whole = jnp.concatenate(parts, axis=0).astype(BF16)
    for chip in range(chips):
        out[chip] = whole


def token_rows(packs, sample, start, stop):
    return jnp.concatenate([pack[sample, :, start:stop] for pack in packs], axis=0)


def tail_column(packs, sample, which):
    tail = token_rows(packs, sample, 128, 256).astype(F32)
    at = CHANNELS + 3 * which
    return tail[:, at : at + 1] + tail[:, at + 1 : at + 2] + tail[:, at + 2 : at + 3]


def both_inputs(packs, sample):
    inputs = token_rows(packs, sample, 0, 128).astype(F32)
    low_lanes = lane_index((1, 128)) < CHANNELS
    same = jnp.where(low_lanes, inputs, pltpu.roll(inputs, CHANNELS, 1))
    return jnp.where(on_critic(), same, inputs)


def fill_rows(which, packs, rows, turned, scale, lines):
    low_lanes = lane_index((1, 128)) < CHANNELS
    lines[...] = jnp.zeros_like(lines)
    for sample in range(2):
        inputs = both_inputs(packs, sample)
        tokens = inputs.shape[0]
        own = slice(sample * tokens, (sample + 1) * tokens)
        flipped = pltpu.roll(inputs, CHANNELS, 1)
        level = jnp.broadcast_to(tail_column(packs, sample, 2 + which), inputs.shape)
        norm = jnp.broadcast_to(tail_column(packs, sample, which), inputs.shape)
        plain, scaled_part = (flipped, inputs) if which else (inputs, flipped)
        both = jnp.where(low_lanes, plain, scaled_part * level)
        rows[own, :] = both.astype(BF16)
        turned[:, own] = both.T.astype(BF16)
        scale[own, :] = norm
        lines[0:1, own] = norm.T[0:1]
        lines[1:2, own] = level.T[0:1]


def tokens_kernel(here, there, rows, turned, scale, lines, known, scaled, scaled_turned):
    packs = (here, there)
    fill_rows(1, packs, rows, turned, scale, lines)
    low_lanes = lane_index((1, 128)) < CHANNELS
    parts = []
    for sample in range(2):
        inputs = both_inputs(packs, sample)
        whole = jnp.where(low_lanes, pltpu.roll(inputs, CHANNELS, 1), inputs)
        whole = whole * (tail_column(packs, sample, 1) * tail_column(packs, sample, 3))
        scaled[sample] = whole.astype(BF16)
        scaled_turned[sample] = whole.T.astype(BF16)
        high = token_rows(packs, sample, 128, 256).astype(F32)[:, 0:CHANNELS]
        low = token_rows(packs, sample, 0, 128).astype(F32)[:, CHANNELS:]
        parts.append(high + jnp.where(on_critic(), low, 0.0))
    known[...] = jnp.concatenate(parts, axis=1)


def sample_level(lines, sample):
    at = sample * (lines.shape[1] // 2)
    return lines[1:2, at : at + 1]


def forward(which, rows, turned, scale, lines, matrices, offsets, output_turned, keys_out, probs_out, velocity, crossing):
    heads = output_turned.shape[1] // HEAD_DIM
    tokens = rows.shape[0] // 2
    inputs = rows[...]
    inputs_turned = turned[...]
    levels = [sample_level(lines, sample) for sample in range(2)]
    offset = offsets[which : which + 1, :]
    offset_turned = jnp.broadcast_to(offset, (128, offset.shape[1])).T[:, 0:1]
    units = []
    for head in range(heads):
        at = head * 3 * HEAD_DIM
        span = slice(at, at + 3 * HEAD_DIM)
        matrix = matrices[span, :]
        product = dot(inputs, matrix[HEAD_DIM : 2 * HEAD_DIM], NT)
        product_turned = dot(matrix, inputs_turned)
        line = offset[:, at + HEAD_DIM : at + 2 * HEAD_DIM]
        for sample in range(2):
            own = slice(sample * tokens, (sample + 1) * tokens)
            key = (product[own] * scale[own, :] + line * levels[sample]).astype(BF16)
            norms = lines[0:1, own]
            flipped = product_turned[:, own] * norms + offset_turned[span] * levels[sample]
            flipped = flipped.astype(BF16)
            if keys_out is not None:
                keys_out[2 * head + sample] = flipped[HEAD_DIM : 2 * HEAD_DIM]
            units.append((key, flipped[0:HEAD_DIM], flipped[2 * HEAD_DIM :]))
    totals = [None, None]
    scores = [dot(key, query) * (HEAD_DIM**-0.5) for key, query, _ in units]
    for unit, score in enumerate(scores):
        powers = jnp.exp(score - jnp.max(score, axis=0, keepdims=True))
        probs = powers * (1.0 / jnp.sum(powers, axis=0, keepdims=True))
        if probs_out is not None:
            probs_out[unit] = probs
        mixed = dot(units[unit][2], probs.astype(BF16)).astype(BF16)
        head = unit // 2
        term = dot(output_turned[:, head * HEAD_DIM : (head + 1) * HEAD_DIM], mixed)
        before = totals[unit % 2]
        totals[unit % 2] = term if before is None else before + term
    whole = jnp.concatenate(totals, axis=0).T
    velocity[...] = whole
    if crossing is not None:
        crossing[...] = pltpu.roll(whole, CHANNELS, 1)


def second_pass_kernel(
    block,
    taken,
    rows,
    turned,
    scale,
    lines_in,
    output_turned,
    matrices,
    offsets,
    keys_turned,
    probs,
    velocity,
    crossing,
    stacked,
):
    chips = taken.shape[0]
    half = block // 2
    low_lanes = lane_index((half, 128)) < CHANNELS
    lines = [[], []]
    for chip in range(chips):
        piece = taken[chip].astype(F32)
        at = chip * block
        folded = piece[block : block + half]
        moved = pltpu.roll(folded, CHANNELS, 1)
        stacked[at : at + half, :] = jnp.where(low_lanes, piece[0:half], moved)
        stacked[at + half : at + block, :] = jnp.where(low_lanes, piece[half:block], folded)
        for which in range(2):
            line = piece[block + half + which : block + half + which + 1]
            lines[which].append((line + pltpu.roll(line, CHANNELS, 1))[:, 0:block])
    joined = [jnp.concatenate(line, axis=1) for line in lines]
    offsets[...] = jnp.concatenate(joined + [jnp.zeros((6, offsets.shape[1]), F32)], axis=0)
    matrices[...] = stacked[...].astype(BF16)
    forward(
        1,
        rows,
        turned,
        scale,
        lines_in,
        matrices[...],
        offsets,
        output_turned,
        keys_turned,
        probs,
        velocity,
        crossing,
    )


def first_pass_kernel(
    block,
    taken,
    matrices,
    offsets,
    here,
    there,
    rows_b,
    scale_b,
    lines,
    output_turned,
    after,
    velocity,
    kept,
    stacked,
    rows,
    turned,
    scale,
    lines_a,
):
    fill_rows(0, (here, there), rows, turned, scale, lines_a)
    for chip in range(taken.shape[0]):
        stacked[chip * block : (chip + 1) * block, :] = taken[chip].astype(F32)[0:block]
    forward(
        0,
        rows,
        turned,
        scale,
        lines_a,
        stacked[...].astype(BF16),
        offsets,
        output_turned,
        None,
        None,
        velocity,
        None,
    )
    inputs = rows_b[...]
    tokens = inputs.shape[0] // 2
    for head in range(output_turned.shape[1] // HEAD_DIM):
        for place, part in enumerate((0, 2)):
            at = (3 * head + part) * HEAD_DIM
            to = (2 * head + place) * HEAD_DIM
            product = dot(inputs, matrices[at : at + HEAD_DIM, :], NT)
            line = offsets[1:2, at : at + HEAD_DIM]
            for sample in range(2):
                own = slice(sample * tokens, (sample + 1) * tokens)
                value = product[own] * scale_b[own, :] + line * sample_level(lines, sample)
                kept[sample, :, to : to + HEAD_DIM] = value.astype(BF16)


def swap_tokens(value):
    half = value.shape[0] // 2
    return jnp.concatenate([value[half:], value[:half]], axis=0)


def backward_kernel(
    block,
    kept,
    scaled,
    rows,
    keys_turned,
    probs_turned,
    lines,
    known,
    vel_here,
    vel_there,
    output_turned,
    vel_a,
    out,
    first,
    crossing,
    gathered,
    summed,
):
    critic = on_critic()
    first[...] = vel_a[...]
    crossing[...] = pltpu.roll(vel_a[...], CHANNELS, 1)
    heads = output_turned.shape[1] // HEAD_DIM
    velocity = vel_here[...] + swap_tokens(vel_there[...].astype(F32))
    level_rows = []
    for sample in range(2):
        tokens = lines.shape[1] // 2
        level = lines[1:2, sample * tokens : (sample + 1) * tokens]
        high = rounded(level)
        level_rows.append(jnp.concatenate([high, level - high, jnp.zeros((14, tokens), F32)], axis=0).astype(BF16))
    known = known[...]
    grad_velocity = jnp.where(critic, velocity - known, known)
    grads_turned = grad_velocity.T.astype(BF16)
    grads = grad_velocity.astype(BF16)
    grad_mixed, grad_probs = [], []
    for unit in range(2 * heads):
        head, sample = unit // 2, unit % 2
        weight = output_turned[:, head * HEAD_DIM : (head + 1) * HEAD_DIM]
        lanes = slice(sample * CHANNELS, (sample + 1) * CHANNELS)
        grad_mixed.append(dot(grads[:, lanes], weight).astype(BF16))
        turned = dot(weight, grads_turned[lanes], TN).astype(BF16)
        value = kept[sample, :, (2 * head + 1) * HEAD_DIM : (2 * head + 2) * HEAD_DIM]
        grad_probs.append(dot(value, turned))
    columns = heads * 3 * HEAD_DIM
    gathered[columns:, :] = jnp.zeros((gathered.shape[0] - columns, 128), F32)
    height = out.shape[1]
    half = block // 2
    row = row_index((height, 128))
    low_lanes = lane_index((height, 128)) < CHANNELS
    pad = jnp.zeros((1, 128 - block), F32) if block < 128 else None
    for head in range(heads):
        at = head * 3 * HEAD_DIM
        query_total, rest_total = None, None
        ends = []
        for sample in range(2):
            unit = 2 * head + sample
            probs = probs_turned[unit]
            grad = grad_probs[unit]
            inner = jnp.sum(grad * probs, axis=0, keepdims=True)
            grad_scores = (probs * (grad - inner) * (HEAD_DIM**-0.5)).astype(BF16)
            grad_value = dot(probs.astype(BF16), grad_mixed[unit])
            grad_key = dot(grad_scores, kept[sample, :, 2 * head * HEAD_DIM : (2 * head + 1) * HEAD_DIM])
            grad_query = dot(keys_turned[unit], grad_scores).astype(BF16)
            rest = jnp.concatenate([grad_key, grad_value], axis=1).astype(BF16)
            query_term = dot(grad_query, scaled[sample])
            rest_term = dot(jnp.concatenate([rows[sample], level_rows[sample]], axis=0), rest)
            query_total = query_term if query_total is None else query_total + query_term
            rest_total = rest_term if rest_total is None else rest_total + rest_term
            ends.append(dot(level_rows[sample], grad_query, NT))
        ends = jnp.concatenate([ends[0] + ends[1], rest_total[128:]], axis=1)
        gathered[at : at + HEAD_DIM, :] = query_total
        gathered[at + HEAD_DIM : at + 3 * HEAD_DIM, :] = rest_total[0:128].T
        summed[:, at : at + 3 * HEAD_DIM] = ends[0:1] + ends[1:2]
        start = columns * head // heads // block
        stop = columns * (head + 1) // heads // block
        for chip in range(start, stop):
            base = chip * block
            piece = jnp.where(low_lanes, gathered[base : base + height, :], gathered[base + half : base + half + height, :])
            line = summed[:, base : base + block]
            high = rounded(line)
            pair = [high, line - high]
            if pad is not None:
                pair = [jnp.concatenate([part, pad], axis=1) for part in pair]
            tail = jnp.where(row == half, pair[0], jnp.where(row == half + 1, pair[1], 0.0))
            out[chip] = jnp.where(row < half, piece, tail).astype(BF16)


def closing_kernel(block, factor, taken, weight, embed, kept, sent):
    second = on_second_core()
    total = taken[0].astype(F32)
    for chip in range(1, taken.shape[0]):
        total = total + taken[chip].astype(F32)
    half = block // 2
    height = total.shape[0]
    row = row_index((height, 128))
    ends = total[half : half + 1] + total[half + 1 : half + 2]
    lines = [jnp.where(row < half, total, 0.0), jnp.zeros((128 - height, 128), F32)]
    turned = jnp.concatenate(lines, axis=0).T
    products = turned[0:CHANNELS] + pltpu.roll(turned[CHANNELS:], half, 1)
    joined = jnp.concatenate([products, ends, jnp.zeros((7, 128), F32)], axis=0)[:, 0 : weight.shape[0]]
    high = joined.astype(BF16)
    low = (joined - high.astype(F32)).astype(BF16)
    middle = embed.shape[1] // 2
    step = middle // 3
    parts = []
    for start in range(0, 2 * middle, step):
        columns = weight[:, start : start + step]
        product = dot(high, columns) + dot(low, columns)
        scale = jnp.sum(product[:CHANNELS] * embed[:, start : start + step].astype(F32), axis=0, keepdims=True)
        parts.append(jnp.concatenate([scale, product[CHANNELS : CHANNELS + 1]], axis=0) * factor)
    sides = []
    for side in (parts[:3], parts[3:]):
        lines = [part[which : which + 1, i : i + 128] for which in range(2) for part in side for i in range(0, step, 128)]
        sides.append(jnp.concatenate(lines, axis=0))
    kept[...] = jnp.where(second, sides[1], sides[0])
    sent[...] = jnp.where(second, sides[0], sides[1])


def payload_kernel(noise_levels, own, vel_a, vel_b, here, there):
    tokens = own.shape[0]
    velocity = vel_a[:, 0:CHANNELS]
    part = jnp.where(on_critic(), vel_b[:, 0:CHANNELS] - velocity, -noise_levels[0, 0] * velocity)
    sample = jnp.where(on_critic(), 0.0, own[:, 0:CHANNELS].astype(F32))
    here[...] = (sample + part[0:tokens]).T
    there[...] = part[tokens:].T


def spread_kernel(total, other, out):
    line = (total[...] + other[...]).astype(BF16)
    for chip in range(out.shape[0]):
        out[chip] = line


def join_kernel(total, near, crossed_here, crossed_there, out, crossed):
    crossed[...] = (crossed_here[...] + crossed_there[...]).astype(BF16)
    second = on_second_core()
    count = total.shape[0] // 2
    left = jnp.where(second, near[...], total[...])
    right = jnp.where(second, total[...], near[...])
    for which in range(2):
        for side, half in enumerate((left, right)):
            for i in range(count):
                at = (side * count + i) * 128
                out[which : which + 1, at : at + 128] = half[which * count + i : which * count + i + 1, :]


def call(kernel, out_shapes, inputs, scalars=0, scratch=(), flops=0, after=()):
    specs = [pl.BlockSpec(memory_space=pltpu.SMEM)] * scalars
    specs += [pl.BlockSpec(memory_space=pltpu.VMEM)] * (len(inputs) - scalars)
    specs += [pl.BlockSpec(memory_space=pl.ANY)] * len(after)
    return pl.pallas_call(
        kernel,
        out_shape=out_shapes,
        in_specs=specs,
        out_specs=jax.tree.map(lambda _: pl.BlockSpec(memory_space=pltpu.VMEM), out_shapes),
        scratch_shapes=list(scratch),
        compiler_params=pltpu.CompilerParams(vmem_limit_bytes=28 * 2**20),
        cost_estimate=pl.CostEstimate(flops=flops, bytes_accessed=0, transcendentals=0),
    )(*inputs, *after)


def struct(shape, dtype):
    return jax.ShapeDtypeStruct(shape, dtype)


def other_core(value):
    return lax.ppermute(value, "fsdp", [(i, i ^ 1) for i in range(lax.axis_size("fsdp"))])


def other_half(value):
    return lax.ppermute(value, "seq", [(0, 1), (1, 0)])


def between_chips(value):
    count = lax.axis_size("fsdp")
    groups = [list(range(core, count, 2)) for core in range(2)]
    return lax.all_to_all(value, "fsdp", 0, 0, tiled=True, axis_index_groups=groups)


def per_device(
    base_latents,
    noise_latents,
    noise_levels,
    replay_latents,
    replay_levels,
    cotangent,
    embed_weight,
    qkv_weight,
    output_weight,
    modulation,
):
    second_core = on_second_core()
    devices = lax.axis_size("fsdp")
    chips = devices // 2
    embed = embed_weight[0]
    weight = qkv_weight[0]
    width = embed.shape[1]
    columns = weight.shape[1] // 2
    block = columns // chips
    height = block - 4
    packed = round_up(block + block // 2 + 2, 8)
    folded = round_up(block // 2 + 2, 8)
    padded = round_up(2 * weight.shape[0], 128)
    tokens = base_latents.shape[2]
    heads = columns // (3 * HEAD_DIM)
    out_columns = output_weight.shape[1] // 2
    output_turned = output_weight[0].T
    output_turned = jnp.where(second_core, output_turned[:, out_columns:], output_turned[:, :out_columns])

    received = other_core(weight)
    own_turned = call(own_rows_kernel, struct((columns, padded), F32), (weight,))
    turned = call(
        functools.partial(weight_kernel, chips),
        struct((chips, height, padded), BF16),
        (own_turned, received),
        scratch=[pltpu.VMEM((columns, padded), F32)],
    )
    taken = between_chips(turned)
    stack = call(stack_kernel, struct((256, width), BF16), (embed, modulation[0]), after=(taken,))

    matrices, own_columns = call(
        functools.partial(product_kernel, block),
        (struct((chips, packed, 128), BF16), struct((height + 8, width), BF16)),
        (taken, stack),
    )
    own = call(
        pack_kernel,
        struct((tokens, 256), BF16),
        (
            noise_levels,
            replay_levels,
            base_latents[0, 0].T,
            noise_latents[0, 0].T,
            replay_latents[0, 0].T,
            cotangent[0, 0].T,
            embed,
        ),
        scalars=2,
        after=(matrices,),
    )
    here = jnp.stack([own, other_core(own)])
    there = other_half(here)

    rows, rows_turned, scale, lines, known, scaled, scaled_turned = call(
        tokens_kernel,
        (
            struct((4 * tokens, 2 * CHANNELS), BF16),
            struct((2 * CHANNELS, 4 * tokens), BF16),
            struct((4 * tokens, 2 * CHANNELS), F32),
            struct((8, 4 * tokens), F32),
            struct((2 * tokens, 2 * CHANNELS), F32),
            struct((2, 2 * tokens, 2 * CHANNELS), BF16),
            struct((2, 2 * CHANNELS, 2 * tokens), BF16),
        ),
        (here, there),
    )
    taken = between_chips(matrices)
    whole, offsets, keys_turned, probs, vel_b, vel_crossing = call(
        functools.partial(second_pass_kernel, block),
        (
            struct((columns, 2 * CHANNELS), BF16),
            struct((8, columns), F32),
            struct((2 * heads, HEAD_DIM, 2 * tokens), BF16),
            struct((2 * heads, 2 * tokens, 2 * tokens), F32),
            struct((2 * tokens, 2 * CHANNELS), F32),
            struct((2 * tokens, 2 * CHANNELS), F32),
        ),
        (taken, rows, rows_turned, scale, lines, output_turned),
        scratch=[pltpu.VMEM((columns, 2 * CHANNELS), F32)],
    )
    vel_here = vel_b + other_core(vel_crossing)
    vel_there = other_half(vel_here.astype(BF16))
    vel_a, kept = call(
        functools.partial(first_pass_kernel, block),
        (struct((2 * tokens, 2 * CHANNELS), F32), struct((2, 2 * tokens, 2 * heads * HEAD_DIM), BF16)),
        (taken, whole, offsets, here, there, rows, scale, lines, output_turned),
        scratch=[
            pltpu.VMEM((columns, 2 * CHANNELS), F32),
            pltpu.VMEM((4 * tokens, 2 * CHANNELS), BF16),
            pltpu.VMEM((2 * CHANNELS, 4 * tokens), BF16),
            pltpu.VMEM((4 * tokens, 2 * CHANNELS), F32),
            pltpu.VMEM((8, 4 * tokens), F32),
        ],
        flops=4 * 10**9,
        after=(vel_here,),
    )
    products, vel_a, vel_crossing = call(
        functools.partial(backward_kernel, block),
        (
            struct((chips, folded, 128), BF16),
            struct((2 * tokens, 2 * CHANNELS), F32),
            struct((2 * tokens, 2 * CHANNELS), F32),
        ),
        (kept, scaled, scaled_turned, keys_turned, probs, lines, known, vel_here, vel_there, output_turned, vel_a),
        scratch=[pltpu.VMEM((columns + 2 * folded, 128), F32), pltpu.VMEM((1, columns), F32)],
    )

    vel_a_here = vel_a + other_core(vel_crossing)
    part_here, part_there = call(
        payload_kernel,
        (struct((CHANNELS, tokens), F32), struct((CHANNELS, tokens), F32)),
        (noise_levels, own, vel_a_here, vel_here),
        scalars=1,
    )
    crossed_here = lax.ppermute(part_here, "role", [(0, 1), (1, 0)])
    crossed_there = lax.ppermute(part_there, ("role", "seq"), [(i, i ^ 3) for i in range(4)])

    samples = devices * base_latents.shape[1]
    height = width // 128
    kept_half, sent_half = call(
        functools.partial(closing_kernel, block, 1.0 / (samples * 2 * tokens)),
        (struct((height, 128), F32), struct((height, 128), F32)),
        (between_chips(products), own_columns, embed),
    )
    total = kept_half + other_core(sent_half)
    spread = call(spread_kernel, struct((chips, height, 128), BF16), (total, other_half(total)))
    total = jnp.sum(between_chips(spread).astype(F32), axis=0)
    mod_grads, crossed = call(
        join_kernel,
        (struct((2, width), F32), struct((CHANNELS, tokens), BF16)),
        (total, other_core(total), crossed_here, crossed_there),
    )
    return (crossed.T[None, None], mod_grads[None])


def solution(mesh):
    return jax.shard_map(
        per_device,
        mesh=mesh,
        in_specs=(
            P("role", "fsdp", "seq", None),
            P("role", "fsdp", "seq", None),
            P("role", "fsdp"),
            P("role", "fsdp", "seq", None),
            P("role", "fsdp"),
            P("role", "fsdp", "seq", None),
            P("role", None, None),
            P("role", "fsdp", "seq"),
            P("role", "seq", None),
            P("role", None, None, None),
        ),
        out_specs=(P("role", "fsdp", "seq", None), P("role", None, None)),
        check_vma=False,
    )
```

```python
import functools

import jax
import jax.numpy as jnp
from jax import lax
from jax.experimental import pallas as pl
from jax.experimental.pallas import tpu as pltpu
from jax.sharding import PartitionSpec as P

HEAD_DIM = 128
CHANNELS = 64
EPSILON = 1e-06
F32 = jnp.float32
BF16 = jnp.bfloat16
NT = (((1,), (1,)), ((), ()))
NN = (((1,), (0,)), ((), ()))
TN = (((0,), (0,)), ((), ()))


def dot(a, b, dims=NN):
    return lax.dot_general(a, b, dims, preferred_element_type=F32)


def round_up(value, step):
    return (value + step - 1) // step * step


def rounded(value):
    return value.astype(BF16).astype(F32)


def three_parts(value):
    high = rounded(value)
    middle = rounded(value - high)
    return high, middle, rounded(value - high - middle)


def lane_index(shape):
    return lax.broadcasted_iota(jnp.int32, shape, len(shape) - 1)


def row_index(shape):
    return lax.broadcasted_iota(jnp.int32, shape, len(shape) - 2)


def on_second_core():
    return lax.rem(lax.axis_index("fsdp"), 2) == 1


def on_critic():
    return lax.axis_index("role") == 1


def stack_kernel(embed, modulation, after, stack):
    modulation_a = modulation[0]
    modulation_b = jnp.where(on_critic(), modulation[1], modulation_a)
    embed_f = embed[...].astype(F32)
    stack[0:64, :] = embed[...]
    stack[64:128, :] = (embed_f * modulation_a[0:1, :]).astype(BF16)
    stack[128:192, :] = (embed_f * modulation_b[0:1, :]).astype(BF16)
    shifts = []
    for pair in (modulation_a, modulation_b):
        shift = pair[1:2, :]
        high = rounded(shift)
        shifts += [high, shift - high]
    shifts.append(jnp.zeros((60, embed.shape[1]), F32))
    stack[192:256, :] = jnp.concatenate(shifts, axis=0).astype(BF16)


def pack_kernel(noise_levels, replay_levels, base, noise, replay, cotangent, embed, after, pack):
    critic = on_critic()
    level = noise_levels[0, 0]
    level_two = jnp.where(critic, level, replay_levels[0, 0])
    base_f = base[...].astype(F32).T
    noise_f = noise[...].astype(F32).T
    input_a = rounded((1.0 - level) * base_f + level * noise_f)
    input_b = jnp.where(critic, input_a, replay[...].astype(F32).T)
    known = jnp.where(critic, noise_f - base_f, cotangent[...].astype(F32).T)
    known_high = rounded(known)
    tokens = input_a.shape[0]
    rows = jnp.concatenate([input_a, input_b], axis=0).astype(BF16)
    total = jnp.zeros((2 * tokens, 1), F32)
    width = embed.shape[1]
    for start in range(0, width, 512):
        embedded = dot(rows, embed[:, start : start + 512])
        total = total + jnp.sum(embedded * embedded, axis=-1, keepdims=True)
    scale = lax.rsqrt(total / width + EPSILON)
    lane = lane_index((tokens, CHANNELS))
    tail = jnp.zeros((tokens, CHANNELS), F32)
    ones = jnp.ones((tokens, 1), F32)
    for which, column in enumerate((scale[:tokens], scale[tokens:], ones * level, ones * level_two)):
        for part, value in enumerate(three_parts(column)):
            tail = jnp.where(lane == which * 3 + part, value, tail)
    pack[:, 0:64] = input_a.astype(BF16)
    pack[:, 64:128] = jnp.where(critic, known - known_high, input_b).astype(BF16)
    pack[:, 128:192] = known_high.astype(BF16)
    pack[:, 192:256] = tail.astype(BF16)


def turn_rows(rows, padded, second):
    count, columns = rows.shape
    empty = jnp.zeros((count, columns), F32)
    parts = [jnp.where(second, empty, rows), jnp.where(second, rows, empty)]
    if padded > 2 * count:
        parts.append(jnp.zeros((padded - 2 * count, columns), F32))
    return jnp.concatenate(parts, axis=0).T


def half_columns(weight, second):
    columns = weight.shape[1] // 2
    start = pl.multiple_of(jnp.where(second, columns, 0), 128)
    return weight[:, pl.ds(start, columns)].astype(F32)


def own_rows_kernel(weight, out):
    second = on_second_core()
    out[...] = turn_rows(half_columns(weight, second), out.shape[1], second)


def weight_kernel(chips, own, received, out, turned):
    second = on_second_core()
    columns, padded = own.shape
    turned[0:columns, :] = own[...] + turn_rows(half_columns(received, second), padded, jnp.logical_not(second))
    block = columns // chips
    height = out.shape[1]
    spare = padded // 4
    upper_lanes = lane_index((16, padded)) >= padded - spare
    for chip in range(chips):
        piece = turned[chip * block : chip * block + height, :]
        last = turned[chip * block + height : (chip + 1) * block, :]
        lines = [pltpu.roll(last, padded - spare * (part + 1), 1) for part in range(3)]
        lines.append(jnp.zeros_like(last))
        top = jnp.where(upper_lanes, jnp.concatenate(lines, axis=0), piece[0:16])
        out[chip] = jnp.concatenate([top, piece[16:]], axis=0).astype(BF16)


def product_kernel(block, taken, stack, out, columns_out):
    chips, height, padded = taken.shape
    half = block // 2
    width = stack.shape[1]
    depth = width // chips
    group = 128 // (depth & -depth)
    spare = padded - depth
    lane = lane_index((4, padded))
    for start in range(0, chips, group):
        mains, lasts = [], []
        for chip in range(start, start + group):
            piece = taken[chip].astype(F32)
            mains.append(piece[:, 0:depth])
            top, next_top = piece[0:8], piece[8:16]
            low = pltpu.roll(top, spare, 1)[0:4]
            middle = pltpu.roll(top, 2 * spare, 1)[4:8]
            high = pltpu.roll(next_top, 3 * spare, 1)[0:4]
            lasts.append(jnp.where(lane < spare, low, jnp.where(lane < 2 * spare, middle, high))[:, 0:depth])
        last = jnp.concatenate(lasts, axis=1)
        joined = jnp.concatenate([jnp.concatenate(mains, axis=1), last, jnp.zeros_like(last)], axis=0)
        span = slice(start * depth, (start + group) * depth)
        columns_out[:, span] = joined.astype(BF16)
    weight = columns_out[...]
    products = dot(weight, stack[...], NT)
    first, second = products[:, 0:128], products[:, 128:256]
    tall = jnp.concatenate([second, jnp.zeros((128 - second.shape[0], 128), F32)], axis=0).T
    lines = []
    gap = jnp.zeros((1, CHANNELS - block), F32)
    for at in (CHANNELS, CHANNELS + 2):
        offset = tall[at : at + 1, 0:block] + tall[at + 1 : at + 2, 0:block]
        high = rounded(offset)
        lines.append(jnp.concatenate([high, gap, offset - high, gap], axis=1))
    low_lanes = lane_index((half, 128)) < CHANNELS
    folded = jnp.where(low_lanes, second[0:half], pltpu.roll(second, CHANNELS, 1)[half:block])
    spare = out.shape[1] - block - half - 2
    parts = [first[0:block], folded] + lines
    if spare:
        parts.append(jnp.zeros((spare, 128), F32))
    whole = jnp.concatenate(parts, axis=0).astype(BF16)
    for chip in range(chips):
        out[chip] = whole


def token_rows(packs, sample, start, stop):
    return jnp.concatenate([pack[sample, :, start:stop] for pack in packs], axis=0)


def tail_column(packs, sample, which):
    tail = token_rows(packs, sample, 128, 256).astype(F32)
    at = CHANNELS + 3 * which
    return tail[:, at : at + 1] + tail[:, at + 1 : at + 2] + tail[:, at + 2 : at + 3]


def both_inputs(packs, sample):
    inputs = token_rows(packs, sample, 0, 128).astype(F32)
    low_lanes = lane_index((1, 128)) < CHANNELS
    same = jnp.where(low_lanes, inputs, pltpu.roll(inputs, CHANNELS, 1))
    return jnp.where(on_critic(), same, inputs)


def fill_rows(which, packs, rows, turned, scale, lines):
    low_lanes = lane_index((1, 128)) < CHANNELS
    lines[...] = jnp.zeros_like(lines)
    for sample in range(2):
        inputs = both_inputs(packs, sample)
        tokens = inputs.shape[0]
        own = slice(sample * tokens, (sample + 1) * tokens)
        flipped = pltpu.roll(inputs, CHANNELS, 1)
        level = jnp.broadcast_to(tail_column(packs, sample, 2 + which), inputs.shape)
        norm = jnp.broadcast_to(tail_column(packs, sample, which), inputs.shape)
        plain, scaled_part = (flipped, inputs) if which else (inputs, flipped)
        both = jnp.where(low_lanes, plain, scaled_part * level)
        rows[own, :] = both.astype(BF16)
        turned[:, own] = both.T.astype(BF16)
        scale[own, :] = norm
        lines[0:1, own] = norm.T[0:1]
        lines[1:2, own] = level.T[0:1]


def tokens_kernel(here, there, rows, turned, scale, lines):
    fill_rows(1, (here, there), rows, turned, scale, lines)


def fill_backward(packs, known, scaled, scaled_turned):
    low_lanes = lane_index((1, 128)) < CHANNELS
    parts = []
    for sample in range(2):
        inputs = both_inputs(packs, sample)
        whole = jnp.where(low_lanes, pltpu.roll(inputs, CHANNELS, 1), inputs)
        whole = whole * (tail_column(packs, sample, 1) * tail_column(packs, sample, 3))
        scaled[sample] = whole.astype(BF16)
        scaled_turned[sample] = whole.T.astype(BF16)
        high = token_rows(packs, sample, 128, 256).astype(F32)[:, 0:CHANNELS]
        low = token_rows(packs, sample, 0, 128).astype(F32)[:, CHANNELS:]
        parts.append(high + jnp.where(on_critic(), low, 0.0))
    known[...] = jnp.concatenate(parts, axis=1)


def sample_level(lines, sample):
    at = sample * (lines.shape[1] // 2)
    return lines[1:2, at : at + 1]


def forward(which, rows, turned, scale, lines, matrices, offsets, output_turned, keys_out, probs_out, velocity, crossing):
    heads = output_turned.shape[1] // HEAD_DIM
    tokens = rows.shape[0] // 2
    inputs = rows[...]
    inputs_turned = turned[...]
    levels = [sample_level(lines, sample) for sample in range(2)]
    offset = offsets[which : which + 1, :]
    offset_turned = jnp.broadcast_to(offset, (128, offset.shape[1])).T[:, 0:1]
    units = []
    for head in range(heads):
        at = head * 3 * HEAD_DIM
        span = slice(at, at + 3 * HEAD_DIM)
        matrix = matrices[span, :]
        product = dot(inputs, matrix[HEAD_DIM : 2 * HEAD_DIM], NT)
        product_turned = dot(matrix, inputs_turned)
        line = offset[:, at + HEAD_DIM : at + 2 * HEAD_DIM]
        for sample in range(2):
            own = slice(sample * tokens, (sample + 1) * tokens)
            key = (product[own] * scale[own, :] + line * levels[sample]).astype(BF16)
            norms = lines[0:1, own]
            flipped = product_turned[:, own] * norms + offset_turned[span] * levels[sample]
            flipped = flipped.astype(BF16)
            if keys_out is not None:
                keys_out[2 * head + sample] = flipped[HEAD_DIM : 2 * HEAD_DIM]
            units.append((key, flipped[0:HEAD_DIM], flipped[2 * HEAD_DIM :]))
    totals = [None, None]
    scores = [dot(key, query) * (HEAD_DIM**-0.5) for key, query, _ in units]
    for unit, score in enumerate(scores):
        powers = jnp.exp(score - jnp.max(score, axis=0, keepdims=True))
        probs = powers * (1.0 / jnp.sum(powers, axis=0, keepdims=True))
        if probs_out is not None:
            probs_out[unit] = probs
        mixed = dot(units[unit][2], probs.astype(BF16)).astype(BF16)
        head = unit // 2
        term = dot(output_turned[:, head * HEAD_DIM : (head + 1) * HEAD_DIM], mixed)
        before = totals[unit % 2]
        totals[unit % 2] = term if before is None else before + term
    whole = jnp.concatenate(totals, axis=0).T
    velocity[...] = whole
    if crossing is not None:
        crossing[...] = pltpu.roll(whole, CHANNELS, 1)


def second_pass_kernel(
    block,
    taken,
    rows,
    turned,
    scale,
    lines_in,
    output_turned,
    matrices,
    offsets,
    keys_turned,
    probs,
    velocity,
    crossing,
    stacked,
):
    chips = taken.shape[0]
    half = block // 2
    low_lanes = lane_index((half, 128)) < CHANNELS
    lines = [[], []]
    for chip in range(chips):
        piece = taken[chip].astype(F32)
        at = chip * block
        folded = piece[block : block + half]
        moved = pltpu.roll(folded, CHANNELS, 1)
        stacked[at : at + half, :] = jnp.where(low_lanes, piece[0:half], moved)
        stacked[at + half : at + block, :] = jnp.where(low_lanes, piece[half:block], folded)
        for which in range(2):
            line = piece[block + half + which : block + half + which + 1]
            lines[which].append((line + pltpu.roll(line, CHANNELS, 1))[:, 0:block])
    joined = [jnp.concatenate(line, axis=1) for line in lines]
    offsets[...] = jnp.concatenate(joined + [jnp.zeros((6, offsets.shape[1]), F32)], axis=0)
    matrices[...] = stacked[...].astype(BF16)
    forward(
        1,
        rows,
        turned,
        scale,
        lines_in,
        matrices[...],
        offsets,
        output_turned,
        keys_turned,
        probs,
        velocity,
        crossing,
    )


def first_pass_kernel(
    block,
    taken,
    matrices,
    offsets,
    here,
    there,
    rows_b,
    scale_b,
    lines,
    output_turned,
    after,
    velocity,
    kept,
    known,
    scaled,
    scaled_turned,
    stacked,
    rows,
    turned,
    scale,
    lines_a,
):
    fill_rows(0, (here, there), rows, turned, scale, lines_a)
    fill_backward((here, there), known, scaled, scaled_turned)
    for chip in range(taken.shape[0]):
        stacked[chip * block : (chip + 1) * block, :] = taken[chip].astype(F32)[0:block]
    forward(
        0,
        rows,
        turned,
        scale,
        lines_a,
        stacked[...].astype(BF16),
        offsets,
        output_turned,
        None,
        None,
        velocity,
        None,
    )
    inputs = rows_b[...]
    tokens = inputs.shape[0] // 2
    for head in range(output_turned.shape[1] // HEAD_DIM):
        for place, part in enumerate((0, 2)):
            at = (3 * head + part) * HEAD_DIM
            to = (2 * head + place) * HEAD_DIM
            product = dot(inputs, matrices[at : at + HEAD_DIM, :], NT)
            line = offsets[1:2, at : at + HEAD_DIM]
            for sample in range(2):
                own = slice(sample * tokens, (sample + 1) * tokens)
                value = product[own] * scale_b[own, :] + line * sample_level(lines, sample)
                kept[sample, :, to : to + HEAD_DIM] = value.astype(BF16)


def swap_tokens(value):
    half = value.shape[0] // 2
    return jnp.concatenate([value[half:], value[:half]], axis=0)


def backward_kernel(
    block,
    kept,
    scaled,
    rows,
    keys_turned,
    probs_turned,
    lines,
    known,
    vel_here,
    vel_there,
    output_turned,
    vel_a,
    out,
    first,
    crossing,
    gathered,
    summed,
):
    critic = on_critic()
    first[...] = vel_a[...]
    crossing[...] = pltpu.roll(vel_a[...], CHANNELS, 1)
    heads = output_turned.shape[1] // HEAD_DIM
    velocity = vel_here[...] + swap_tokens(vel_there[...].astype(F32))
    level_rows = []
    for sample in range(2):
        tokens = lines.shape[1] // 2
        level = lines[1:2, sample * tokens : (sample + 1) * tokens]
        high = rounded(level)
        level_rows.append(jnp.concatenate([high, level - high, jnp.zeros((14, tokens), F32)], axis=0).astype(BF16))
    known = known[...]
    grad_velocity = jnp.where(critic, velocity - known, known)
    grads_turned = grad_velocity.T.astype(BF16)
    grads = grad_velocity.astype(BF16)
    grad_mixed, grad_probs = [], []
    for unit in range(2 * heads):
        head, sample = unit // 2, unit % 2
        weight = output_turned[:, head * HEAD_DIM : (head + 1) * HEAD_DIM]
        lanes = slice(sample * CHANNELS, (sample + 1) * CHANNELS)
        grad_mixed.append(dot(grads[:, lanes], weight).astype(BF16))
        turned = dot(weight, grads_turned[lanes], TN).astype(BF16)
        value = kept[sample, :, (2 * head + 1) * HEAD_DIM : (2 * head + 2) * HEAD_DIM]
        grad_probs.append(dot(value, turned))
    columns = heads * 3 * HEAD_DIM
    gathered[columns:, :] = jnp.zeros((gathered.shape[0] - columns, 128), F32)
    height = out.shape[1]
    half = block // 2
    row = row_index((height, 128))
    low_lanes = lane_index((height, 128)) < CHANNELS
    pad = jnp.zeros((1, 128 - block), F32) if block < 128 else None
    for head in range(heads):
        at = head * 3 * HEAD_DIM
        query_total, rest_total = None, None
        ends = []
        for sample in range(2):
            unit = 2 * head + sample
            probs = probs_turned[unit]
            grad = grad_probs[unit]
            inner = jnp.sum(grad * probs, axis=0, keepdims=True)
            grad_scores = (probs * (grad - inner) * (HEAD_DIM**-0.5)).astype(BF16)
            grad_value = dot(probs.astype(BF16), grad_mixed[unit])
            grad_key = dot(grad_scores, kept[sample, :, 2 * head * HEAD_DIM : (2 * head + 1) * HEAD_DIM])
            grad_query = dot(keys_turned[unit], grad_scores).astype(BF16)
            rest = jnp.concatenate([grad_key, grad_value], axis=1).astype(BF16)
            query_term = dot(grad_query, scaled[sample])
            rest_term = dot(jnp.concatenate([rows[sample], level_rows[sample]], axis=0), rest)
            query_total = query_term if query_total is None else query_total + query_term
            rest_total = rest_term if rest_total is None else rest_total + rest_term
            ends.append(dot(level_rows[sample], grad_query, NT))
        ends = jnp.concatenate([ends[0] + ends[1], rest_total[128:]], axis=1)
        gathered[at : at + HEAD_DIM, :] = query_total
        gathered[at + HEAD_DIM : at + 3 * HEAD_DIM, :] = rest_total[0:128].T
        summed[:, at : at + 3 * HEAD_DIM] = ends[0:1] + ends[1:2]
        start = columns * head // heads // block
        stop = columns * (head + 1) // heads // block
        for chip in range(start, stop):
            base = chip * block
            piece = jnp.where(low_lanes, gathered[base : base + height, :], gathered[base + half : base + half + height, :])
            line = summed[:, base : base + block]
            high = rounded(line)
            pair = [high, line - high]
            if pad is not None:
                pair = [jnp.concatenate([part, pad], axis=1) for part in pair]
            tail = jnp.where(row == half, pair[0], jnp.where(row == half + 1, pair[1], 0.0))
            out[chip] = jnp.where(row < half, piece, tail).astype(BF16)


def closing_kernel(block, factor, taken, weight, embed, kept, sent):
    second = on_second_core()
    total = taken[0].astype(F32)
    for chip in range(1, taken.shape[0]):
        total = total + taken[chip].astype(F32)
    half = block // 2
    height = total.shape[0]
    row = row_index((height, 128))
    ends = total[half : half + 1] + total[half + 1 : half + 2]
    lines = [jnp.where(row < half, total, 0.0), jnp.zeros((128 - height, 128), F32)]
    turned = jnp.concatenate(lines, axis=0).T
    products = turned[0:CHANNELS] + pltpu.roll(turned[CHANNELS:], half, 1)
    joined = jnp.concatenate([products, ends, jnp.zeros((7, 128), F32)], axis=0)[:, 0 : weight.shape[0]]
    high = joined.astype(BF16)
    low = (joined - high.astype(F32)).astype(BF16)
    middle = embed.shape[1] // 2
    step = middle // 3
    parts = []
    for start in range(0, 2 * middle, step):
        columns = weight[:, start : start + step]
        product = dot(high, columns) + dot(low, columns)
        scale = jnp.sum(product[:CHANNELS] * embed[:, start : start + step].astype(F32), axis=0, keepdims=True)
        parts.append(jnp.concatenate([scale, product[CHANNELS : CHANNELS + 1]], axis=0) * factor)
    sides = []
    for side in (parts[:3], parts[3:]):
        lines = [part[which : which + 1, i : i + 128] for which in range(2) for part in side for i in range(0, step, 128)]
        sides.append(jnp.concatenate(lines, axis=0))
    kept[...] = jnp.where(second, sides[1], sides[0])
    sent[...] = jnp.where(second, sides[0], sides[1])


def payload_kernel(noise_levels, own, vel_a, vel_b, here, there):
    tokens = own.shape[0]
    velocity = vel_a[:, 0:CHANNELS]
    part = jnp.where(on_critic(), vel_b[:, 0:CHANNELS] - velocity, -noise_levels[0, 0] * velocity)
    sample = jnp.where(on_critic(), 0.0, own[:, 0:CHANNELS].astype(F32))
    here[...] = (sample + part[0:tokens]).T
    there[...] = part[tokens:].T


def spread_kernel(total, other, out):
    line = (total[...] + other[...]).astype(BF16)
    for chip in range(out.shape[0]):
        out[chip] = line


def join_kernel(total, near, crossed_here, crossed_there, out, crossed):
    crossed[...] = (crossed_here[...] + crossed_there[...]).astype(BF16)
    second = on_second_core()
    count = total.shape[0] // 2
    left = jnp.where(second, near[...], total[...])
    right = jnp.where(second, total[...], near[...])
    for which in range(2):
        for side, half in enumerate((left, right)):
            for i in range(count):
                at = (side * count + i) * 128
                out[which : which + 1, at : at + 128] = half[which * count + i : which * count + i + 1, :]


def call(kernel, out_shapes, inputs, scalars=0, scratch=(), flops=0, after=()):
    specs = [pl.BlockSpec(memory_space=pltpu.SMEM)] * scalars
    specs += [pl.BlockSpec(memory_space=pltpu.VMEM)] * (len(inputs) - scalars)
    specs += [pl.BlockSpec(memory_space=pl.ANY)] * len(after)
    return pl.pallas_call(
        kernel,
        out_shape=out_shapes,
        in_specs=specs,
        out_specs=jax.tree.map(lambda _: pl.BlockSpec(memory_space=pltpu.VMEM), out_shapes),
        scratch_shapes=list(scratch),
        compiler_params=pltpu.CompilerParams(vmem_limit_bytes=28 * 2**20),
        cost_estimate=pl.CostEstimate(flops=flops, bytes_accessed=0, transcendentals=0),
    )(*inputs, *after)


def struct(shape, dtype):
    return jax.ShapeDtypeStruct(shape, dtype)


def other_core(value):
    return lax.ppermute(value, "fsdp", [(i, i ^ 1) for i in range(lax.axis_size("fsdp"))])


def other_half(value):
    return lax.ppermute(value, "seq", [(0, 1), (1, 0)])


def between_chips(value):
    count = lax.axis_size("fsdp")
    groups = [list(range(core, count, 2)) for core in range(2)]
    return lax.all_to_all(value, "fsdp", 0, 0, tiled=True, axis_index_groups=groups)


def per_device(
    base_latents,
    noise_latents,
    noise_levels,
    replay_latents,
    replay_levels,
    cotangent,
    embed_weight,
    qkv_weight,
    output_weight,
    modulation,
):
    second_core = on_second_core()
    devices = lax.axis_size("fsdp")
    chips = devices // 2
    embed = embed_weight[0]
    weight = qkv_weight[0]
    width = embed.shape[1]
    columns = weight.shape[1] // 2
    block = columns // chips
    height = block - 4
    packed = round_up(block + block // 2 + 2, 8)
    folded = round_up(block // 2 + 2, 8)
    padded = round_up(2 * weight.shape[0], 128)
    tokens = base_latents.shape[2]
    heads = columns // (3 * HEAD_DIM)
    out_columns = output_weight.shape[1] // 2
    output_turned = output_weight[0].T
    output_turned = jnp.where(second_core, output_turned[:, out_columns:], output_turned[:, :out_columns])

    received = other_core(weight)
    own_turned = call(own_rows_kernel, struct((columns, padded), F32), (weight,))
    turned = call(
        functools.partial(weight_kernel, chips),
        struct((chips, height, padded), BF16),
        (own_turned, received),
        scratch=[pltpu.VMEM((columns, padded), F32)],
    )
    taken = between_chips(turned)
    stack = call(stack_kernel, struct((256, width), BF16), (embed, modulation[0]), after=(taken,))

    matrices, own_columns = call(
        functools.partial(product_kernel, block),
        (struct((chips, packed, 128), BF16), struct((height + 8, width), BF16)),
        (taken, stack),
    )
    own = call(
        pack_kernel,
        struct((tokens, 256), BF16),
        (
            noise_levels,
            replay_levels,
            base_latents[0, 0].T,
            noise_latents[0, 0].T,
            replay_latents[0, 0].T,
            cotangent[0, 0].T,
            embed,
        ),
        scalars=2,
        after=(matrices,),
    )
    here = jnp.stack([own, other_core(own)])
    there = other_half(here)

    rows, rows_turned, scale, lines = call(
        tokens_kernel,
        (
            struct((4 * tokens, 2 * CHANNELS), BF16),
            struct((2 * CHANNELS, 4 * tokens), BF16),
            struct((4 * tokens, 2 * CHANNELS), F32),
            struct((8, 4 * tokens), F32),
        ),
        (here, there),
    )
    taken = between_chips(matrices)
    whole, offsets, keys_turned, probs, vel_b, vel_crossing = call(
        functools.partial(second_pass_kernel, block),
        (
            struct((columns, 2 * CHANNELS), BF16),
            struct((8, columns), F32),
            struct((2 * heads, HEAD_DIM, 2 * tokens), BF16),
            struct((2 * heads, 2 * tokens, 2 * tokens), F32),
            struct((2 * tokens, 2 * CHANNELS), F32),
            struct((2 * tokens, 2 * CHANNELS), F32),
        ),
        (taken, rows, rows_turned, scale, lines, output_turned),
        scratch=[pltpu.VMEM((columns, 2 * CHANNELS), F32)],
    )
    vel_here = vel_b + other_core(vel_crossing)
    vel_there = other_half(vel_here.astype(BF16))
    vel_a, kept, known, scaled, scaled_turned = call(
        functools.partial(first_pass_kernel, block),
        (
            struct((2 * tokens, 2 * CHANNELS), F32),
            struct((2, 2 * tokens, 2 * heads * HEAD_DIM), BF16),
            struct((2 * tokens, 2 * CHANNELS), F32),
            struct((2, 2 * tokens, 2 * CHANNELS), BF16),
            struct((2, 2 * CHANNELS, 2 * tokens), BF16),
        ),
        (taken, whole, offsets, here, there, rows, scale, lines, output_turned),
        scratch=[
            pltpu.VMEM((columns, 2 * CHANNELS), F32),
            pltpu.VMEM((4 * tokens, 2 * CHANNELS), BF16),
            pltpu.VMEM((2 * CHANNELS, 4 * tokens), BF16),
            pltpu.VMEM((4 * tokens, 2 * CHANNELS), F32),
            pltpu.VMEM((8, 4 * tokens), F32),
        ],
        flops=4 * 10**9,
        after=(vel_here,),
    )
    products, vel_a, vel_crossing = call(
        functools.partial(backward_kernel, block),
        (
            struct((chips, folded, 128), BF16),
            struct((2 * tokens, 2 * CHANNELS), F32),
            struct((2 * tokens, 2 * CHANNELS), F32),
        ),
        (kept, scaled, scaled_turned, keys_turned, probs, lines, known, vel_here, vel_there, output_turned, vel_a),
        scratch=[pltpu.VMEM((columns + 2 * folded, 128), F32), pltpu.VMEM((1, columns), F32)],
    )

    vel_a_here = vel_a + other_core(vel_crossing)
    part_here, part_there = call(
        payload_kernel,
        (struct((CHANNELS, tokens), F32), struct((CHANNELS, tokens), F32)),
        (noise_levels, own, vel_a_here, vel_here),
        scalars=1,
    )
    crossed_here = lax.ppermute(part_here, "role", [(0, 1), (1, 0)])
    crossed_there = lax.ppermute(part_there, ("role", "seq"), [(i, i ^ 3) for i in range(4)])

    samples = devices * base_latents.shape[1]
    height = width // 128
    kept_half, sent_half = call(
        functools.partial(closing_kernel, block, 1.0 / (samples * 2 * tokens)),
        (struct((height, 128), F32), struct((height, 128), F32)),
        (between_chips(products), own_columns, embed),
    )
    total = kept_half + other_core(sent_half)
    spread = call(spread_kernel, struct((chips, height, 128), BF16), (total, other_half(total)))
    total = jnp.sum(between_chips(spread).astype(F32), axis=0)
    mod_grads, crossed = call(
        join_kernel,
        (struct((2, width), F32), struct((CHANNELS, tokens), BF16)),
        (total, other_core(total), crossed_here, crossed_there),
    )
    return (crossed.T[None, None], mod_grads[None])


def solution(mesh):
    return jax.shard_map(
        per_device,
        mesh=mesh,
        in_specs=(
            P("role", "fsdp", "seq", None),
            P("role", "fsdp", "seq", None),
            P("role", "fsdp"),
            P("role", "fsdp", "seq", None),
            P("role", "fsdp"),
            P("role", "fsdp", "seq", None),
            P("role", None, None),
            P("role", "fsdp", "seq"),
            P("role", "seq", None),
            P("role", None, None, None),
        ),
        out_specs=(P("role", "fsdp", "seq", None), P("role", None, None)),
        check_vma=False,
    )
```
